32 devices in a mesh: dp: 8 (over z, x), tensor: 4 (over y, core).
Axes of the slice: x: 2, y: 2, z: 4, core: 2. Of those that a mesh axis runs over, the one named last changes fastest.
Arguments:
- activations: bfloat16 [8192, 2048], P(('dp', 'tensor')), may hold values from -6 to 6
- cotangent: bfloat16 [8192, 2048], P(('dp', 'tensor')), may hold values from -6 to 6
- segments: int32 [8192], P('dp'), may hold values from 0 to 2, as said below
- norm_one_gain: bfloat16 [2048], P(('dp', 'tensor')), may hold values from 0.099609375 to 1.8984375
- norm_one_bias: bfloat16 [2048], P(('dp', 'tensor')), may hold values from -3 to 3
- w_query: bfloat16 [2048, 2048], P('dp', 'tensor'), may hold values from -0.1875 to 0.1875
- w_key: bfloat16 [2048, 2048], P('dp', 'tensor'), may hold values from -0.1875 to 0.1875
- w_value: bfloat16 [2048, 2048], P('dp', 'tensor'), may hold values from -0.125 to 0.125
- qkv_bias: bfloat16 [3, 32, 64], P(None, 'tensor', 'dp'), may hold values from -3 to 3
- w_out: bfloat16 [2048, 2048], P('tensor', 'dp'), may hold values from -0.75 to 0.75
- norm_two_gain: bfloat16 [2048], P(('dp', 'tensor')), may hold values from 0.099609375 to 1.8984375
- norm_two_bias: bfloat16 [2048], P(('dp', 'tensor')), may hold values from -3 to 3
- w_gate: bfloat16 [2048, 5632], P('dp', 'tensor'), may hold values from -0.125 to 0.125
- w_up: bfloat16 [2048, 5632], P('dp', 'tensor'), may hold values from -0.125 to 0.125
- w_down: bfloat16 [5632, 2048], P('tensor', 'dp'), may hold values from -0.109375 to 0.109375
Outputs:
- result: bfloat16 [8192, 2048], P(('dp', 'tensor'))
- input_grad: bfloat16 [8192, 2048], P(('dp', 'tensor'))
- grad_norm_one_gain: float32 [2048], P(('dp', 'tensor'))
- grad_norm_one_bias: float32 [2048], P(('dp', 'tensor'))
- grad_w_query: float32 [2048, 2048], P('dp', 'tensor')
- grad_w_key: float32 [2048, 2048], P('dp', 'tensor')
- grad_w_value: float32 [2048, 2048], P('dp', 'tensor')
- grad_qkv_bias: float32 [3, 32, 64], P(None, 'tensor', 'dp')
- grad_w_out: float32 [2048, 2048], P('tensor', 'dp')
- grad_norm_two_gain: float32 [2048], P(('dp', 'tensor'))
- grad_norm_two_bias: float32 [2048], P(('dp', 'tensor'))
- grad_w_gate: float32 [2048, 5632], P('dp', 'tensor')
- grad_w_up: float32 [2048, 5632], P('dp', 'tensor')
- grad_w_down: float32 [5632, 2048], P('tensor', 'dp')
The draws below stay inside these ranges and needn't reach their ends.
Inputs may be any that keep to these rules, and one draw needn't show every extreme that they name: `segments`: within each sequence the segment numbers never fall, start at 0 and end at 2; each tells the document of its token.
All inputs are finite; a program needn't handle non-finite values.
Results may differ from the reference program's by a relative error of at most 0.023.
Values may be sent and summed in bfloat16 or wider, within the bound.
No kernel may reach another device: no remote copies, remote signals or barrier semaphores. Data moves between devices by JAX's collectives and lax.ppermute only.
A program may use at most 192 MiB of HBM per device.

```python
import jax
import jax.numpy as jnp
from jax import lax

D = 2048
H = 32
HD = 64
FF = 5632
ROT = 16
SEQ = 1024
TOKENS = 8192
N_DP = 8


def draw_segments(key, part):
    key = jax.random.fold_in(key, 11)
    first_key, second_key = jax.random.split(key)
    openings = jax.random.randint(first_key, (N_DP, 1), 1, SEQ // 8 + 1)
    closing = jax.random.randint(second_key, (N_DP, 1), SEQ - SEQ // 8, SEQ)
    places = jnp.arange(SEQ, dtype=jnp.int32)[None, :]
    labels = (places >= openings).astype(jnp.int32) + (places >= closing).astype(jnp.int32)
    return labels.reshape(TOKENS)


def block_levels(rng, extent, pieces, least, top_value):
    def one(axis_at, shards_of):
        steps = jax.random.uniform(jax.random.fold_in(jax.random.fold_in(rng, 6), axis_at), (shards_of,), jnp.float32, least / len(pieces), top_value / len(pieces))
        return jnp.repeat(jnp.exp(steps), extent[axis_at] // shards_of).reshape((-1,) + (1,) * (len(extent) - axis_at - 1))

    factor_of = one(*pieces[0])
    for cut in pieces[1:]:
        factor_of = factor_of * one(*cut)
    return factor_of


def scatter_about(stream_key, shape, deviation, bound, cuts=(), kind=jnp.bfloat16):
    loudness = block_levels(stream_key, shape, cuts, -0.22, 0.18) if cuts else 1.0
    entries = jax.random.normal(stream_key, shape, jnp.float32) * deviation * loudness
    return jnp.minimum(jnp.maximum(entries, -bound), bound).astype(kind)


def setup_inputs(seed: int = 0) -> dict:
    key_list = jax.random.split(jax.random.key(seed), 16)
    activations = scatter_about(key_list[0], (TOKENS, D), 1.0, 6.0, ((0, 32),))
    cotangent = scatter_about(key_list[1], (TOKENS, D), 1.0, 6.0, ((0, 32),))
    segments = draw_segments(jax.random.fold_in(key_list[15], 71), 0)
    norm_one_gain = jnp.clip(1.0 + 0.18 * jax.random.normal(key_list[3], (D,), jnp.float32), 0.099609375, 1.8984375).astype(jnp.bfloat16)
    norm_one_bias = scatter_about(key_list[4], (D,), 0.5, 3.0, ((0, 32),))
    w_query = scatter_about(key_list[5], (D, D), (D // 2) ** -0.5, 0.1875, ((0, 8), (1, 4)))
    w_key = scatter_about(key_list[6], (D, D), (D // 2) ** -0.5, 0.1875, ((0, 8), (1, 4)))
    w_value = scatter_about(key_list[7], (D, D), D ** -0.5, 0.125, ((0, 8), (1, 4)))
    qkv_bias = scatter_about(key_list[8], (3, H, HD), 0.5, 3.0, ((1, 4), (2, 8)))
    w_out = scatter_about(key_list[9], (D, D), (D // 32) ** -0.5, 0.75, ((0, 4), (1, 8)))
    norm_two_gain = jnp.clip(1.0 + 0.18 * jax.random.normal(key_list[10], (D,), jnp.float32), 0.099609375, 1.8984375).astype(jnp.bfloat16)
    norm_two_bias = scatter_about(key_list[11], (D,), 0.5, 3.0, ((0, 32),))
    w_gate = scatter_about(key_list[12], (D, FF), D ** -0.5, 0.125, ((0, 8), (1, 4)))
    w_up = scatter_about(key_list[13], (D, FF), D ** -0.5, 0.125, ((0, 8), (1, 4)))
    w_down = scatter_about(key_list[14], (FF, D), (FF // 2) ** -0.5, 0.109375, ((0, 4), (1, 8)))
    return {"activations": activations, "cotangent": cotangent, "segments": segments, "norm_one_gain": norm_one_gain, "norm_one_bias": norm_one_bias, "w_query": w_query, "w_key": w_key, "w_value": w_value, "qkv_bias": qkv_bias, "w_out": w_out, "norm_two_gain": norm_two_gain, "norm_two_bias": norm_two_bias, "w_gate": w_gate, "w_up": w_up, "w_down": w_down}


@jax.custom_vjp
def low(v):
    return lax.optimization_barrier(v.astype(jnp.bfloat16)).astype(jnp.float32)

@jax.custom_vjp
def low_back(v):
    return v

def low_keep(v):
    return (low(v), None)

def low_pass(kept, grad):
    return (grad,)

def back_keep(v):
    return (v, None)

def back_low(kept, grad):
    return (low(grad),)
low.defvjp(low_keep, low_pass)
low_back.defvjp(back_keep, back_low)
EPSILON = 1e-05
HIGHEST = lax.Precision.HIGHEST
NEGATIVE = -1e+30

def product(left, right):
    return jnp.dot(left, right, precision=HIGHEST, preferred_element_type=jnp.float32)

def layer_norm(inputs, gain_vec, shift_vec):
    average = lax.optimization_barrier(jnp.mean(inputs, axis=-1, keepdims=True))
    centred = inputs - average
    variance = lax.optimization_barrier(jnp.mean(centred * centred, axis=-1, keepdims=True))
    return centred * lax.rsqrt(variance + EPSILON) * gain_vec + shift_vec

def rotary_tables(segment_ids):
    length = segment_ids.shape[0]
    places = jnp.arange(length, dtype=jnp.int32)
    starts = jnp.concatenate([jnp.ones((1,), dtype=jnp.bool_), segment_ids[1:] != segment_ids[:-1]])
    begins = lax.cummax(jnp.where(starts, places, 0), axis=0)
    within = (places - begins).astype(jnp.float32)
    frequency = 10000.0 ** (-2.0 * jnp.arange(ROT // 2, dtype=jnp.float32) / ROT)
    angles = within[:, None] * frequency[None, :]
    return (jnp.cos(angles), jnp.sin(angles))

def rotate(heads, cos_table, sin_table):
    halves = ROT // 2
    first_half = heads[..., :halves]
    second_half = heads[..., halves:ROT]
    cos_part = cos_table[:, None, :]
    sin_part = sin_table[:, None, :]
    return jnp.concatenate([first_half * cos_part - second_half * sin_part, second_half * cos_part + first_half * sin_part, heads[..., ROT:]], axis=-1)

def forward(inputs, gain_one, shift_one, w_query, w_key, w_value, qkv_bias, w_out, gain_two, shift_two, w_gate, w_up, w_down, cos_table, sin_table, segment_ids):
    length = inputs.shape[0]
    block_rows = min(512, length)
    blocks = length // block_rows
    scaling = HD ** (-0.5)
    normed = low(layer_norm(inputs, gain_one, shift_one))
    queries = low_back(product(normed, w_query) + qkv_bias[0].reshape(-1))
    key_heads = low_back(product(normed, w_key) + qkv_bias[1].reshape(-1))
    value_heads = low(low_back(product(normed, w_value) + qkv_bias[2].reshape(-1))).reshape(length, H, HD)
    queries = low(rotate(queries.reshape(length, H, HD), cos_table, sin_table))
    key_heads = low(rotate(key_heads.reshape(length, H, HD), cos_table, sin_table))
    key_places = jnp.arange(length, dtype=jnp.int32)

    def attend(inputs_block):
        query_block, segment_block, offset = inputs_block
        row_places = offset + jnp.arange(block_rows, dtype=jnp.int32)
        allowed = (segment_block[:, None] == segment_ids[None, :]) & (row_places[:, None] >= key_places[None, :])
        scores = low_back(jnp.einsum('qhd,khd->hqk', query_block, key_heads, precision=HIGHEST) * scaling)
        scores = jnp.where(allowed[None], scores, NEGATIVE)
        weights = low(jax.nn.softmax(scores, axis=-1))
        return jnp.einsum('hqk,khd->qhd', weights, value_heads, precision=HIGHEST)
    attended = lax.map(jax.checkpoint(attend), (queries.reshape(blocks, block_rows, H, HD), segment_ids.reshape(blocks, block_rows), jnp.arange(blocks, dtype=jnp.int32) * block_rows))
    mixed_heads = low(low_back(attended.reshape(length, D)))
    middle = inputs + low_back(product(mixed_heads, w_out))
    normed_two = low(layer_norm(middle, gain_two, shift_two))
    gate_values = low_back(product(normed_two, w_gate))
    up_values = low_back(product(normed_two, w_up))
    hidden = low(jax.nn.silu(gate_values) * up_values)
    return middle + product(hidden, w_down)

def reference(activations, cotangent, segments, norm_one_gain, norm_one_bias, w_query, w_key, w_value, qkv_bias, w_out, norm_two_gain, norm_two_bias, w_gate, w_up, w_down):
    params = tuple((weight.astype(jnp.float32) for weight in (norm_one_gain, norm_one_bias, w_query, w_key, w_value, qkv_bias, w_out, norm_two_gain, norm_two_bias, w_gate, w_up, w_down)))
    inputs = activations.astype(jnp.float32).reshape(N_DP, SEQ, D)
    grads_in = cotangent.astype(jnp.float32).reshape(N_DP, SEQ, D)
    segment_rows = segments.reshape(N_DP, SEQ)

    def sequence(totals, sequence_inputs):
        seq_inputs, seq_grad, seq_segments = sequence_inputs
        cos_table, sin_table = rotary_tables(seq_segments)

        def layer_run(layer_input, *weights):
            return forward(layer_input, *weights, cos_table, sin_table, seq_segments)
        result, pullback = jax.vjp(layer_run, seq_inputs, *params)
        gradients = pullback(seq_grad)
        totals = tuple((running + contribution for running, contribution in zip(totals, gradients[1:])))
        return (totals, (result, gradients[0]))
    zero_grads = tuple((jnp.zeros_like(weight) for weight in params))
    totals, (results, input_grads) = lax.scan(sequence, zero_grads, (inputs, grads_in, segment_rows))
    return (results.reshape(TOKENS, D).astype(jnp.bfloat16), input_grads.reshape(TOKENS, D).astype(jnp.bfloat16), totals[0], totals[1], totals[2], totals[3], totals[4], totals[5], totals[6], totals[7], totals[8], totals[9], totals[10], totals[11])
```

```python
import functools

import jax
import jax.experimental.pallas as pl
import jax.experimental.pallas.tpu as pltpu
import jax.numpy as jnp
from jax import lax
from jax.sharding import PartitionSpec as P

HD = 64
ROT = 16
PAIR = 2 * HD
EPSILON = 1e-05
NEGATIVE = -1e30
F32 = jnp.float32
BF16 = jnp.bfloat16
MIB = 2**20


def product(left, right, left_dim, right_dim):
    return lax.dot_general(
        left, right, (((left_dim,), (right_dim,)), ((), ())), preferred_element_type=F32
    )


def turn(columns, cos_values, sin_values, opening):
    partner = jnp.where(opening, pltpu.roll(columns, PAIR - 8, 1), pltpu.roll(columns, 8, 1))
    return columns * cos_values + partner * sin_values


def opening_lanes(rows):
    return lax.broadcasted_iota(jnp.int32, (rows, PAIR), 1) % HD < 8


def qkv_body(x_ref, qk_weight, v_weight, bias_ref, cos_ref, sin_ref, qk_ref, v_ref):
    width = qk_ref.shape[1]
    rows = x_ref[...]
    opening = opening_lanes(rows.shape[0])
    cos_values = cos_ref[...]
    sin_values = sin_ref[...]
    both = product(rows, qk_weight[...], 1, 0) + bias_ref[:, :width]
    for at in range(0, width, PAIR):
        part = turn(both[:, at : at + PAIR], cos_values, sin_values, opening)
        qk_ref[:, at : at + PAIR] = part.astype(BF16)
    v_ref[...] = (product(rows, v_weight[...], 1, 0) + bias_ref[:, width:]).astype(BF16)


def project_qkv(rows, weight_qk, weight_vo, bias_row, cos_table, sin_table):
    length, depth = rows.shape
    wide = weight_qk.shape[1]
    block = min(256, length)
    by_rows = lambda columns: pl.BlockSpec((block, columns), lambda i: (i, 0))
    whole = lambda shape: pl.BlockSpec(shape, lambda i: (0, 0))
    return pl.pallas_call(
        qkv_body,
        grid=(length // block,),
        in_specs=[
            by_rows(depth),
            whole((depth, wide)),
            whole((depth, wide // 2)),
            whole((1, 3 * wide // 2)),
            by_rows(PAIR),
            by_rows(PAIR),
        ],
        out_specs=[by_rows(wide), by_rows(wide // 2)],
        out_shape=[
            jax.ShapeDtypeStruct((length, wide), BF16),
            jax.ShapeDtypeStruct((length, wide // 2), BF16),
        ],
        compiler_params=pltpu.CompilerParams(vmem_limit_bytes=48 * MIB),
        cost_estimate=pl.CostEstimate(
            flops=3 * length * depth * wide, bytes_accessed=8 * length * depth, transcendentals=0
        ),
        name="project_qkv",
    )(rows, weight_qk, weight_vo, bias_row, cos_table, sin_table)


def forward_body(block, count, place_ref, q_ref, k_ref, v_ref, down_ref, across_ref, mixed_ref, lse_ref):
    place = place_ref[0]
    lane = lax.broadcasted_iota(jnp.int32, (block, PAIR), 1)
    earlier = lax.broadcasted_iota(jnp.int32, (block, block), 0) <= lax.broadcasted_iota(
        jnp.int32, (block, block), 1
    )
    spans = [
        pl.ds(pl.multiple_of(jnp.bitwise_xor(i, place) * block, block), block) for i in range(count)
    ]
    for i in range(count):
        queries = q_ref[spans[i], :] * jnp.asarray(HD**-0.5, BF16)
        segment = across_ref[:, spans[i]]
        kept = [down_ref[spans[j], :] == segment for j in range(i + 1)]
        kept[i] = kept[i] & earlier
        sums = []
        for half in range(2):
            mine = lane < HD if half == 0 else lane >= HD
            chosen = jnp.where(mine, queries, jnp.zeros_like(queries))
            scores = [
                jnp.where(kept[j], product(k_ref[spans[j], :], chosen, 1, 1), NEGATIVE)
                for j in range(i + 1)
            ]
            top = scores[0].max(0, keepdims=True)
            for part in scores[1:]:
                top = jnp.maximum(top, part.max(0, keepdims=True))
            raised = [jnp.exp(part - top) for part in scores]
            total = raised[0].sum(0, keepdims=True)
            for part in raised[1:]:
                total = total + part.sum(0, keepdims=True)
            inverse = 1.0 / total
            out = None
            for j in range(i + 1):
                term = product((raised[j] * inverse).astype(BF16), v_ref[spans[j], :], 0, 0)
                out = term if out is None else out + term
            sums.append(out)
            lse_ref[0, half : half + 1, spans[i]] = top + jnp.log(total)
        mixed_ref[spans[i], :] = jnp.where(lane < HD, sums[0], sums[1]).astype(BF16)


def attend_forward(place, qk, values, segment_down, segment_across, count):
    length, width = values.shape
    pairs = width // PAIR
    columns = lambda first: pl.BlockSpec((length, PAIR), lambda h, place: (0, h + first))
    whole = lambda shape: pl.BlockSpec(shape, lambda h, place: (0, 0))
    return pl.pallas_call(
        functools.partial(forward_body, length // count, count),
        grid_spec=pltpu.PrefetchScalarGridSpec(
            num_scalar_prefetch=1,
            grid=(pairs,),
            in_specs=[columns(0), columns(pairs), columns(0), whole((length, 1)), whole((1, length))],
            out_specs=[columns(0), pl.BlockSpec((1, 2, length), lambda h, place: (h, 0, 0))],
        ),
        out_shape=[
            jax.ShapeDtypeStruct((length, width), BF16),
            jax.ShapeDtypeStruct((pairs, 2, length), F32),
        ],
        compiler_params=pltpu.CompilerParams(vmem_limit_bytes=48 * MIB),
        cost_estimate=pl.CostEstimate(
            flops=4 * length * length * width,
            bytes_accessed=8 * length * width,
            transcendentals=length * length * width // PAIR,
        ),
        name="attend_forward",
    )(place, qk, qk, values, segment_down, segment_across)


def backward_body(
    block,
    count,
    place_ref,
    q_ref,
    k_ref,
    v_ref,
    mixed_ref,
    grad_ref,
    lse_ref,
    down_ref,
    across_ref,
    cos_ref,
    sin_ref,
    q_grad_ref,
    k_grad_ref,
    v_grad_ref,
    bias_ref,
    q_total,
    k_total,
    v_total,
):
    place = place_ref[0]
    lane = lax.broadcasted_iota(jnp.int32, (block, PAIR), 1)
    earlier = lax.broadcasted_iota(jnp.int32, (block, block), 0) <= lax.broadcasted_iota(
        jnp.int32, (block, block), 1
    )
    spans = [
        pl.ds(pl.multiple_of(jnp.bitwise_xor(i, place) * block, block), block) for i in range(count)
    ]
    for i in range(count):
        queries = q_ref[spans[i], :] * jnp.asarray(HD**-0.5, BF16)
        upstream = grad_ref[spans[i], :]
        centres = (upstream.astype(F32) * mixed_ref[spans[i], :].astype(F32)).T
        segment = across_ref[:, spans[i]]
        kept = [down_ref[spans[j], :] == segment for j in range(i + 1)]
        kept[i] = kept[i] & earlier
        sums = []
        for half in range(2):
            mine = lane < HD if half == 0 else lane >= HD
            nothing = jnp.zeros_like(queries)
            chosen = jnp.where(mine, queries, nothing)
            chosen_grad = jnp.where(mine, upstream, nothing)
            log_total = lse_ref[0, half : half + 1, spans[i]]
            centre = centres[half * HD : (half + 1) * HD, :].sum(0, keepdims=True)
            q_sum = None
            for j in range(i + 1):
                keys = k_ref[spans[j], :]
                scores = jnp.where(kept[j], product(keys, chosen, 1, 1), NEGATIVE)
                weights = jnp.exp(scores - log_total)
                weight_grad = product(v_ref[spans[j], :], chosen_grad, 1, 1)
                score_grad = (weights * (weight_grad - centre)).astype(BF16)
                v_term = product(weights.astype(BF16), chosen_grad, 1, 0)
                k_term = product(score_grad, chosen, 1, 0)
                term = product(score_grad, keys, 0, 0)
                q_sum = term if q_sum is None else q_sum + term
                if i == j and half == 0:
                    v_total[spans[j], :] = v_term
                    k_total[spans[j], :] = k_term
                else:
                    v_total[spans[j], :] += v_term
                    k_total[spans[j], :] += k_term
            sums.append(q_sum)
        q_total[spans[i], :] = jnp.where(lane < HD, sums[0], sums[1])
    opening = opening_lanes(block * count)
    cos_values = cos_ref[...]
    sin_values = -sin_ref[...]
    q_grad = turn(q_total[...] * (HD**-0.5), cos_values, sin_values, opening).astype(BF16)
    k_grad = turn(k_total[...], cos_values, sin_values, opening).astype(BF16)
    v_grad = v_total[...].astype(BF16)
    for at, (ref, grad) in enumerate(
        ((q_grad_ref, q_grad), (k_grad_ref, k_grad), (v_grad_ref, v_grad))
    ):
        ref[...] = grad
        bias_ref[0, at : at + 1, :] = grad.astype(F32).sum(0, keepdims=True)


def attend_backward(
    place, qk, values, mixed, mixed_grad, lse, segment_down, segment_across, cos_table, sin_table, count
):
    length, width = values.shape
    pairs = width // PAIR
    columns = lambda first: pl.BlockSpec((length, PAIR), lambda h, place: (0, h + first))
    whole = lambda shape: pl.BlockSpec(shape, lambda h, place: (0, 0))
    return pl.pallas_call(
        functools.partial(backward_body, length // count, count),
        grid_spec=pltpu.PrefetchScalarGridSpec(
            num_scalar_prefetch=1,
            grid=(pairs,),
            in_specs=[
                columns(0),
                columns(pairs),
                columns(0),
                columns(0),
                columns(0),
                pl.BlockSpec((1, 2, length), lambda h, place: (h, 0, 0)),
                whole((length, 1)),
                whole((1, length)),
                whole((length, PAIR)),
                whole((length, PAIR)),
            ],
            out_specs=[
                columns(0),
                columns(0),
                columns(0),
                pl.BlockSpec((1, 3, PAIR), lambda h, place: (h, 0, 0)),
            ],
            scratch_shapes=[pltpu.VMEM((length, PAIR), F32)] * 3,
        ),
        out_shape=[jax.ShapeDtypeStruct((length, width), BF16)] * 3
        + [jax.ShapeDtypeStruct((pairs, 3, PAIR), F32)],
        compiler_params=pltpu.CompilerParams(vmem_limit_bytes=48 * MIB),
        cost_estimate=pl.CostEstimate(
            flops=10 * length * length * width,
            bytes_accessed=20 * length * width,
            transcendentals=length * length * width // PAIR,
        ),
        name="attend_backward",
    )(
        place, qk, qk, values, mixed, mixed_grad, lse, segment_down, segment_across, cos_table, sin_table
    )


class Route:
    def __init__(self, count):
        self.count = count
        self.reach = count // 2
        self.ring = list(range(0, count, 2)) + list(range(count - 1, 0, -2))
        ahead = [(self.ring[i], self.ring[(i + 1) % count]) for i in range(count)]
        self.pairs = (ahead, [(b, a) for a, b in ahead])

    def send(self, values, direction):
        return lax.ppermute(values, "dp", self.pairs[direction])


class Gathering:
    def __init__(self, route, block, longer):
        self.route = route
        self.blocks = {0: block}
        self.hops = [route.reach - (direction != longer) for direction in range(2)]
        self.done = 0
        self.flying = [block]

    def pending(self):
        return self.flying

    def resume(self, arrived):
        route = self.route
        if self.done == 0:
            self.blocks[0] = arrived[0]
            latest = [arrived[0], arrived[0]]
        else:
            arrived = list(arrived)
            latest = [None, None]
            for direction in range(2):
                if self.done <= self.hops[direction]:
                    latest[direction] = arrived.pop(0)
                    at = route.count - self.done if direction == 0 else self.done
                    self.blocks[at] = latest[direction]
        self.done += 1
        self.flying = [
            route.send(latest[direction], direction)
            for direction in range(2)
            if self.done <= self.hops[direction]
        ]

    def all(self, axis):
        return jnp.concatenate([self.blocks[j] for j in range(self.route.count)], axis=axis)


class Summing:
    def __init__(self, route, own, longer):
        self.route = route
        self.own = own
        self.hops = [route.reach - (direction != longer) for direction in range(2)]
        self.done = 0
        self.flying = None
        self.last = [None, None]

    def target(self, direction):
        left = self.hops[direction] - self.done
        return left if direction == 0 else (self.route.count - left) % self.route.count

    def pending(self):
        if self.done == 0:
            return [self.own(self.target(direction)) for direction in range(2)]
        return self.flying

    def resume(self, arrived):
        arrived = list(arrived)
        sending = []
        for direction in range(2):
            if self.done <= self.hops[direction]:
                values = arrived.pop(0)
                if self.done == self.hops[direction]:
                    self.last[direction] = values
                    continue
                if self.done:
                    own = self.own(self.target(direction))
                    values = (values.astype(F32) + own.astype(F32)).astype(BF16)
                sending.append((direction, values))
        self.done += 1
        self.flying = [self.route.send(values, direction) for direction, values in sending]

    def total(self):
        return self.own(0).astype(F32) + self.last[0].astype(F32) + self.last[1].astype(F32)


STEPS = 10


class Flow:
    def __init__(self, first, second):
        self.streams = (first, second)
        self.events = 2 * first.route.reach + 2
        self.event = 0
        self.step = 0

    def moves(self):
        self.event += 1
        event = self.event - 1
        stream = self.streams[event % 2]
        return [stream]

    def due(self):
        return self.event * STEPS < self.step * self.events


def advance(flows, *carried):
    for flow in flows:
        flow.step += 1
    first = True
    while first or any(flow.due() for flow in flows):
        first = False
        moving = [stream for flow in flows if flow.due() for stream in flow.moves()]
        waiting = [list(stream.pending()) for stream in moving]
        flat = [values for group in waiting for values in group]
        out = lax.optimization_barrier(tuple(flat) + tuple(carried))
        carried = out[len(flat) :]
        at = 0
        for stream, group in zip(moving, waiting):
            stream.resume(out[at : at + len(group)])
            at += len(group)
    return carried[0] if len(carried) == 1 else carried


def standardize(inputs):
    average = jnp.mean(inputs, axis=-1, keepdims=True)
    centred = inputs - average
    inverse = lax.rsqrt(jnp.mean(centred * centred, axis=-1, keepdims=True) + EPSILON)
    return centred * inverse, average, inverse


def norm_backward(upstream, standard, inverse, gain_vec):
    scaled = upstream * gain_vec
    inner = (
        scaled
        - jnp.mean(scaled, axis=-1, keepdims=True)
        - standard * jnp.mean(scaled * standard, axis=-1, keepdims=True)
    )
    return inverse * inner


def turning_tables(segment_ids):
    length = segment_ids.shape[0]
    places = jnp.arange(length, dtype=jnp.int32)
    starts = jnp.concatenate([jnp.ones((1,), dtype=jnp.bool_), segment_ids[1:] != segment_ids[:-1]])
    begins = lax.cummax(jnp.where(starts, places, 0), axis=0)
    return (places - begins).astype(F32)


def across_core(values):
    return lax.ppermute(values, "tensor", [(i, i ^ 1) for i in range(4)])


def across_chip(values):
    return lax.ppermute(values, "tensor", [(i, i ^ 2) for i in range(4)])


def on_device(
    route,
    activations,
    cotangent,
    segments,
    norm_one_gain,
    norm_one_bias,
    w_query,
    w_key,
    w_value,
    qkv_bias,
    w_out,
    norm_two_gain,
    norm_two_bias,
    w_gate,
    w_up,
    w_down,
):
    count = route.count
    own_rows, depth = activations.shape
    length = segments.shape[0]
    width = depth // count
    heads_wide = w_query.shape[1]
    local_heads = heads_wide // HD
    hidden_wide = w_gate.shape[1]
    shards = length // own_rows
    here = lax.axis_index("tensor")
    ring = jnp.array(route.ring, jnp.int32)
    positions = jnp.array([route.ring.index(i) for i in range(count)], jnp.int32)
    position = positions[lax.axis_index("dp")]
    order = ring[(position + jnp.arange(count, dtype=jnp.int32)) % count]
    back_order = (positions - position) % count

    def pick_columns(values, chosen):
        return jnp.concatenate(
            [
                lax.dynamic_slice_in_dim(values, chosen[j] * width, width, axis=-1)
                for j in range(count)
            ],
            axis=-1,
        )

    def pick_rows(values):
        return jnp.concatenate(
            [
                lax.dynamic_slice_in_dim(
                    values, jnp.bitwise_xor(i, here) * own_rows, own_rows, axis=0
                )
                for i in range(shards)
            ],
            axis=0,
        )

    own_bf16 = pick_columns(activations, order)
    own_grad = pick_columns(cotangent, order)
    own_inputs = own_bf16.astype(F32)

    bias_size = qkv_bias.size
    norm_part = norm_one_gain.shape[0]
    packed = jnp.concatenate(
        [norm_one_gain, norm_one_bias, norm_two_gain, norm_two_bias, qkv_bias.reshape(-1)]
    )
    packed = jnp.pad(packed, (0, 16 * 128 - packed.shape[0])).reshape(16, 128)
    small = lax.all_gather(packed, ("dp", "tensor"), axis=0, tiled=True)

    flow_one = Flow(
        Gathering(route, jnp.concatenate([w_query, w_key], axis=1), 0),
        Gathering(route, jnp.concatenate([w_value, w_out.T], axis=1), 1),
    )
    flow_two = Flow(Gathering(route, w_gate, 0), Gathering(route, w_up, 1))
    flow_three = Flow(
        Gathering(route, w_down[: hidden_wide // 2], 0),
        Gathering(route, w_down[hidden_wide // 2 :], 1),
    )

    x_chip = across_chip(own_bf16)
    x_core = across_core(own_bf16)
    advance([flow_one])
    advance([flow_one])
    within = turning_tables(segments)
    frequency = 10000.0 ** (-2.0 * jnp.arange(ROT // 2, dtype=F32) / ROT)
    within = pick_rows(within)
    angles = within[:, None] * frequency[None, :]
    cos_part, sin_part = jnp.cos(angles), jnp.sin(angles)
    rest = jnp.zeros((length, HD - ROT), F32)
    cos_table = jnp.concatenate([cos_part, cos_part, rest + 1.0] * 2, axis=1)
    sin_table = jnp.concatenate([-sin_part, sin_part, rest] * 2, axis=1)
    segment_rel = pick_rows(segments)
    segment_down, segment_across = segment_rel[:, None], segment_rel[None, :]
    place = here.astype(jnp.int32).reshape(1)
    x_core, cos_table, sin_table = advance([flow_one], x_core, cos_table, sin_table)
    x_chip, own_grad = advance([flow_one], x_chip, own_grad)
    x_far = across_core(x_chip)
    g_chip = across_chip(own_grad)
    g_core = across_core(own_grad)
    x_far, small, g_core = advance([flow_one], x_far, small, g_core)

    table = small.reshape(count, shards, 16 * 128)
    norm_values = [
        table[:, :, k * norm_part : (k + 1) * norm_part].reshape(1, depth).astype(F32)
        for k in range(4)
    ]
    gain_one, shift_one, gain_two, shift_two = (pick_columns(v, order) for v in norm_values)
    bias_row = lax.dynamic_index_in_dim(table, here, axis=1, keepdims=False)
    bias_row = bias_row[:, 4 * norm_part : 4 * norm_part + bias_size]
    bias_row = bias_row.reshape(count, 3, local_heads, HD // count).transpose(1, 2, 0, 3)
    bias_row = bias_row.reshape(1, 3 * heads_wide).astype(F32)

    x_all = jnp.concatenate([own_bf16, x_core, x_chip, x_far], axis=0)
    standard_one, mean_one, inverse_one = standardize(x_all.astype(F32))
    normed = (standard_one * gain_one + shift_one).astype(BF16)
    normed, x_all, mean_one, inverse_one, gain_two, shift_two, bias_row = advance(
        [flow_one], normed, x_all, mean_one, inverse_one, gain_two, shift_two, bias_row
    )
    g_chip = advance([flow_one, flow_two], g_chip)
    g_far = across_core(g_chip)
    g_far = advance([flow_one, flow_two], g_far)
    grad_all = jnp.concatenate([own_grad, g_core, g_chip, g_far], axis=0)
    grad_all = advance([flow_one], grad_all)
    advance([flow_one, flow_two])
    weight_qk = flow_one.streams[0].all(0)
    weight_vo = flow_one.streams[1].all(0)
    weight_out = weight_vo[:, heads_wide:]

    qk, values = project_qkv(normed, weight_qk, weight_vo, bias_row, cos_table, sin_table)
    qk, values, weight_out = advance([flow_two], qk, values, weight_out)
    mixed, lse = attend_forward(place, qk, values, segment_down, segment_across, shards)
    mixed, lse = advance([flow_two], mixed, lse)

    half = length // 2
    third = own_rows

    def sum_over_heads(far):
        crossed = across_core(far[third:])
        return (far[:third].astype(F32) + crossed.astype(F32)).astype(BF16)

    far = product(mixed[half:], weight_out, 1, 1).astype(BF16)
    far_sum = sum_over_heads(far)
    arriving = across_chip(far_sum)
    near = product(mixed[:half], weight_out, 1, 1).astype(BF16)
    near_core = across_core(near[third:])
    near, near_core = advance([flow_two], near, near_core)
    near_sum = own_inputs + near[:third].astype(F32) + near_core.astype(F32)
    arriving, near_sum = advance([flow_two], arriving, near_sum)
    middle = near_sum + arriving.astype(F32)
    standard_two, _, inverse_two = standardize(middle)
    normed_two_own = (standard_two * gain_two + shift_two).astype(BF16)
    n_chip = across_chip(normed_two_own)
    n_core = across_core(normed_two_own)
    middle, standard_two, inverse_two, normed_two_own, n_core = advance(
        [flow_two, flow_three], middle, standard_two, inverse_two, normed_two_own, n_core
    )
    n_chip = advance([flow_two, flow_three], n_chip)
    n_far = across_core(n_chip)
    n_far = advance([flow_two, flow_three], n_far)
    normed_two = jnp.concatenate([normed_two_own, n_core, n_chip, n_far], axis=0)
    normed_two = advance([flow_three], normed_two)

    weight_gate = flow_two.streams[0].all(0)
    weight_up = flow_two.streams[1].all(0)
    gate_values = product(normed_two, weight_gate, 1, 0)
    gate_values, weight_up = advance([flow_three], gate_values, weight_up)
    up_values = product(normed_two, weight_up, 1, 0)
    sigmoid_gate = jax.nn.sigmoid(gate_values)
    silu_gate = gate_values * sigmoid_gate
    hidden = (silu_gate * up_values).astype(BF16)
    hidden, up_values = advance([flow_three], hidden, up_values)
    down_grad = product(hidden, grad_all, 0, 0).astype(BF16)
    down_grad = advance([flow_three], down_grad)
    block = lambda j: slice(j * width, (j + 1) * width)
    back_one = Flow(
        Summing(route, lambda j: down_grad[: hidden_wide // 2, block(j)], 0),
        Summing(route, lambda j: down_grad[hidden_wide // 2 :, block(j)], 1),
    )
    advance([flow_three, back_one])
    advance([flow_three, back_one])
    advance([flow_three])
    down_blocks = [stream.all(1) for stream in flow_three.streams]
    weight_down = jnp.concatenate(down_blocks, axis=0)

    hidden_grad = product(grad_all, weight_down, 1, 1)
    gate_grad = (hidden_grad * up_values * (sigmoid_gate + silu_gate * (1.0 - sigmoid_gate))).astype(
        BF16
    )
    up_grad = (hidden_grad * silu_gate).astype(BF16)
    gate_grad, up_grad = advance([back_one], gate_grad, up_grad)

    def through_gates(rows):
        return (
            product(gate_grad[rows], weight_gate, 1, 1) + product(up_grad[rows], weight_up, 1, 1)
        ).astype(BF16)

    far = through_gates(slice(half, None))
    far = advance([back_one], far)
    far_sum = sum_over_heads(far)
    arriving = across_chip(far_sum)
    near = through_gates(slice(0, half))
    near_core = across_core(near[third:])
    near, near_core = advance([back_one], near, near_core)
    gate_sum = product(normed_two, gate_grad, 0, 0).astype(BF16)
    gate_sum = advance([back_one], gate_sum)
    up_sum = product(normed_two, up_grad, 0, 0).astype(BF16)
    near_sum = near[:third].astype(F32) + near_core.astype(F32)
    up_sum, near_sum, arriving = advance([back_one], up_sum, near_sum, arriving)
    back_two = Flow(
        Summing(route, lambda j: gate_sum[block(j)], 0),
        Summing(route, lambda j: up_sum[block(j)], 1),
    )
    advance([back_one, back_two])
    normed_two_grad = near_sum + arriving.astype(F32)
    middle_grad = own_grad.astype(F32) + norm_backward(
        normed_two_grad, standard_two, inverse_two, gain_two
    )
    gain_two_grad = jnp.sum(normed_two_grad * standard_two, axis=0, keepdims=True)
    shift_two_grad = jnp.sum(normed_two_grad, axis=0, keepdims=True)
    branch_own = middle_grad.astype(BF16)
    b_chip = across_chip(branch_own)
    b_core = across_core(branch_own)
    middle_grad, branch_own, gain_two_grad, shift_two_grad, b_core = advance(
        [back_one, back_two], middle_grad, branch_own, gain_two_grad, shift_two_grad, b_core
    )
    far_result = product(hidden[half:], weight_down, 1, 0).astype(BF16)
    far_result = advance([back_one, back_two], far_result)
    near_result = product(hidden[:half], weight_down, 1, 0).astype(BF16)
    near_result, b_chip = advance([back_two], near_result, b_chip)
    b_far = across_core(b_chip)
    far_sum = sum_over_heads(far_result)
    arriving_result = across_chip(far_sum)
    near_core = across_core(near_result[third:])
    b_far, near_core = advance([back_two], b_far, near_core)
    branch = jnp.concatenate([branch_own, b_core, b_chip, b_far], axis=0)
    mixed_grad = product(branch, weight_out, 1, 0).astype(BF16)
    near_sum = middle + near_result[:third].astype(F32) + near_core.astype(F32)
    mixed_grad, branch, near_sum = advance([back_two], mixed_grad, branch, near_sum)
    q_grad, k_grad, v_grad, bias_sums = attend_backward(
        place,
        qk,
        values,
        mixed,
        mixed_grad,
        lse,
        segment_down,
        segment_across,
        cos_table,
        sin_table,
        shards,
    )
    q_grad, k_grad, v_grad, bias_sums, arriving_result = advance(
        [back_two], q_grad, k_grad, v_grad, bias_sums, arriving_result
    )
    result = pick_columns((near_sum + arriving_result.astype(F32)).astype(BF16), back_order)

    def through_heads(rows):
        return (
            product(q_grad[rows], weight_qk[:, :heads_wide], 1, 1)
            + product(k_grad[rows], weight_qk[:, heads_wide:], 1, 1)
            + product(v_grad[rows], weight_vo[:, :heads_wide], 1, 1)
        )

    far_whole = through_heads(slice(half, None))
    far_sum = sum_over_heads(far_whole.astype(BF16))
    arriving = across_chip(far_sum)
    out_sum = product(branch, mixed, 0, 0).astype(BF16)
    v_sum = product(normed, v_grad, 0, 0).astype(BF16)
    out_sum, v_sum, far_whole, result = advance([back_two], out_sum, v_sum, far_whole, result)
    near_whole = through_heads(slice(0, half))
    near = near_whole.astype(BF16)
    near_core = across_core(near[third:])

    def token_sums(rows, upstream):
        standard = (x_all[rows].astype(F32) - mean_one[rows]) * inverse_one[rows]
        return jnp.concatenate(
            [
                jnp.sum(upstream * standard, axis=0, keepdims=True),
                jnp.sum(upstream, axis=0, keepdims=True),
            ],
            axis=0,
        )

    one_grads = token_sums(slice(half, None), far_whole) + token_sums(slice(0, half), near_whole)
    q_sum = product(normed, q_grad, 0, 0).astype(BF16)
    k_sum = product(normed, k_grad, 0, 0).astype(BF16)
    near, near_core, one_grads, q_sum, k_sum = advance(
        [back_two], near, near_core, one_grads, q_sum, k_sum
    )
    norm_grads = jnp.concatenate([one_grads, gain_two_grad, shift_two_grad], axis=0)
    bias_sums = bias_sums.transpose(1, 0, 2).reshape(3, local_heads, count, HD // count)
    bias_sums = jnp.take(bias_sums, order, axis=2).transpose(2, 0, 1, 3).reshape(count, bias_size)
    extras = jnp.concatenate(
        [norm_grads.reshape(4, count, width).transpose(1, 0, 2).reshape(count, 4 * width), bias_sums],
        axis=1,
    )
    wide = 2 * heads_wide
    extras = jnp.pad(extras, ((0, 0), (0, 16 * wide - extras.shape[1])))
    extras = extras.reshape(count, 16, wide).astype(BF16)
    back_three = Flow(
        Summing(
            route, lambda j: jnp.concatenate([v_sum[block(j)], out_sum[block(j)]], axis=1), 0
        ),
        Summing(
            route,
            lambda j: jnp.concatenate(
                [jnp.concatenate([q_sum[block(j)], k_sum[block(j)]], axis=1), extras[j]], axis=0
            ),
            1,
        ),
    )
    advance([back_three])
    advance([back_two, back_three])
    advance([back_three])
    near_sum = near[:third].astype(F32) + near_core.astype(F32)
    arriving, near_sum = advance([back_three], arriving, near_sum)
    normed_grad = near_sum + arriving.astype(F32)
    standard_own = (own_inputs - mean_one[:third]) * inverse_one[:third]
    input_part = norm_backward(normed_grad, standard_own, inverse_one[:third], gain_one)
    input_grad = pick_columns((middle_grad + input_part).astype(BF16), back_order)
    input_grad = advance([back_three], input_grad)
    for _ in range(5):
        input_grad = advance([back_three], input_grad)

    v_o = back_three.streams[0].total()
    q_k = back_three.streams[1].total()
    small_sums = q_k[width:].reshape(-1)
    norm_sums = small_sums[: 4 * width].reshape(4, width)
    norm_sums = norm_sums + across_core(norm_sums)
    norm_sums = norm_sums + across_chip(norm_sums)
    norm_sums = lax.dynamic_slice_in_dim(norm_sums, here * norm_part, norm_part, axis=1)
    bias_grad = small_sums[4 * width : 4 * width + bias_size].reshape(qkv_bias.shape)
    grad_down = jnp.concatenate([stream.total() for stream in back_one.streams], axis=0)
    return (
        result,
        input_grad,
        norm_sums[0],
        norm_sums[1],
        q_k[:width, :heads_wide],
        q_k[:width, heads_wide:],
        v_o[:, :heads_wide],
        bias_grad,
        v_o[:, heads_wide:].T,
        norm_sums[2],
        norm_sums[3],
        back_two.streams[0].total(),
        back_two.streams[1].total(),
        grad_down,
    )


def solution(mesh):
    both = P(("dp", "tensor"))
    tokens = P(("dp", "tensor"), None)
    rows = P("dp", "tensor")
    columns = P("tensor", "dp")
    biases = P(None, "tensor", "dp")
    return jax.shard_map(
        functools.partial(on_device, Route(mesh.shape["dp"])),
        mesh=mesh,
        in_specs=(
            tokens,
            tokens,
            P("dp"),
            both,
            both,
            rows,
            rows,
            rows,
            biases,
            columns,
            both,
            both,
            rows,
            rows,
            columns,
        ),
        out_specs=(
            tokens,
            tokens,
            both,
            both,
            rows,
            rows,
            rows,
            biases,
            columns,
            both,
            both,
            rows,
            rows,
            columns,
        ),
        check_vma=False,
    )
```

```python
import functools

import jax
import jax.experimental.pallas as pl
import jax.experimental.pallas.tpu as pltpu
import jax.numpy as jnp
from jax import lax
from jax.sharding import PartitionSpec as P

HD = 64
ROT = 16
PAIR = 2 * HD
EPSILON = 1e-05
NEGATIVE = -1e30
F32 = jnp.float32
BF16 = jnp.bfloat16
MIB = 2**20
LIGHT = pl.CostEstimate(flops=10**9, bytes_accessed=1, transcendentals=1)
LONG = pl.CostEstimate(flops=5 * 10**10, bytes_accessed=1, transcendentals=1)


def product(left, right, left_dim, right_dim):
    return lax.dot_general(
        left, right, (((left_dim,), (right_dim,)), ((), ())), preferred_element_type=F32
    )


def turn(columns, cos_values, sin_values, opening):
    partner = jnp.where(opening, pltpu.roll(columns, PAIR - 8, 1), pltpu.roll(columns, 8, 1))
    return columns * cos_values + partner * sin_values


def opening_lanes(rows):
    return lax.broadcasted_iota(jnp.int32, (rows, PAIR), 1) % HD < 8


def forward_body(block, count, q_ref, k_ref, v_ref, down_ref, across_ref, mixed_ref, lse_ref):
    lane = lax.broadcasted_iota(jnp.int32, (block, PAIR), 1)
    earlier = lax.broadcasted_iota(jnp.int32, (block, block), 0) <= lax.broadcasted_iota(
        jnp.int32, (block, block), 1
    )
    spans = [pl.ds(i * block, block) for i in range(count)]
    for i in range(count):
        queries = q_ref[spans[i], :] * jnp.asarray(HD**-0.5, BF16)
        segment = across_ref[:, spans[i]]
        kept = [down_ref[spans[j], :] == segment for j in range(i + 1)]
        kept[i] = kept[i] & earlier
        sums = []
        for half in range(2):
            mine = lane < HD if half == 0 else lane >= HD
            chosen = jnp.where(mine, queries, jnp.zeros_like(queries))
            scores = [
                jnp.where(kept[j], product(k_ref[spans[j], :], chosen, 1, 1), NEGATIVE)
                for j in range(i + 1)
            ]
            top = scores[0].max(0, keepdims=True)
            for part in scores[1:]:
                top = jnp.maximum(top, part.max(0, keepdims=True))
            raised = [jnp.exp(part - top) for part in scores]
            total = raised[0].sum(0, keepdims=True)
            for part in raised[1:]:
                total = total + part.sum(0, keepdims=True)
            inverse = 1.0 / total
            out = None
            for j in range(i + 1):
                term = product((raised[j] * inverse).astype(BF16), v_ref[spans[j], :], 0, 0)
                out = term if out is None else out + term
            sums.append(out)
            lse_ref[0, half : half + 1, spans[i]] = top + jnp.log(total)
        mixed_ref[spans[i], :] = jnp.where(lane < HD, sums[0], sums[1]).astype(BF16)


def attend_forward(qk, values, segment_down, segment_across, count):
    length, width = values.shape
    pairs = width // PAIR
    columns = lambda first: pl.BlockSpec((length, PAIR), lambda h: (0, h + first))
    whole = lambda shape: pl.BlockSpec(shape, lambda h: (0, 0))
    return pl.pallas_call(
        functools.partial(forward_body, length // count, count),
        grid_spec=pltpu.PrefetchScalarGridSpec(
            num_scalar_prefetch=0,
            grid=(pairs,),
            in_specs=[columns(0), columns(pairs), columns(0), whole((length, 1)), whole((1, length))],
            out_specs=[columns(0), pl.BlockSpec((1, 2, length), lambda h: (h, 0, 0))],
        ),
        out_shape=[
            jax.ShapeDtypeStruct((length, width), BF16),
            jax.ShapeDtypeStruct((pairs, 2, length), F32),
        ],
        compiler_params=pltpu.CompilerParams(vmem_limit_bytes=60 * MIB),
        cost_estimate=LIGHT,
        name="attend_forward",
    )(qk, qk, values, segment_down, segment_across)


def backward_body(
    block,
    count,
    q_ref,
    k_ref,
    v_ref,
    mixed_ref,
    grad_ref,
    lse_ref,
    down_ref,
    across_ref,
    cos_ref,
    sin_ref,
    q_grad_ref,
    k_grad_ref,
    v_grad_ref,
    bias_ref,
    q_total,
    k_total,
    v_total,
):
    lane = lax.broadcasted_iota(jnp.int32, (block, PAIR), 1)
    earlier = lax.broadcasted_iota(jnp.int32, (block, block), 0) <= lax.broadcasted_iota(
        jnp.int32, (block, block), 1
    )
    spans = [pl.ds(i * block, block) for i in range(count)]
    for i in range(count):
        queries = q_ref[spans[i], :] * jnp.asarray(HD**-0.5, BF16)
        upstream = grad_ref[spans[i], :]
        centres = (upstream.astype(F32) * mixed_ref[spans[i], :].astype(F32)).T
        segment = across_ref[:, spans[i]]
        kept = [down_ref[spans[j], :] == segment for j in range(i + 1)]
        kept[i] = kept[i] & earlier
        sums = []
        for half in range(2):
            mine = lane < HD if half == 0 else lane >= HD
            nothing = jnp.zeros_like(queries)
            chosen = jnp.where(mine, queries, nothing)
            chosen_grad = jnp.where(mine, upstream, nothing)
            log_total = lse_ref[0, half : half + 1, spans[i]]
            centre = centres[half * HD : (half + 1) * HD, :].sum(0, keepdims=True)
            q_sum = None
            for j in range(i + 1):
                keys = k_ref[spans[j], :]
                scores = jnp.where(kept[j], product(keys, chosen, 1, 1), NEGATIVE)
                weights = jnp.exp(scores - log_total)
                weight_grad = product(v_ref[spans[j], :], chosen_grad, 1, 1)
                score_grad = (weights * (weight_grad - centre)).astype(BF16)
                v_term = product(weights.astype(BF16), chosen_grad, 1, 0)
                k_term = product(score_grad, chosen, 1, 0)
                term = product(score_grad, keys, 0, 0)
                q_sum = term if q_sum is None else q_sum + term
                if i == j and half == 0:
                    v_total[spans[j], :] = v_term
                    k_total[spans[j], :] = k_term
                else:
                    v_total[spans[j], :] += v_term
                    k_total[spans[j], :] += k_term
            sums.append(q_sum)
        q_total[spans[i], :] = jnp.where(lane < HD, sums[0], sums[1])
    opening = opening_lanes(block * count)
    cos_values = cos_ref[...]
    sin_values = -sin_ref[...]
    q_grad = turn(q_total[...] * (HD**-0.5), cos_values, sin_values, opening).astype(BF16)
    k_grad = turn(k_total[...], cos_values, sin_values, opening).astype(BF16)
    v_grad = v_total[...].astype(BF16)
    for at, (ref, grad) in enumerate(
        ((q_grad_ref, q_grad), (k_grad_ref, k_grad), (v_grad_ref, v_grad))
    ):
        ref[...] = grad
        bias_ref[0, at : at + 1, :] = grad.astype(F32).sum(0, keepdims=True)


def attend_backward(
    qk, values, mixed, mixed_grad, lse, segment_down, segment_across, cos_table, sin_table, count
):
    length, width = values.shape
    pairs = width // PAIR
    columns = lambda first: pl.BlockSpec((length, PAIR), lambda h: (0, h + first))
    whole = lambda shape: pl.BlockSpec(shape, lambda h: (0, 0))
    return pl.pallas_call(
        functools.partial(backward_body, length // count, count),
        grid_spec=pltpu.PrefetchScalarGridSpec(
            num_scalar_prefetch=0,
            grid=(pairs,),
            in_specs=[
                columns(0),
                columns(pairs),
                columns(0),
                columns(0),
                columns(0),
                pl.BlockSpec((1, 2, length), lambda h: (h, 0, 0)),
                whole((length, 1)),
                whole((1, length)),
                whole((length, PAIR)),
                whole((length, PAIR)),
            ],
            out_specs=[
                columns(0),
                columns(0),
                columns(0),
                pl.BlockSpec((1, 3, PAIR), lambda h: (h, 0, 0)),
            ],
            scratch_shapes=[pltpu.VMEM((length, PAIR), F32)] * 3,
        ),
        out_shape=[jax.ShapeDtypeStruct((length, width), BF16)] * 3
        + [jax.ShapeDtypeStruct((pairs, 3, PAIR), F32)],
        compiler_params=pltpu.CompilerParams(vmem_limit_bytes=60 * MIB),
        cost_estimate=LONG,
        name="attend_backward",
    )(
        qk, qk, values, mixed, mixed_grad, lse, segment_down, segment_across, cos_table, sin_table
    )


HBM = pl.BlockSpec(memory_space=pl.ANY)


def whole(shape):
    return pl.BlockSpec(shape, lambda *_: (0,) * len(shape), pipeline_mode=pl.Buffered(1))


def shaped(shape, dtype=BF16):
    return jax.ShapeDtypeStruct(shape, dtype)


def kernel_call(body, name, operands, in_specs, out_specs, out_shape, grid=(), scratch=(), scalars=(), aliases=None, vmem=40, flops=1, kept=False):
    return pl.pallas_call(
        body,
        grid_spec=pltpu.PrefetchScalarGridSpec(
            num_scalar_prefetch=len(scalars),
            grid=grid,
            in_specs=in_specs,
            out_specs=out_specs,
            scratch_shapes=list(scratch),
        ),
        out_shape=out_shape,
        input_output_aliases=aliases or {},
        compiler_params=pltpu.CompilerParams(vmem_limit_bytes=vmem * MIB, has_side_effects=kept),
        cost_estimate=pl.CostEstimate(flops=flops, bytes_accessed=1, transcendentals=1),
        name=name,
    )(*scalars, *operands)


def copies_into(blocks, target, semaphores, first, columns=None, rows=None):
    copies, at = [], 0
    for i, block in enumerate(blocks):
        deep = rows or block.shape[0]
        source = block if columns is None else block.at[pl.ds(0, deep), columns]
        copies.append(
            pltpu.make_async_copy(source, target.at[pl.ds(at, deep), :], semaphores.at[first + i])
        )
        at += deep
    return copies


def start_all(step, copies):
    @pl.when(step == 0)
    def _():
        for copy in copies:
            copy.start()


def wait_at(step, when, copies):
    @pl.when(step == when)
    def _():
        for copy in copies:
            copy.wait()


def halves(copies):
    return copies[: len(copies) // 2], copies[len(copies) // 2 :]


def mark_body(in_ref, out_ref):
    out_ref[...] = in_ref[...]


def mark(token, flops):
    return kernel_call(
        mark_body,
        "mark",
        [token],
        [whole(token.shape)],
        whole(token.shape),
        shaped(token.shape, token.dtype),
        grid=(1,),
        flops=flops,
        kept=True,
    )


def pick_columns(order, values):
    count = order.shape[0]
    width = values.shape[1] // count
    parts = [lax.dynamic_slice_in_dim(values, order[j] * width, width, 1) for j in range(count)]
    return jnp.concatenate(parts, axis=1)


def back_in_place(order, values):
    count = order.shape[0]
    if values.shape[1] // count % 128 == 0:
        return values
    places = jnp.arange(count, dtype=jnp.int32)
    back = jnp.sum(jnp.where(order[:, None] == places[None, :], places[:, None], 0), axis=0)
    return pick_columns(back, values)


def reorder_body(count, width, order_ref, in_ref, out_ref):
    for j in range(count):
        source = pl.ds(pl.multiple_of(order_ref[j] * width, width), width)
        out_ref[:, j * width : (j + 1) * width] = in_ref[:, source]


def reorder(order, values):
    count = order.shape[0]
    if values.shape[1] // count % 128:
        return pick_columns(order, values)
    return kernel_call(
        functools.partial(reorder_body, count, values.shape[1] // count),
        "reorder",
        [values],
        [whole(values.shape)],
        whole(values.shape),
        shaped(values.shape),
        grid=(1,),
        scalars=[order],
    )


def put_back(order_ref, out_ref, values):
    count = order_ref.shape[0]
    width = values.shape[1] // count
    if width % 128:
        out_ref[...] = values.astype(out_ref.dtype)
        return
    for j in range(count):
        target = pl.ds(pl.multiple_of(order_ref[j] * width, width), width)
        out_ref[:, target] = values[:, j * width : (j + 1) * width].astype(out_ref.dtype)


def stats_body(x_ref, mean_ref, inverse_ref):
    values = x_ref[...].astype(F32)
    mean = jnp.mean(values, axis=-1, keepdims=True)
    centred = values - mean
    mean_ref[...] = mean
    inverse_ref[...] = lax.rsqrt(jnp.mean(centred * centred, axis=-1, keepdims=True) + EPSILON)


def row_stats(inputs):
    length, depth = inputs.shape
    by_rows = lambda columns: pl.BlockSpec((length // 4, columns), lambda i: (i, 0))
    return kernel_call(
        stats_body,
        "row_stats",
        [inputs],
        [by_rows(depth)],
        [by_rows(1)] * 2,
        [shaped((length, 1), F32)] * 2,
        grid=(4,),
    )


def decode_body(count, chunk, order_ref, *refs):
    blocks, norm_ref, bias_ref = refs[:count], refs[-2], refs[-1]
    width = norm_ref.shape[1] // count
    wide = bias_ref.shape[1]
    small = wide // count
    rows = []
    for j, block in enumerate(blocks):
        norm_ref[:, j * width : (j + 1) * width] = block[0:4, :width].astype(F32)
        rows.append(block[4:5, :small].astype(F32))
    lane = lax.broadcasted_iota(jnp.int32, (small, wide), 1)
    source = lax.broadcasted_iota(jnp.int32, (small, wide), 0)
    spread = (lane // HD * chunk + lane % chunk == source).astype(BF16)
    spread = product(jnp.concatenate(rows, axis=0).astype(BF16), spread, 1, 0)
    lane = lax.broadcasted_iota(jnp.int32, (1, wide), 1)
    total = jnp.zeros((1, wide), F32)
    for j in range(count):
        total = jnp.where(lane % HD // chunk == order_ref[j], spread[j : j + 1, :], total)
    bias_ref[...] = total


def decode(order, blocks, depth, bias_wide):
    count = len(blocks)
    rows, wide = blocks[0].shape
    return kernel_call(
        functools.partial(decode_body, count, HD // count),
        "decode",
        blocks,
        [pl.BlockSpec((16, wide), lambda i, order: (rows // 16 - 1, 0))] * count,
        [whole((4, depth)), whole((1, bias_wide))],
        [shaped((4, depth), F32), shaped((1, bias_wide), F32)],
        grid=(1,),
        scalars=[order],
    )


def qkv_body(count, x_ref, norm_ref, bias_ref, mean_ref, inverse_ref, cos_ref, sin_ref, *refs):
    blocks_a, blocks_b, refs = refs[:count], refs[count : 2 * count], refs[2 * count :]
    qk_ref, v_ref, normed_ref, weight_a, weight_v, semaphores = refs
    step = pl.program_id(0)
    width = qk_ref.shape[1]
    deep = weight_a.shape[0] // count
    copies_a = copies_into(blocks_a, weight_a, semaphores, 0, rows=deep)
    copies_v = copies_into(blocks_b, weight_v, semaphores, count, pl.ds(0, width // 2), deep)
    start_all(step, copies_a + copies_v)
    values = (x_ref[...].astype(F32) - mean_ref[...]) * inverse_ref[...]
    normed = (values * norm_ref[0:1, :] + norm_ref[1:2, :]).astype(BF16)
    normed_ref[...] = normed
    wait_at(step, 0, copies_a)
    both = product(normed, weight_a[...], 1, 0) + bias_ref[:, :width]
    opening = opening_lanes(normed.shape[0])
    cos_values = cos_ref[...]
    sin_values = sin_ref[...]
    for at in range(0, width, PAIR):
        part = turn(both[:, at : at + PAIR], cos_values, sin_values, opening)
        qk_ref[:, at : at + PAIR] = part.astype(BF16)
    wait_at(step, 0, copies_v)
    v_ref[...] = (product(normed, weight_v[...], 1, 0) + bias_ref[:, width:]).astype(BF16)


def project_qkv(inputs, mean, inverse, norm_rows, bias_row, cos_table, sin_table, blocks_a, blocks_b):
    length, depth = inputs.shape
    rows = length // 4
    wide = blocks_a[0].shape[1]
    count = len(blocks_a)
    by_rows = lambda columns: pl.BlockSpec((rows, columns), lambda i: (i, 0))
    return kernel_call(
        functools.partial(qkv_body, count),
        "project_qkv",
        [inputs, norm_rows, bias_row, mean, inverse, cos_table, sin_table, *blocks_a, *blocks_b],
        [
            by_rows(depth),
            whole(norm_rows.shape),
            whole(bias_row.shape),
            by_rows(1),
            by_rows(1),
            by_rows(PAIR),
            by_rows(PAIR),
        ]
        + [HBM] * (2 * count),
        [by_rows(wide), by_rows(wide // 2), by_rows(depth)],
        [shaped((length, wide)), shaped((length, wide // 2)), shaped((length, depth))],
        grid=(4,),
        flops=10**9,
        scratch=[
            pltpu.VMEM((depth, wide), BF16),
            pltpu.VMEM((depth, wide // 2), BF16),
            pltpu.SemaphoreType.DMA((2 * count,)),
        ],
        vmem=60,
    )


def gated_body(count, x_ref, *refs):
    gate_blocks, up_blocks, refs = refs[:count], refs[count : 2 * count], refs[2 * count :]
    gate_ref, up_ref, hidden_ref, gate_weight, up_weight, semaphores = refs[-6:]
    step = pl.program_id(0)
    early, late = halves(copies_into(gate_blocks, gate_weight, semaphores, 0))
    early_up, late_up = halves(copies_into(up_blocks, up_weight, semaphores, count))
    start_all(step, early + late + early_up + late_up)
    half = gate_weight.shape[0] // 2
    wait_at(step, 0, early)
    gate = product(x_ref[:, :half], gate_weight[:half, :], 1, 0)
    wait_at(step, 0, late)
    gate = gate + product(x_ref[:, half:], gate_weight[half:, :], 1, 0)
    gate_ref[...] = gate.astype(BF16)
    wait_at(step, 0, early_up + late_up)
    up = product(x_ref[...], up_weight[...], 1, 0)
    up_ref[...] = up.astype(BF16)
    hidden_ref[...] = (gate * jax.nn.sigmoid(gate) * up).astype(BF16)


def gated_forward(inputs, gate_blocks, up_blocks, half, kept):
    length, depth = inputs.shape
    rows = length // 4
    wide = gate_blocks[0].shape[1]
    count = len(gate_blocks)
    kept = list(kept or [])
    place = lambda columns: pl.BlockSpec((rows, columns), lambda i: (2 * half + i, 0))
    first = 1 + 2 * count
    return kernel_call(
        functools.partial(gated_body, count),
        "gated_forward",
        [inputs, *gate_blocks, *up_blocks, *kept],
        [place(depth)] + [HBM] * (2 * count + len(kept)),
        [place(wide)] * 3,
        [shaped((length, wide))] * 3,
        grid=(2,),
        flops=10**9,
        scratch=[
            pltpu.VMEM((depth, wide), BF16),
            pltpu.VMEM((depth, wide), BF16),
            pltpu.SemaphoreType.DMA((2 * count,)),
        ],
        aliases={first + i: i for i in range(len(kept))},
        vmem=60,
    )


def gated_back_body(count, *refs):
    grad_ref, gate_ref, up_ref, refs = refs[0], refs[1], refs[2], refs[3:]
    blocks = refs[:count]
    gate_grad_ref, up_grad_ref, weight, semaphores = refs[-4:]
    step = pl.program_id(0)
    early, late = halves(copies_into(blocks, weight, semaphores, 0))
    start_all(step, early + late)
    gate = gate_ref[...].astype(F32)
    sigmoid = jax.nn.sigmoid(gate)
    silu = gate * sigmoid
    slope = sigmoid + silu * (1.0 - sigmoid)
    half = weight.shape[0] // 2
    wait_at(step, 0, early)
    hidden_grad = product(grad_ref[:, :half], weight[:half, :], 1, 0)
    wait_at(step, 0, late)
    hidden_grad = hidden_grad + product(grad_ref[:, half:], weight[half:, :], 1, 0)
    up_grad_ref[...] = (hidden_grad * silu).astype(BF16)
    gate_grad_ref[...] = (hidden_grad * up_ref[...].astype(F32) * slope).astype(BF16)


def gated_backward(grads, gate, up, blocks):
    length, wide = gate.shape
    rows = length // 4
    depth = grads.shape[1]
    count = len(blocks)
    by_rows = lambda columns: pl.BlockSpec((rows, columns), lambda i: (i, 0))
    return kernel_call(
        functools.partial(gated_back_body, count),
        "gated_backward",
        [grads, gate, up, *blocks],
        [by_rows(depth), by_rows(wide), by_rows(wide)] + [HBM] * count,
        [by_rows(wide)] * 2,
        [shaped((length, wide))] * 2,
        grid=(4,),
        flops=10**9,
        scratch=[pltpu.VMEM((depth, wide), BF16), pltpu.SemaphoreType.DMA((count,))],
        vmem=60,
    )


STRIPES = 4


def outward_body(shape, columns, deep, *refs):
    lefts, refs = refs[: len(shape)], refs[len(shape) :]
    out_ref = refs[sum(shape)]
    weights, semaphores = refs[sum(shape) + 1 : -1], refs[-1]
    step = pl.program_id(0)
    at, groups = 0, []
    for count, weight, column in zip(shape, weights, columns):
        groups.append(
            copies_into(refs[at : at + count], weight, semaphores, at, column, deep)
        )
        at += count
    for stripe in range(STRIPES):
        start_all(
            step,
            [
                copy
                for group in groups
                for copy in group[stripe * len(group) // STRIPES : (stripe + 1) * len(group) // STRIPES]
            ],
        )
    for stripe in range(STRIPES):
        for group in groups:
            wait_at(
                step,
                stripe,
                group[stripe * len(group) // STRIPES : (stripe + 1) * len(group) // STRIPES],
            )
    tall = weights[0].shape[0] // STRIPES
    span = pl.ds(pl.multiple_of(step * tall, tall), tall)
    total = None
    for left, weight in zip(lefts, weights):
        term = product(left[...], weight[span, :], 1, 1)
        total = term if total is None else total + term
    out_ref[...] = total.astype(BF16)


def outward(parts, depth, name):
    lefts = [left for left, _, _ in parts]
    length = lefts[0].shape[0]
    shape = [len(blocks) for _, blocks, _ in parts]
    deep = None
    columns = []
    for left, blocks, column in parts:
        if column is None:
            columns.append(None)
        else:
            columns.append(pl.ds(column, left.shape[1]))
            deep = depth // len(blocks)
    return kernel_call(
        functools.partial(outward_body, shape, columns, deep),
        name,
        [*lefts, *(block for _, blocks, _ in parts for block in blocks)],
        [whole(left.shape) for left in lefts] + [HBM] * sum(shape),
        pl.BlockSpec((length, depth // STRIPES), lambda i: (0, i)),
        shaped((length, depth)),
        grid=(STRIPES,),
        flops=10**9,
        scratch=[pltpu.VMEM((depth, left.shape[1]), BF16) for left in lefts]
        + [pltpu.SemaphoreType.DMA((sum(shape),))],
        vmem=60,
    )


def mixed_grad_body(count, rows_ref, *refs):
    blocks = refs[:count]
    out_ref, weight, semaphores = refs[count:]
    step = pl.program_id(0)
    wide = weight.shape[1]
    copies = copies_into(blocks, weight, semaphores, 0, pl.ds(wide, wide), weight.shape[0] // count)
    start_all(step, copies)
    wait_at(step, 0, copies)
    out_ref[...] = product(rows_ref[...], weight[...], 1, 0).astype(BF16)


def through_out(branch, blocks):
    length, depth = branch.shape
    rows = length // 4
    wide = blocks[0].shape[1] // 2
    count = len(blocks)
    return kernel_call(
        functools.partial(mixed_grad_body, count),
        "through_out",
        [branch, *blocks],
        [pl.BlockSpec((rows, depth), lambda i: (i, 0))] + [HBM] * count,
        pl.BlockSpec((rows, wide), lambda i: (i, 0)),
        shaped((length, wide)),
        grid=(4,),
        flops=10**9,
        scratch=[pltpu.VMEM((depth, wide), BF16), pltpu.SemaphoreType.DMA((count,))],
        vmem=60,
    )


def heads_body(count, q_ref, k_ref, v_ref, x_ref, mean_ref, inverse_ref, *refs):
    blocks_a, blocks_b = refs[:count], refs[count : 2 * count]
    out_ref, sums_ref, weight_a, weight_v, semaphores = refs[2 * count :]
    step = pl.program_id(0)
    wide = q_ref.shape[1]
    deep = weight_a.shape[0] // count
    copies_a = copies_into(blocks_a, weight_a, semaphores, 0, rows=deep)
    copies_v = copies_into(blocks_b, weight_v, semaphores, count, pl.ds(0, wide), deep)
    start_all(step, [copy for pair in zip(copies_a, copies_v) for copy in pair])
    for stripe in range(STRIPES):
        span = slice(stripe * count // STRIPES, (stripe + 1) * count // STRIPES)
        wait_at(step, stripe, copies_a[span] + copies_v[span])
    tall = weight_a.shape[0] // STRIPES
    span = pl.ds(pl.multiple_of(step * tall, tall), tall)
    total = product(q_ref[...], weight_a[span, :wide], 1, 1)
    total = total + product(k_ref[...], weight_a[span, wide:], 1, 1)
    total = total + product(v_ref[...], weight_v[span, :], 1, 1)
    out_ref[...] = total.astype(BF16)
    standard = (x_ref[...].astype(F32) - mean_ref[...]) * inverse_ref[...]
    sums_ref[0:1, :] = (total * standard).sum(0, keepdims=True)
    sums_ref[1:2, :] = total.sum(0, keepdims=True)


def through_heads(grads, inputs, mean, inverse, blocks_a, blocks_b):
    length, wide = grads[0].shape
    depth = inputs.shape[1]
    count = len(blocks_a)
    striped = lambda tall: pl.BlockSpec((tall, depth // STRIPES), lambda i: (0, i))
    return kernel_call(
        functools.partial(heads_body, count),
        "through_heads",
        [*grads, inputs, mean, inverse, *blocks_a, *blocks_b],
        [whole((length, wide))] * 3
        + [striped(length), whole((length, 1)), whole((length, 1))]
        + [HBM] * (2 * count),
        [striped(length), striped(2)],
        [shaped((length, depth)), shaped((2, depth), F32)],
        grid=(STRIPES,),
        flops=10**9,
        scratch=[
            pltpu.VMEM((depth, 2 * wide), BF16),
            pltpu.VMEM((depth, wide), BF16),
            pltpu.SemaphoreType.DMA((2 * count,)),
        ],
        vmem=60,
    )


def added(refs):
    total = refs[0][...].astype(F32)
    for ref in refs[1:]:
        total = total + ref[...].astype(F32)
    return total


def second_norm_body(x_ref, term_ref, norm_ref, middle_ref, mean_ref, inverse_ref, out_ref):
    middle = added([x_ref, term_ref])
    middle_ref[...] = middle
    mean = jnp.mean(middle, axis=-1, keepdims=True)
    centred = middle - mean
    inverse = lax.rsqrt(jnp.mean(centred * centred, axis=-1, keepdims=True) + EPSILON)
    mean_ref[...] = mean
    inverse_ref[...] = inverse
    out_ref[...] = (centred * inverse * norm_ref[2:3, :] + norm_ref[3:4, :]).astype(BF16)


def second_norm(inputs, term, norm_rows):
    shape = inputs.shape
    column = (shape[0], 1)
    return kernel_call(
        second_norm_body,
        "second_norm",
        [inputs, term, norm_rows],
        [whole(shape)] * 2 + [whole(norm_rows.shape)],
        [whole(shape), whole(column), whole(column), whole(shape)],
        [shaped(shape, F32), shaped(column, F32), shaped(column, F32), shaped(shape)],
        grid=(1,),
    )


def norm_gradient(upstream, standard, inverse, gain):
    scaled = upstream * gain
    inner = (
        scaled
        - jnp.mean(scaled, axis=-1, keepdims=True)
        - standard * jnp.mean(scaled * standard, axis=-1, keepdims=True)
    )
    return inverse * inner


def second_back_body(upstream_ref, middle_ref, mean_ref, inverse_ref, norm_ref, grad_ref, full_ref, branch_ref, sums_ref):
    upstream = upstream_ref[...].astype(F32)
    inverse = inverse_ref[...]
    standard = (middle_ref[...] - mean_ref[...]) * inverse
    sums_ref[0:1, :] = (upstream * standard).sum(0, keepdims=True)
    sums_ref[1:2, :] = upstream.sum(0, keepdims=True)
    grad = grad_ref[...].astype(F32) + norm_gradient(upstream, standard, inverse, norm_ref[2:3, :])
    full_ref[...] = grad
    branch_ref[...] = grad.astype(BF16)


def second_norm_back(upstream, middle, mean, inverse, norm_rows, grads):
    shape = middle.shape
    column = (shape[0], 1)
    return kernel_call(
        second_back_body,
        "second_norm_back",
        [upstream, middle, mean, inverse, norm_rows, grads],
        [whole(shape)] * 2 + [whole(column)] * 2 + [whole(norm_rows.shape), whole(shape)],
        [whole(shape), whole(shape), whole((2, shape[1]))],
        [shaped(shape, F32), shaped(shape), shaped((2, shape[1]), F32)],
        grid=(1,),
    )


def input_back_body(order_ref, upstream_ref, x_ref, norm_ref, grad_ref, out_ref):
    values = x_ref[...].astype(F32)
    centred = values - jnp.mean(values, axis=-1, keepdims=True)
    inverse = lax.rsqrt(jnp.mean(centred * centred, axis=-1, keepdims=True) + EPSILON)
    upstream = upstream_ref[...].astype(F32)
    grad = grad_ref[...] + norm_gradient(upstream, centred * inverse, inverse, norm_ref[0:1, :])
    put_back(order_ref, out_ref, grad)


def input_back(order, upstream, inputs, norm_rows, grads):
    shape = inputs.shape
    out = kernel_call(
        input_back_body,
        "input_back",
        [upstream, inputs, norm_rows, grads],
        [whole(shape)] * 2 + [whole(norm_rows.shape), whole(shape)],
        whole(shape),
        shaped(shape),
        grid=(1,),
        scalars=[order],
    )
    return back_in_place(order, out)


def result_body(order_ref, middle_ref, term_ref, out_ref):
    put_back(order_ref, out_ref, added([middle_ref, term_ref]))


def finish_result(order, middle, term):
    shape = middle.shape
    out = kernel_call(
        result_body,
        "finish_result",
        [middle, term],
        [whole(shape)] * 2,
        whole(shape),
        shaped(shape),
        grid=(1,),
        scalars=[order],
    )
    return back_in_place(order, out)


def hand_on_body(arrivals, sides, *refs):
    arrived, own, outs = refs[:arrivals], refs[arrivals : -sides], refs[-sides:]
    parts = len(own) // sides
    for side in range(sides):
        first = 0
        for part in own[side * parts : (side + 1) * parts]:
            span = slice(first, first + part.shape[1])
            values = part[...]
            if arrivals:
                values = (values.astype(F32) + arrived[side][:, span].astype(F32)).astype(BF16)
            outs[side][:, span] = values
            first += part.shape[1]


def hand_on(arrived, own, rows, places):
    shape = (rows, sum(part.shape[1] for part in own))
    sides = len(places)
    return kernel_call(
        functools.partial(hand_on_body, len(arrived), sides),
        "hand_on",
        [*arrived, *(part for _ in places for part in own)],
        [whole(shape)] * len(arrived)
        + [
            pl.BlockSpec((rows, part.shape[1]), lambda i, at=at: (at, 0))
            for at in places
            for part in own
        ],
        [whole(shape)] * sides,
        [shaped(shape)] * sides,
        grid=(1,),
    )


class Route:
    def __init__(self, count):
        self.count = count
        self.reach = count // 2
        self.ring = list(range(0, count, 2)) + list(range(count - 1, 0, -2))
        ahead = [(self.ring[i], self.ring[(i + 1) % count]) for i in range(count)]
        self.pairs = (ahead, [(b, a) for a, b in ahead])

    def send(self, values, direction):
        return lax.ppermute(values, "dp", self.pairs[direction])


class Gathering:
    def __init__(self, route, block, longer):
        self.route = route
        self.blocks = {0: block}
        self.steps = 0
        self.hops = [route.reach - (direction != longer) for direction in range(2)]
        self.done = 0
        self.flying = [block]

    def pending(self):
        return self.flying

    def resume(self, arrived):
        route = self.route
        if self.done == 0:
            self.blocks[0] = arrived[0]
            latest = [arrived[0], arrived[0]]
        else:
            arrived = list(arrived)
            latest = [None, None]
            for direction in range(2):
                if self.done <= self.hops[direction]:
                    latest[direction] = arrived.pop(0)
                    at = route.count - self.done if direction == 0 else self.done
                    self.blocks[at] = latest[direction]
        self.done += 1
        self.flying = [
            route.send(latest[direction], direction)
            for direction in range(2)
            if self.done <= self.hops[direction]
        ]

    def all(self):
        return [self.blocks[j] for j in range(self.route.count)]


class Summing:
    def __init__(self, route, own, rows, per, offset, longer):
        self.route = route
        self.own = own
        self.rows = rows
        self.place = lambda j: per * j + offset
        self.hops = [route.reach - (direction != longer) for direction in range(2)]
        self.steps = 0
        self.done = 0
        self.flying = None
        self.last = [None, None]

    def terms(self, arrived, directions):
        places = []
        for direction in directions:
            left = self.hops[direction] - self.done
            at = left if direction == 0 else (self.route.count - left) % self.route.count
            places.append(self.place(at))
        return hand_on(arrived, self.own(), self.rows, places)

    def pending(self):
        return self.flying if self.done else self.terms([], range(2))

    def resume(self, arrived):
        arrived = list(arrived)
        onward = range(2)
        if self.done:
            landed = [direction for direction in range(2) if self.done <= self.hops[direction]]
            onward = [direction for direction in landed if self.done < self.hops[direction]]
            by_way = dict(zip(landed, arrived))
            for direction in landed:
                if self.done == self.hops[direction]:
                    self.last[direction] = by_way[direction]
            if onward:
                arrived = self.terms([by_way[direction] for direction in onward], onward)
        self.done += 1
        self.flying = [self.route.send(values, way) for way, values in zip(onward, arrived)]

    def total(self, part, first):
        at = self.place(0) * self.rows
        own = part[at : at + self.rows].astype(F32)
        span = slice(first, first + part.shape[1])
        return own + self.last[0][:, span].astype(F32) + self.last[1][:, span].astype(F32)


STEPS = 5


class Pace:
    def __init__(self, token):
        self.token = token

    def __call__(self, streams, *carried, busy=False, long=False):
        last = {}
        for stream in streams:
            stream.steps += 1
            last[stream] = (stream.steps * (stream.route.reach + 1)) // STEPS
        first = True
        while first or any(stream.done < last[stream] for stream in streams):
            first = False
            moving = [stream for stream in streams if stream.done < last[stream]]
            waiting = [list(stream.pending()) for stream in moving]
            flat = [values for group in waiting for values in group]
            self.token, *out = lax.optimization_barrier((self.token, *flat, *carried))
            carried = out[len(flat) :]
            at = 0
            for stream, group in zip(moving, waiting):
                stream.resume(out[at : at + len(group)])
                at += len(group)
        if not busy:
            self.token = mark(self.token, 5 * 10**10 if long else 10**9)
            self.token, *carried = lax.optimization_barrier((self.token, *carried))
        return carried[0] if len(carried) == 1 else carried


def across_core(values):
    return lax.ppermute(values, "tensor", [(i, i ^ 1) for i in range(4)])


def across_chip(values):
    return lax.ppermute(values, "tensor", [(i, i ^ 2) for i in range(4)])


def spread_over_dp(route, table):
    left = route.count
    while left > 1:
        left //= 2
        pairs = [
            (route.ring[i], route.ring[(i + left) % route.count]) for i in range(route.count)
        ]
        table = table[:left] + lax.ppermute(table[left:], "dp", pairs)
    return table[0]


def on_device(
    route,
    activations,
    cotangent,
    segments,
    norm_one_gain,
    norm_one_bias,
    w_query,
    w_key,
    w_value,
    qkv_bias,
    w_out,
    norm_two_gain,
    norm_two_bias,
    w_gate,
    w_up,
    w_down,
):
    count = route.count
    third, depth = activations.shape
    length = segments.shape[0]
    width = depth // count
    part = width // 2
    heads_wide = w_query.shape[1]
    local_heads = heads_wide // HD
    shards = length // third
    here = lax.axis_index("tensor")
    advance = Pace(jnp.zeros((8, 128), jnp.int32) + here)
    device = lax.axis_index("dp").astype(jnp.int32)
    position = jnp.where(device % 2 == 0, device // 2, count - 1 - device // 2)
    ahead = (position + jnp.arange(count, dtype=jnp.int32)) % count
    order = jnp.where(ahead < count // 2, 2 * ahead, 2 * (count - 1 - ahead) + 1)

    def gather(values):
        return lax.all_gather(values, "tensor", axis=0, tiled=True)

    def scatter(values):
        return lax.psum_scatter(values, "tensor", scatter_dimension=0, tiled=True)

    def relative(values):
        def pick(entries):
            return jnp.concatenate([values[i : i + 1] for i in entries], axis=0)

        values = jnp.where(here % 2 == 1, pick((1, 0, 3, 2)), values)
        return jnp.where(here >= 2, pick((2, 3, 0, 1)), values)

    bias_size = qkv_bias.size
    norm_part = norm_one_gain.shape[0]
    ring_qk = Gathering(route, jnp.concatenate([w_query, w_key], axis=1), 0)
    ring_vo = Gathering(route, None, 1)
    ring_gate = Gathering(route, w_gate, 0)
    ring_up = Gathering(route, w_up, 1)
    ring_down = [Gathering(route, None, 0), Gathering(route, None, 1)]

    packed = jnp.stack([norm_one_gain, norm_one_bias, norm_two_gain, norm_two_bias])
    packed_core = across_core(packed)
    own_bf16 = reorder(order, activations)
    x_all = gather(own_bf16)
    packed = jnp.concatenate([packed, packed_core], axis=0)
    packed, w_down, w_value, w_out, cotangent = advance(
        [], packed, w_down, w_value, w_out, cotangent
    )
    packed_chip = across_chip(packed)
    weight_vo = jnp.concatenate([w_value, w_out.T], axis=1)
    packed_chip, weight_vo, cotangent, w_down = advance(
        [], packed_chip, weight_vo, cotangent, w_down
    )
    packed = jnp.concatenate([packed, packed_chip], axis=0).reshape(shards, 4, norm_part)
    packed = relative(packed).transpose(1, 0, 2).reshape(4, width)
    wide = 2 * heads_wide
    packed = jnp.concatenate(
        [
            jnp.pad(packed, ((0, 0), (0, wide - width))),
            jnp.pad(qkv_bias.reshape(1, bias_size), ((0, 11), (0, wide - bias_size))),
        ],
        axis=0,
    )
    ring_vo.flying = [jnp.concatenate([weight_vo, packed], axis=0)]
    cotangent, w_down = advance([ring_qk, ring_vo], cotangent, w_down, long=True)
    own_grad = reorder(order, cotangent)
    own_grad, w_down = advance([ring_qk], own_grad, w_down)
    down_rows = w_down.T
    ring_down[0].flying = [down_rows[:part]]
    ring_down[1].flying = [down_rows[part:]]
    x_all, own_grad = advance([ring_vo], x_all, own_grad)
    grad_all = gather(own_grad)
    mean_one, inverse_one = row_stats(x_all)
    mean_one, inverse_one, segments = advance([ring_qk], mean_one, inverse_one, segments)
    segment_down, segment_across = segments[:, None], segments[None, :]
    begins = jnp.sum((segment_across < segment_down).astype(F32), axis=1, keepdims=True)
    places = jnp.arange(length, dtype=jnp.int32)[:, None].astype(F32)
    lanes = jnp.arange(PAIR, dtype=jnp.int32) % HD
    frequency = 10000.0 ** (-2.0 * (lanes % (ROT // 2)).astype(F32) / ROT)
    angles = (places - begins) * frequency[None, :]
    cos_table = jnp.where(lanes < ROT, jnp.cos(angles), 1.0)
    sin_table = jnp.where(
        lanes < ROT, jnp.where(lanes < ROT // 2, -1.0, 1.0) * jnp.sin(angles), 0.0
    )
    cos_table, sin_table, segment_down, segment_across = advance(
        [ring_vo], cos_table, sin_table, segment_down, segment_across
    )
    advance([ring_qk], long=True)
    grad_all = advance([ring_vo, ring_gate], grad_all)
    advance([ring_qk])
    advance([ring_vo, ring_up], busy=True)
    blocks_a = ring_qk.all()
    blocks_b = ring_vo.all()
    norm_rows, bias_row = decode(order, blocks_b, depth, 3 * heads_wide)
    qk, values, normed = project_qkv(
        x_all, mean_one, inverse_one, norm_rows, bias_row, cos_table, sin_table, blocks_a, blocks_b
    )
    qk, values = advance([ring_gate], qk, values, busy=True)
    mixed, lse = attend_forward(qk, values, segment_down, segment_across, shards)
    mixed, lse = advance([ring_up], mixed, lse, busy=True)
    arriving = scatter(outward([(mixed, blocks_b, heads_wide)], depth, "from_heads"))
    advance([ring_gate])
    advance([ring_up], long=True)
    arriving = advance([ring_gate], arriving)
    middle, mean_two, inverse_two, n_own = second_norm(own_bf16, arriving, norm_rows)
    normed_two = gather(n_own)
    middle = advance([ring_up, ring_down[0]], middle)
    advance([ring_gate], long=True)
    normed_two = advance([ring_up, ring_down[1]], normed_two, busy=True)
    gate_blocks = ring_gate.all()
    up_blocks = ring_up.all()
    kept = gated_forward(normed_two, gate_blocks, up_blocks, 0, None)
    kept = advance([ring_down[0]], *kept)
    kept = advance([ring_down[1]], *kept, busy=True)
    gate, up, hidden = gated_forward(normed_two, gate_blocks, up_blocks, 1, kept)
    gate, up, hidden = advance([ring_down[0]], gate, up, hidden)
    hidden = advance([ring_down[1]], hidden)
    down_sum = product(grad_all, hidden, 0, 0).astype(BF16)
    down_sum = advance([ring_down[0]], down_sum)
    sum_down = Summing(route, lambda: [down_sum], width, 1, 0, 0)
    advance([ring_down[1], sum_down])
    advance([ring_down[0]])
    advance([ring_down[1]], busy=True)
    down_blocks = [block for pair in zip(*(ring.all() for ring in ring_down)) for block in pair]

    gate_grad, up_grad = gated_backward(grad_all, gate, up, down_blocks)
    gate_grad, up_grad = advance([sum_down], gate_grad, up_grad, busy=True)
    arriving = scatter(
        outward([(gate_grad, gate_blocks, None), (up_grad, up_blocks, None)], depth, "from_gates")
    )
    gate_grad, up_grad = advance([sum_down], gate_grad, up_grad)
    gate_sum = product(normed_two, gate_grad, 0, 0).astype(BF16)
    sum_gate = Summing(route, lambda: [gate_sum], width, 1, 0, 1)
    gate_sum, up_grad = advance([sum_gate], gate_sum, up_grad, long=True)
    up_sum = product(normed_two, up_grad, 0, 0).astype(BF16)
    sum_up = Summing(route, lambda: [up_sum], width, 1, 0, 0)
    up_sum = advance([sum_down], up_sum)
    arriving = advance([sum_gate], arriving)
    middle_grad, b_own, two_sums = second_norm_back(
        arriving, middle, mean_two, inverse_two, norm_rows, own_grad
    )
    branch = gather(b_own)
    hidden = advance([sum_down], hidden, busy=True)
    result_terms = outward([(hidden, down_blocks, None)], depth, "from_hidden")
    result_terms = advance([sum_gate, sum_up], result_terms, long=True)
    branch, result_terms = advance([sum_gate], branch, result_terms, busy=True)
    arriving_result = scatter(result_terms)
    mixed_grad = through_out(branch, blocks_b)
    mixed_grad, branch = advance([sum_up], mixed_grad, branch, busy=True)
    q_grad, k_grad, v_grad, bias_sums = attend_backward(
        qk,
        values,
        mixed,
        mixed_grad,
        lse,
        segment_down,
        segment_across,
        cos_table,
        sin_table,
        shards,
    )
    q_grad, k_grad, v_grad, bias_sums = advance([sum_gate], q_grad, k_grad, v_grad, bias_sums)
    q_sum = product(normed, q_grad, 0, 0).astype(BF16)
    k_sum = product(normed, k_grad, 0, 0).astype(BF16)
    sum_qk = Summing(route, lambda: [q_sum, k_sum], width, 1, 0, 1)
    q_sum, k_sum, v_grad, branch, arriving_result = advance(
        [sum_up, sum_qk], q_sum, k_sum, v_grad, branch, arriving_result
    )
    out_sum = product(branch, mixed, 0, 0).astype(BF16)
    v_sum = product(normed, v_grad, 0, 0).astype(BF16)
    sum_vo = Summing(route, lambda: [v_sum, out_sum], width, 1, 0, 0)
    out_sum, v_sum, q_grad = advance([sum_up], out_sum, v_sum, q_grad)
    q_grad = advance([sum_vo, sum_qk], q_grad, busy=True)
    heads_terms, one_sums = through_heads(
        [q_grad, k_grad, v_grad], x_all, mean_one, inverse_one, blocks_a, blocks_b
    )
    arriving = scatter(heads_terms)
    one_sums, middle, arriving_result = advance([sum_up], one_sums, middle, arriving_result, long=True)
    norm_grads = jnp.concatenate([one_sums, two_sums], axis=0)
    bias_sums = bias_sums.transpose(1, 0, 2).reshape(3, local_heads, count, HD // count)
    bias_sums = bias_sums.transpose(2, 0, 1, 3).reshape(count, bias_size)[order]
    extras = jnp.concatenate(
        [norm_grads.reshape(4, count, width).transpose(1, 0, 2).reshape(count, 4 * width), bias_sums],
        axis=1,
    )
    extras = jnp.pad(extras, ((0, 0), (0, -extras.shape[1] % 128)))
    result = finish_result(order, middle, arriving_result)
    grad_down = sum_down.total(down_sum, 0).T
    grad_gate = sum_gate.total(gate_sum, 0)
    extras, result, grad_down, grad_gate = advance(
        [sum_vo, sum_qk], extras, result, grad_down, grad_gate
    )
    extras = spread_over_dp(route, extras)
    grad_up = sum_up.total(up_sum, 0)
    grad_up = advance([sum_vo, sum_qk], grad_up)
    arriving, extras = advance([sum_vo, sum_qk], arriving, extras)
    input_grad = input_back(order, arriving, own_bf16, norm_rows, middle_grad)
    norm_sums = extras[: 4 * width].reshape(4, width)
    norm_sums = norm_sums + across_core(norm_sums)
    norm_sums = norm_sums + across_chip(norm_sums)
    norm_sums = lax.dynamic_slice_in_dim(norm_sums, here * norm_part, norm_part, axis=1)
    bias_grad = extras[4 * width : 4 * width + bias_size].reshape(qkv_bias.shape)
    input_grad, norm_sums = advance([sum_vo], input_grad, norm_sums)

    return (
        result,
        input_grad,
        norm_sums[0],
        norm_sums[1],
        sum_qk.total(q_sum, 0),
        sum_qk.total(k_sum, heads_wide),
        sum_vo.total(v_sum, 0),
        bias_grad,
        sum_vo.total(out_sum, heads_wide).T,
        norm_sums[2],
        norm_sums[3],
        grad_gate,
        grad_up,
        grad_down,
    )


def solution(mesh):
    both = P(("dp", "tensor"))
    tokens = P(("dp", "tensor"), None)
    rows = P("dp", "tensor")
    columns = P("tensor", "dp")
    biases = P(None, "tensor", "dp")
    return jax.shard_map(
        functools.partial(on_device, Route(mesh.shape["dp"])),
        mesh=mesh,
        in_specs=(
            tokens,
            tokens,
            P("dp"),
            both,
            both,
            rows,
            rows,
            rows,
            biases,
            columns,
            both,
            both,
            rows,
            rows,
            columns,
        ),
        out_specs=(
            tokens,
            tokens,
            both,
            both,
            rows,
            rows,
            rows,
            biases,
            columns,
            both,
            both,
            rows,
            rows,
            columns,
        ),
        check_vma=False,
    )
```

```python
import functools

import jax
import jax.experimental.pallas as pl
import jax.experimental.pallas.tpu as pltpu
import jax.numpy as jnp
from jax import lax
from jax.sharding import PartitionSpec as P

HD = 64
ROT = 16
PAIR = 2 * HD
EPSILON = 1e-05
NEGATIVE = -1e30
F32 = jnp.float32
BF16 = jnp.bfloat16
MIB = 2**20
LIGHT = pl.CostEstimate(flops=10**9, bytes_accessed=1, transcendentals=1)
LONG = pl.CostEstimate(flops=10**12, bytes_accessed=1, transcendentals=1)


def product(left, right, left_dim, right_dim):
    return lax.dot_general(
        left, right, (((left_dim,), (right_dim,)), ((), ())), preferred_element_type=F32
    )


def turn(columns, cos_values, sin_values, opening):
    partner = jnp.where(opening, pltpu.roll(columns, PAIR - 8, 1), pltpu.roll(columns, 8, 1))
    return columns * cos_values + partner * sin_values


def opening_lanes(rows):
    return lax.broadcasted_iota(jnp.int32, (rows, PAIR), 1) % HD < 8


def forward_body(block, count, q_ref, k_ref, v_ref, down_ref, across_ref, mixed_ref, lse_ref):
    lane = lax.broadcasted_iota(jnp.int32, (block, PAIR), 1)
    earlier = lax.broadcasted_iota(jnp.int32, (block, block), 0) <= lax.broadcasted_iota(
        jnp.int32, (block, block), 1
    )
    spans = [pl.ds(i * block, block) for i in range(count)]
    for i in range(count):
        queries = q_ref[spans[i], :] * jnp.asarray(HD**-0.5, BF16)
        segment = across_ref[:, spans[i]]
        kept = [down_ref[spans[j], :] == segment for j in range(i + 1)]
        kept[i] = kept[i] & earlier
        sums = []
        for half in range(2):
            mine = lane < HD if half == 0 else lane >= HD
            chosen = jnp.where(mine, queries, jnp.zeros_like(queries))
            scores = [
                jnp.where(kept[j], product(k_ref[spans[j], :], chosen, 1, 1), NEGATIVE)
                for j in range(i + 1)
            ]
            top = scores[0].max(0, keepdims=True)
            for part in scores[1:]:
                top = jnp.maximum(top, part.max(0, keepdims=True))
            raised = [jnp.exp(part - top) for part in scores]
            total = raised[0].sum(0, keepdims=True)
            for part in raised[1:]:
                total = total + part.sum(0, keepdims=True)
            inverse = 1.0 / total
            out = None
            for j in range(i + 1):
                term = product((raised[j] * inverse).astype(BF16), v_ref[spans[j], :], 0, 0)
                out = term if out is None else out + term
            sums.append(out)
            lse_ref[0, half : half + 1, spans[i]] = top + jnp.log(total)
        mixed_ref[spans[i], :] = jnp.where(lane < HD, sums[0], sums[1]).astype(BF16)


def attend_forward(qk, values, segment_down, segment_across, count):
    length, width = values.shape
    pairs = width // PAIR
    columns = lambda first: pl.BlockSpec((length, PAIR), lambda h: (0, h + first))
    whole = lambda shape: pl.BlockSpec(shape, lambda h: (0, 0))
    return pl.pallas_call(
        functools.partial(forward_body, length // count, count),
        grid_spec=pltpu.PrefetchScalarGridSpec(
            num_scalar_prefetch=0,
            grid=(pairs,),
            in_specs=[columns(0), columns(pairs), columns(0), whole((length, 1)), whole((1, length))],
            out_specs=[columns(0), pl.BlockSpec((1, 2, length), lambda h: (h, 0, 0))],
        ),
        out_shape=[
            jax.ShapeDtypeStruct((length, width), BF16),
            jax.ShapeDtypeStruct((pairs, 2, length), F32),
        ],
        compiler_params=pltpu.CompilerParams(vmem_limit_bytes=60 * MIB),
        cost_estimate=LIGHT,
        name="attend_forward",
    )(qk, qk, values, segment_down, segment_across)


def backward_body(
    block,
    count,
    kept,
    q_ref,
    k_ref,
    v_ref,
    mixed_ref,
    grad_ref,
    lse_ref,
    down_ref,
    across_ref,
    cos_ref,
    sin_ref,
    *refs,
):
    q_grad_ref, k_grad_ref, v_grad_ref, bias_ref, q_total, k_total, v_total = refs[kept:]
    lane = lax.broadcasted_iota(jnp.int32, (block, PAIR), 1)
    earlier = lax.broadcasted_iota(jnp.int32, (block, block), 0) <= lax.broadcasted_iota(
        jnp.int32, (block, block), 1
    )
    spans = [pl.ds(i * block, block) for i in range(count)]
    for i in range(count):
        queries = q_ref[spans[i], :] * jnp.asarray(HD**-0.5, BF16)
        upstream = grad_ref[spans[i], :]
        centres = (upstream.astype(F32) * mixed_ref[spans[i], :].astype(F32)).T
        segment = across_ref[:, spans[i]]
        allowed = [down_ref[spans[j], :] == segment for j in range(i + 1)]
        allowed[i] = allowed[i] & earlier
        sums = []
        for half in range(2):
            mine = lane < HD if half == 0 else lane >= HD
            nothing = jnp.zeros_like(queries)
            chosen = jnp.where(mine, queries, nothing)
            chosen_grad = jnp.where(mine, upstream, nothing)
            log_total = lse_ref[0, half : half + 1, spans[i]]
            centre = centres[half * HD : (half + 1) * HD, :].sum(0, keepdims=True)
            q_sum = None
            for j in range(i + 1):
                keys = k_ref[spans[j], :]
                scores = jnp.where(allowed[j], product(keys, chosen, 1, 1), NEGATIVE)
                weights = jnp.exp(scores - log_total)
                weight_grad = product(v_ref[spans[j], :], chosen_grad, 1, 1)
                score_grad = (weights * (weight_grad - centre)).astype(BF16)
                v_term = product(weights.astype(BF16), chosen_grad, 1, 0)
                k_term = product(score_grad, chosen, 1, 0)
                term = product(score_grad, keys, 0, 0)
                q_sum = term if q_sum is None else q_sum + term
                if i == j and half == 0:
                    v_total[spans[j], :] = v_term
                    k_total[spans[j], :] = k_term
                else:
                    v_total[spans[j], :] += v_term
                    k_total[spans[j], :] += k_term
            sums.append(q_sum)
        q_total[spans[i], :] = jnp.where(lane < HD, sums[0], sums[1])
    opening = opening_lanes(block * count)
    cos_values = cos_ref[...]
    sin_values = -sin_ref[...]
    q_grad = turn(q_total[...] * (HD**-0.5), cos_values, sin_values, opening).astype(BF16)
    k_grad = turn(k_total[...], cos_values, sin_values, opening).astype(BF16)
    v_grad = v_total[...].astype(BF16)
    for at, (ref, grad) in enumerate(
        ((q_grad_ref, q_grad), (k_grad_ref, k_grad), (v_grad_ref, v_grad))
    ):
        ref[...] = grad
        bias_ref[0, at : at + 1, :] = grad.astype(F32).sum(0, keepdims=True)


def attend_backward(
    qk, values, mixed, mixed_grad, lse, segment_down, segment_across, cos_table, sin_table, count, half, kept
):
    length, width = values.shape
    pairs = width // PAIR
    kept = list(kept or [])
    some = pairs // 2
    start = half * some
    columns = lambda first: pl.BlockSpec((length, PAIR), lambda h: (0, h + first + start))
    whole = lambda shape: pl.BlockSpec(shape, lambda h: (0, 0))
    return pl.pallas_call(
        functools.partial(backward_body, length // count, count, len(kept)),
        grid_spec=pltpu.PrefetchScalarGridSpec(
            num_scalar_prefetch=0,
            grid=(some,),
            in_specs=[
                columns(0),
                columns(pairs),
                columns(0),
                columns(0),
                columns(0),
                pl.BlockSpec((1, 2, length), lambda h: (h + start, 0, 0)),
                whole((length, 1)),
                whole((1, length)),
                whole((length, PAIR)),
                whole((length, PAIR)),
            ]
            + [pl.BlockSpec(memory_space=pl.ANY)] * len(kept),
            out_specs=[
                columns(0),
                columns(0),
                columns(0),
                pl.BlockSpec((1, 3, PAIR), lambda h: (h + start, 0, 0)),
            ],
            scratch_shapes=[pltpu.VMEM((length, PAIR), F32)] * 3,
        ),
        out_shape=[jax.ShapeDtypeStruct((length, width), BF16)] * 3
        + [jax.ShapeDtypeStruct((pairs, 3, PAIR), F32)],
        input_output_aliases={10 + i: i for i in range(len(kept))},
        compiler_params=pltpu.CompilerParams(vmem_limit_bytes=60 * MIB),
        cost_estimate=LONG,
        name="attend_backward",
    )(
        qk, qk, values, mixed, mixed_grad, lse, segment_down, segment_across, cos_table, sin_table, *kept
    )


HBM = pl.BlockSpec(memory_space=pl.ANY)


def whole(shape):
    return pl.BlockSpec(shape, lambda *_: (0,) * len(shape), pipeline_mode=pl.Buffered(1))


def shaped(shape, dtype=BF16):
    return jax.ShapeDtypeStruct(shape, dtype)


def kernel_call(body, name, operands, in_specs, out_specs, out_shape, grid=(), scratch=(), scalars=(), aliases=None, vmem=40, flops=1, kept=False):
    return pl.pallas_call(
        body,
        grid_spec=pltpu.PrefetchScalarGridSpec(
            num_scalar_prefetch=len(scalars),
            grid=grid,
            in_specs=in_specs,
            out_specs=out_specs,
            scratch_shapes=list(scratch),
        ),
        out_shape=out_shape,
        input_output_aliases=aliases or {},
        compiler_params=pltpu.CompilerParams(vmem_limit_bytes=vmem * MIB, has_side_effects=kept),
        cost_estimate=pl.CostEstimate(flops=flops, bytes_accessed=1, transcendentals=1),
        name=name,
    )(*scalars, *operands)


def copies_into(blocks, target, semaphores, first, columns=None, rows=None):
    copies, at = [], 0
    for i, block in enumerate(blocks):
        deep = rows or block.shape[0]
        source = block if columns is None else block.at[pl.ds(0, deep), columns]
        copies.append(
            pltpu.make_async_copy(source, target.at[pl.ds(at, deep), :], semaphores.at[first + i])
        )
        at += deep
    return copies


def start_all(step, copies):
    @pl.when(step == 0)
    def _():
        for copy in copies:
            copy.start()


def wait_at(step, when, copies):
    @pl.when(step == when)
    def _():
        for copy in copies:
            copy.wait()


def halves(copies):
    return copies[: len(copies) // 2], copies[len(copies) // 2 :]


def mark_body(in_ref, out_ref):
    out_ref[...] = in_ref[...]


def mark(token, flops):
    return kernel_call(
        mark_body,
        "mark",
        [token],
        [whole(token.shape)],
        whole(token.shape),
        shaped(token.shape, token.dtype),
        grid=(1,),
        flops=flops,
        kept=True,
    )


def pick_columns(order, values):
    count = order.shape[0]
    width = values.shape[1] // count
    parts = [lax.dynamic_slice_in_dim(values, order[j] * width, width, 1) for j in range(count)]
    return jnp.concatenate(parts, axis=1)


def back_in_place(order, values):
    count = order.shape[0]
    if values.shape[1] // count % 128 == 0:
        return values
    places = jnp.arange(count, dtype=jnp.int32)
    back = jnp.sum(jnp.where(order[:, None] == places[None, :], places[:, None], 0), axis=0)
    return pick_columns(back, values)


def reorder_body(count, width, order_ref, in_ref, out_ref):
    for j in range(count):
        source = pl.ds(pl.multiple_of(order_ref[j] * width, width), width)
        out_ref[:, j * width : (j + 1) * width] = in_ref[:, source]


def reorder(order, values):
    count = order.shape[0]
    if values.shape[1] // count % 128:
        return pick_columns(order, values)
    return kernel_call(
        functools.partial(reorder_body, count, values.shape[1] // count),
        "reorder",
        [values],
        [whole(values.shape)],
        whole(values.shape),
        shaped(values.shape),
        grid=(1,),
        scalars=[order],
    )


def put_back(order_ref, out_ref, values):
    count = order_ref.shape[0]
    width = values.shape[1] // count
    if width % 128:
        out_ref[...] = values.astype(out_ref.dtype)
        return
    for j in range(count):
        target = pl.ds(pl.multiple_of(order_ref[j] * width, width), width)
        out_ref[:, target] = values[:, j * width : (j + 1) * width].astype(out_ref.dtype)


def stats_body(x_ref, mean_ref, inverse_ref):
    values = x_ref[...].astype(F32)
    mean = jnp.mean(values, axis=-1, keepdims=True)
    centred = values - mean
    mean_ref[...] = mean
    inverse_ref[...] = lax.rsqrt(jnp.mean(centred * centred, axis=-1, keepdims=True) + EPSILON)


def row_stats(inputs):
    length, depth = inputs.shape
    by_rows = lambda columns: pl.BlockSpec((length // 4, columns), lambda i: (i, 0))
    return kernel_call(
        stats_body,
        "row_stats",
        [inputs],
        [by_rows(depth)],
        [by_rows(1)] * 2,
        [shaped((length, 1), F32)] * 2,
        grid=(4,),
    )


def decode_body(count, chunk, order_ref, *refs):
    blocks, norm_ref, bias_ref = refs[:count], refs[-2], refs[-1]
    width = norm_ref.shape[1] // count
    wide = bias_ref.shape[1]
    small = wide // count
    rows = []
    for j, block in enumerate(blocks):
        norm_ref[:, j * width : (j + 1) * width] = block[0:4, :width].astype(F32)
        rows.append(block[4:5, :small].astype(F32))
    lane = lax.broadcasted_iota(jnp.int32, (small, wide), 1)
    source = lax.broadcasted_iota(jnp.int32, (small, wide), 0)
    spread = (lane // HD * chunk + lane % chunk == source).astype(BF16)
    spread = product(jnp.concatenate(rows, axis=0).astype(BF16), spread, 1, 0)
    lane = lax.broadcasted_iota(jnp.int32, (1, wide), 1)
    total = jnp.zeros((1, wide), F32)
    for j in range(count):
        total = jnp.where(lane % HD // chunk == order_ref[j], spread[j : j + 1, :], total)
    bias_ref[...] = total


def decode(order, blocks, depth, bias_wide):
    count = len(blocks)
    rows, wide = blocks[0].shape
    return kernel_call(
        functools.partial(decode_body, count, HD // count),
        "decode",
        blocks,
        [pl.BlockSpec((16, wide), lambda i, order: (rows // 16 - 1, 0))] * count,
        [whole((4, depth)), whole((1, bias_wide))],
        [shaped((4, depth), F32), shaped((1, bias_wide), F32)],
        grid=(1,),
        scalars=[order],
    )


def qkv_body(count, x_ref, norm_ref, bias_ref, mean_ref, inverse_ref, cos_ref, sin_ref, *refs):
    blocks_a, blocks_b, refs = refs[:count], refs[count : 2 * count], refs[2 * count :]
    qk_ref, v_ref, normed_ref, weight_a, weight_v, semaphores = refs
    step = pl.program_id(0)
    width = qk_ref.shape[1]
    deep = weight_a.shape[0] // count
    copies_a = copies_into(blocks_a, weight_a, semaphores, 0, rows=deep)
    copies_v = copies_into(blocks_b, weight_v, semaphores, count, pl.ds(0, width // 2), deep)
    start_all(step, copies_a + copies_v)
    values = (x_ref[...].astype(F32) - mean_ref[...]) * inverse_ref[...]
    normed = (values * norm_ref[0:1, :] + norm_ref[1:2, :]).astype(BF16)
    normed_ref[...] = normed
    wait_at(step, 0, copies_a)
    both = product(normed, weight_a[...], 1, 0) + bias_ref[:, :width]
    opening = opening_lanes(normed.shape[0])
    cos_values = cos_ref[...]
    sin_values = sin_ref[...]
    for at in range(0, width, PAIR):
        part = turn(both[:, at : at + PAIR], cos_values, sin_values, opening)
        qk_ref[:, at : at + PAIR] = part.astype(BF16)
    wait_at(step, 0, copies_v)
    v_ref[...] = (product(normed, weight_v[...], 1, 0) + bias_ref[:, width:]).astype(BF16)


def project_qkv(inputs, mean, inverse, norm_rows, bias_row, cos_table, sin_table, blocks_a, blocks_b):
    length, depth = inputs.shape
    rows = length // 4
    wide = blocks_a[0].shape[1]
    count = len(blocks_a)
    by_rows = lambda columns: pl.BlockSpec((rows, columns), lambda i: (i, 0))
    return kernel_call(
        functools.partial(qkv_body, count),
        "project_qkv",
        [inputs, norm_rows, bias_row, mean, inverse, cos_table, sin_table, *blocks_a, *blocks_b],
        [
            by_rows(depth),
            whole(norm_rows.shape),
            whole(bias_row.shape),
            by_rows(1),
            by_rows(1),
            by_rows(PAIR),
            by_rows(PAIR),
        ]
        + [HBM] * (2 * count),
        [by_rows(wide), by_rows(wide // 2), by_rows(depth)],
        [shaped((length, wide)), shaped((length, wide // 2)), shaped((length, depth))],
        grid=(4,),
        flops=10**9,
        scratch=[
            pltpu.VMEM((depth, wide), BF16),
            pltpu.VMEM((depth, wide // 2), BF16),
            pltpu.SemaphoreType.DMA((2 * count,)),
        ],
        vmem=60,
    )


def gated_body(count, x_ref, *refs):
    gate_blocks, up_blocks, refs = refs[:count], refs[count : 2 * count], refs[2 * count :]
    gate_ref, up_ref, hidden_ref, gate_weight, up_weight, semaphores = refs[-6:]
    step = pl.program_id(0)
    early, late = halves(copies_into(gate_blocks, gate_weight, semaphores, 0))
    early_up, late_up = halves(copies_into(up_blocks, up_weight, semaphores, count))
    start_all(step, early + late + early_up + late_up)
    half = gate_weight.shape[0] // 2
    wait_at(step, 0, early)
    gate = product(x_ref[:, :half], gate_weight[:half, :], 1, 0)
    wait_at(step, 0, late)
    gate = gate + product(x_ref[:, half:], gate_weight[half:, :], 1, 0)
    gate_ref[...] = gate.astype(BF16)
    wait_at(step, 0, early_up + late_up)
    up = product(x_ref[...], up_weight[...], 1, 0)
    up_ref[...] = up.astype(BF16)
    hidden_ref[...] = (gate * jax.nn.sigmoid(gate) * up).astype(BF16)


def gated_forward(inputs, gate_blocks, up_blocks, half, kept):
    length, depth = inputs.shape
    rows = length // 4
    wide = gate_blocks[0].shape[1]
    count = len(gate_blocks)
    kept = list(kept or [])
    place = lambda columns: pl.BlockSpec((rows, columns), lambda i: (2 * half + i, 0))
    first = 1 + 2 * count
    return kernel_call(
        functools.partial(gated_body, count),
        "gated_forward",
        [inputs, *gate_blocks, *up_blocks, *kept],
        [place(depth)] + [HBM] * (2 * count + len(kept)),
        [place(wide)] * 3,
        [shaped((length, wide))] * 3,
        grid=(2,),
        flops=10**9,
        scratch=[
            pltpu.VMEM((depth, wide), BF16),
            pltpu.VMEM((depth, wide), BF16),
            pltpu.SemaphoreType.DMA((2 * count,)),
        ],
        aliases={first + i: i for i in range(len(kept))},
        vmem=60,
    )


def gated_back_body(count, *refs):
    grad_ref, gate_ref, up_ref, refs = refs[0], refs[1], refs[2], refs[3:]
    blocks = refs[:count]
    gate_grad_ref, up_grad_ref, weight, semaphores = refs[-4:]
    step = pl.program_id(0)
    early, late = halves(copies_into(blocks, weight, semaphores, 0))
    start_all(step, early + late)
    gate = gate_ref[...].astype(F32)
    sigmoid = jax.nn.sigmoid(gate)
    silu = gate * sigmoid
    slope = sigmoid + silu * (1.0 - sigmoid)
    half = weight.shape[0] // 2
    wait_at(step, 0, early)
    hidden_grad = product(grad_ref[:, :half], weight[:half, :], 1, 0)
    wait_at(step, 0, late)
    hidden_grad = hidden_grad + product(grad_ref[:, half:], weight[half:, :], 1, 0)
    up_grad_ref[...] = (hidden_grad * silu).astype(BF16)
    gate_grad_ref[...] = (hidden_grad * up_ref[...].astype(F32) * slope).astype(BF16)


def gated_backward(grads, gate, up, blocks):
    length, wide = gate.shape
    rows = length // 4
    depth = grads.shape[1]
    count = len(blocks)
    by_rows = lambda columns: pl.BlockSpec((rows, columns), lambda i: (i, 0))
    return kernel_call(
        functools.partial(gated_back_body, count),
        "gated_backward",
        [grads, gate, up, *blocks],
        [by_rows(depth), by_rows(wide), by_rows(wide)] + [HBM] * count,
        [by_rows(wide)] * 2,
        [shaped((length, wide))] * 2,
        grid=(4,),
        flops=10**9,
        scratch=[pltpu.VMEM((depth, wide), BF16), pltpu.SemaphoreType.DMA((count,))],
        vmem=60,
    )


STRIPES = 4


def outward_body(shape, columns, deep, apart, *refs):
    if apart:
        here, refs = refs[0][0], refs[1:]
    lefts, refs = refs[: len(shape)], refs[len(shape) :]
    outs = refs[sum(shape) : sum(shape) + 1 + apart]
    weights, semaphores = refs[sum(shape) + 1 + apart : -1], refs[-1]
    step = pl.program_id(0)
    at, groups = 0, []
    for count, weight, column in zip(shape, weights, columns):
        groups.append(
            copies_into(refs[at : at + count], weight, semaphores, at, column, deep)
        )
        at += count
    for stripe in range(STRIPES):
        start_all(
            step,
            [
                copy
                for group in groups
                for copy in group[stripe * len(group) // STRIPES : (stripe + 1) * len(group) // STRIPES]
            ],
        )
    for stripe in range(STRIPES):
        for group in groups:
            wait_at(
                step,
                stripe,
                group[stripe * len(group) // STRIPES : (stripe + 1) * len(group) // STRIPES],
            )
    tall = weights[0].shape[0] // STRIPES
    span = pl.ds(pl.multiple_of(step * tall, tall), tall)
    total = None
    for left, weight in zip(lefts, weights):
        term = product(left[...], weight[span, :], 1, 1)
        total = term if total is None else total + term
    if not apart:
        outs[0][...] = total.astype(BF16)
        return
    rows = total.shape[0] // 4
    for i in range(4):
        away = jnp.bitwise_xor(here, i)
        span = pl.ds(pl.multiple_of((1 - away // 2) * rows, rows), rows)
        values = total[i * rows : (i + 1) * rows].astype(BF16)
        for other, out_ref in enumerate(outs):

            @pl.when(away % 2 == other)
            def _():
                out_ref[span, :] = values


def outward(parts, depth, name, place=None):
    lefts = [left for left, _, _ in parts]
    length = lefts[0].shape[0]
    shape = [len(blocks) for _, blocks, _ in parts]
    tall = (0,) if place is None else (0, 1)
    deep = None
    columns = []
    for left, blocks, column in parts:
        if column is None:
            columns.append(None)
        else:
            columns.append(pl.ds(column, left.shape[1]))
            deep = depth // len(blocks)
    return kernel_call(
        functools.partial(outward_body, shape, columns, deep, place is not None),
        name,
        [*lefts, *(block for _, blocks, _ in parts for block in blocks)],
        [whole(left.shape) for left in lefts] + [HBM] * sum(shape),
        [pl.BlockSpec((length // len(tall), depth // STRIPES), lambda i, *_: (0, i)) for _ in tall],
        [shaped((length // len(tall), depth)) for _ in tall],
        scalars=() if place is None else (place,),
        grid=(STRIPES,),
        flops=10**9,
        scratch=[pltpu.VMEM((depth, left.shape[1]), BF16) for left in lefts]
        + [pltpu.SemaphoreType.DMA((sum(shape),))],
        vmem=60,
    )


def mixed_grad_body(count, rows_ref, *refs):
    blocks = refs[:count]
    out_ref, weight, semaphores = refs[count:]
    step = pl.program_id(0)
    wide = weight.shape[1]
    copies = copies_into(blocks, weight, semaphores, 0, pl.ds(wide, wide), weight.shape[0] // count)
    start_all(step, copies)
    wait_at(step, 0, copies)
    out_ref[...] = product(rows_ref[...], weight[...], 1, 0).astype(BF16)


def through_out(branch, blocks):
    length, depth = branch.shape
    rows = length // 4
    wide = blocks[0].shape[1] // 2
    count = len(blocks)
    return kernel_call(
        functools.partial(mixed_grad_body, count),
        "through_out",
        [branch, *blocks],
        [pl.BlockSpec((rows, depth), lambda i: (i, 0))] + [HBM] * count,
        pl.BlockSpec((rows, wide), lambda i: (i, 0)),
        shaped((length, wide)),
        grid=(4,),
        flops=10**9,
        scratch=[pltpu.VMEM((depth, wide), BF16), pltpu.SemaphoreType.DMA((count,))],
        vmem=60,
    )


def heads_body(count, q_ref, k_ref, v_ref, x_ref, mean_ref, inverse_ref, *refs):
    blocks_a, blocks_b = refs[:count], refs[count : 2 * count]
    out_ref, sums_ref, weight_a, weight_v, semaphores = refs[2 * count :]
    step = pl.program_id(0)
    wide = q_ref.shape[1]
    deep = weight_a.shape[0] // count
    copies_a = copies_into(blocks_a, weight_a, semaphores, 0, rows=deep)
    copies_v = copies_into(blocks_b, weight_v, semaphores, count, pl.ds(0, wide), deep)
    start_all(step, [copy for pair in zip(copies_a, copies_v) for copy in pair])
    for stripe in range(STRIPES):
        span = slice(stripe * count // STRIPES, (stripe + 1) * count // STRIPES)
        wait_at(step, stripe, copies_a[span] + copies_v[span])
    tall = weight_a.shape[0] // STRIPES
    span = pl.ds(pl.multiple_of(step * tall, tall), tall)
    total = product(q_ref[...], weight_a[span, :wide], 1, 1)
    total = total + product(k_ref[...], weight_a[span, wide:], 1, 1)
    total = total + product(v_ref[...], weight_v[span, :], 1, 1)
    out_ref[...] = total.astype(BF16)
    standard = (x_ref[...].astype(F32) - mean_ref[...]) * inverse_ref[...]
    sums_ref[0:1, :] = (total * standard).sum(0, keepdims=True)
    sums_ref[1:2, :] = total.sum(0, keepdims=True)


def through_heads(grads, inputs, mean, inverse, blocks_a, blocks_b):
    length, wide = grads[0].shape
    depth = inputs.shape[1]
    count = len(blocks_a)
    striped = lambda tall: pl.BlockSpec((tall, depth // STRIPES), lambda i: (0, i))
    return kernel_call(
        functools.partial(heads_body, count),
        "through_heads",
        [*grads, inputs, mean, inverse, *blocks_a, *blocks_b],
        [whole((length, wide))] * 3
        + [striped(length), whole((length, 1)), whole((length, 1))]
        + [HBM] * (2 * count),
        [striped(length), striped(2)],
        [shaped((length, depth)), shaped((2, depth), F32)],
        grid=(STRIPES,),
        flops=10**9,
        scratch=[
            pltpu.VMEM((depth, 2 * wide), BF16),
            pltpu.VMEM((depth, wide), BF16),
            pltpu.SemaphoreType.DMA((2 * count,)),
        ],
        vmem=60,
    )


def added(refs):
    total = refs[0][...].astype(F32)
    for ref in refs[1:]:
        total = total + ref[...].astype(F32)
    return total


def meet_body(own_ref, arrived_ref, far_ref, near_ref):
    rows = far_ref.shape[0]
    total = own_ref[...].astype(F32) + arrived_ref[...].astype(F32)
    far_ref[...] = total[:rows].astype(BF16)
    near_ref[...] = total[rows:]


def meet(own, arrived):
    length, depth = own.shape
    half = (length // 2, depth)
    return kernel_call(
        meet_body,
        "meet",
        [own, arrived],
        [whole(own.shape)] * 2,
        [whole(half)] * 2,
        [shaped(half), shaped(half, F32)],
        grid=(1,),
    )


def second_norm_body(x_ref, term_ref, norm_ref, middle_ref, mean_ref, inverse_ref, out_ref):
    middle = added([x_ref, term_ref])
    middle_ref[...] = middle
    mean = jnp.mean(middle, axis=-1, keepdims=True)
    centred = middle - mean
    inverse = lax.rsqrt(jnp.mean(centred * centred, axis=-1, keepdims=True) + EPSILON)
    mean_ref[...] = mean
    inverse_ref[...] = inverse
    out_ref[...] = (centred * inverse * norm_ref[2:3, :] + norm_ref[3:4, :]).astype(BF16)


def second_norm(inputs, terms, norm_rows):
    shape = inputs.shape
    column = (shape[0], 1)
    return kernel_call(
        second_norm_body,
        "second_norm",
        [inputs, *terms, norm_rows],
        [whole(shape)] * 2 + [whole(norm_rows.shape)],
        [whole(shape), whole(column), whole(column), whole(shape)],
        [shaped(shape, F32), shaped(column, F32), shaped(column, F32), shaped(shape)],
        grid=(1,),
    )


def norm_gradient(upstream, standard, inverse, gain):
    scaled = upstream * gain
    inner = (
        scaled
        - jnp.mean(scaled, axis=-1, keepdims=True)
        - standard * jnp.mean(scaled * standard, axis=-1, keepdims=True)
    )
    return inverse * inner


def second_back_body(near_ref, far_ref, middle_ref, mean_ref, inverse_ref, norm_ref, grad_ref, full_ref, branch_ref, sums_ref):
    upstream = added([near_ref, far_ref])
    inverse = inverse_ref[...]
    standard = (middle_ref[...] - mean_ref[...]) * inverse
    sums_ref[0:1, :] = (upstream * standard).sum(0, keepdims=True)
    sums_ref[1:2, :] = upstream.sum(0, keepdims=True)
    grad = grad_ref[...].astype(F32) + norm_gradient(upstream, standard, inverse, norm_ref[2:3, :])
    full_ref[...] = grad
    branch_ref[...] = grad.astype(BF16)


def second_norm_back(terms, middle, mean, inverse, norm_rows, grads):
    shape = middle.shape
    column = (shape[0], 1)
    return kernel_call(
        second_back_body,
        "second_norm_back",
        [*terms, middle, mean, inverse, norm_rows, grads],
        [whole(shape)] * 3 + [whole(column)] * 2 + [whole(norm_rows.shape), whole(shape)],
        [whole(shape), whole(shape), whole((2, shape[1]))],
        [shaped(shape, F32), shaped(shape), shaped((2, shape[1]), F32)],
        grid=(1,),
    )


def input_back_body(order_ref, upstream_ref, x_ref, norm_ref, grad_ref, out_ref):
    values = x_ref[...].astype(F32)
    centred = values - jnp.mean(values, axis=-1, keepdims=True)
    inverse = lax.rsqrt(jnp.mean(centred * centred, axis=-1, keepdims=True) + EPSILON)
    upstream = upstream_ref[...].astype(F32)
    grad = grad_ref[...] + norm_gradient(upstream, centred * inverse, inverse, norm_ref[0:1, :])
    put_back(order_ref, out_ref, grad)


def input_back(order, upstream, inputs, norm_rows, grads):
    shape = inputs.shape
    out = kernel_call(
        input_back_body,
        "input_back",
        [upstream, inputs, norm_rows, grads],
        [whole(shape)] * 2 + [whole(norm_rows.shape), whole(shape)],
        whole(shape),
        shaped(shape),
        grid=(1,),
        scalars=[order],
    )
    return back_in_place(order, out)


def result_body(order_ref, middle_ref, term_ref, out_ref):
    put_back(order_ref, out_ref, added([middle_ref, term_ref]))


def finish_result(order, middle, term):
    shape = middle.shape
    out = kernel_call(
        result_body,
        "finish_result",
        [middle, term],
        [whole(shape)] * 2,
        whole(shape),
        shaped(shape),
        grid=(1,),
        scalars=[order],
    )
    return back_in_place(order, out)


def hand_on_body(arrivals, sides, *refs):
    arrived, own, outs = refs[:arrivals], refs[arrivals : -sides], refs[-sides:]
    parts = len(own) // sides
    for side in range(sides):
        first = 0
        for part in own[side * parts : (side + 1) * parts]:
            span = slice(first, first + part.shape[1])
            values = part[...]
            if arrivals:
                values = (values.astype(F32) + arrived[side][:, span].astype(F32)).astype(BF16)
            outs[side][:, span] = values
            first += part.shape[1]


def hand_on(arrived, own, rows, places):
    shape = (rows, sum(part.shape[1] for part in own))
    sides = len(places)
    half = (rows // 2, shape[1])
    by_halves = pl.BlockSpec(half, lambda i: (i, 0))
    return kernel_call(
        functools.partial(hand_on_body, len(arrived), sides),
        "hand_on",
        [*arrived, *(part for _ in places for part in own)],
        [by_halves] * len(arrived)
        + [
            pl.BlockSpec((rows // 2, part.shape[1]), lambda i, at=at: (2 * at + i, 0))
            for at in places
            for part in own
        ],
        [by_halves] * sides,
        [shaped(shape)] * sides,
        grid=(2,),
        vmem=60,
    )


class Route:
    def __init__(self, count):
        self.count = count
        self.reach = count // 2
        self.ring = list(range(0, count, 2)) + list(range(count - 1, 0, -2))
        ahead = [(self.ring[i], self.ring[(i + 1) % count]) for i in range(count)]
        self.pairs = (ahead, [(b, a) for a, b in ahead])

    def send(self, values, direction):
        return lax.ppermute(values, "dp", self.pairs[direction])


class Gathering:
    def __init__(self, route, block, longer):
        self.route = route
        self.blocks = {0: block}
        self.steps = 0
        self.hops = [route.reach - (direction != longer) for direction in range(2)]
        self.done = 0
        self.flying = [block]

    def pending(self):
        return self.flying

    def resume(self, arrived):
        route = self.route
        if self.done == 0:
            self.blocks[0] = arrived[0]
            latest = [arrived[0], arrived[0]]
        else:
            arrived = list(arrived)
            latest = [None, None]
            for direction in range(2):
                if self.done <= self.hops[direction]:
                    latest[direction] = arrived.pop(0)
                    at = route.count - self.done if direction == 0 else self.done
                    self.blocks[at] = latest[direction]
        self.done += 1
        self.flying = [
            route.send(latest[direction], direction)
            for direction in range(2)
            if self.done <= self.hops[direction]
        ]

    def all(self):
        return [self.blocks[j] for j in range(self.route.count)]


class Summing:
    def __init__(self, route, own, rows, per, offset, longer):
        self.route = route
        self.own = own
        self.rows = rows
        self.place = lambda j: per * j + offset
        self.hops = [route.reach - (direction != longer) for direction in range(2)]
        self.steps = 0
        self.done = 0
        self.flying = None
        self.last = [None, None]

    def terms(self, arrived, directions):
        places = []
        for direction in directions:
            left = self.hops[direction] - self.done
            at = left if direction == 0 else (self.route.count - left) % self.route.count
            places.append(self.place(at))
        return hand_on(arrived, self.own(), self.rows, places)

    def pending(self):
        return self.flying if self.done else self.terms([], range(2))

    def resume(self, arrived):
        arrived = list(arrived)
        onward = range(2)
        if self.done:
            landed = [direction for direction in range(2) if self.done <= self.hops[direction]]
            onward = [direction for direction in landed if self.done < self.hops[direction]]
            by_way = dict(zip(landed, arrived))
            for direction in landed:
                if self.done == self.hops[direction]:
                    self.last[direction] = by_way[direction]
            if onward:
                arrived = self.terms([by_way[direction] for direction in onward], onward)
        self.done += 1
        self.flying = [self.route.send(values, way) for way, values in zip(onward, arrived)]

    def total(self, part, first):
        at = self.place(0) * self.rows
        own = part[at : at + self.rows].astype(F32)
        span = slice(first, first + part.shape[1])
        return own + self.last[0][:, span].astype(F32) + self.last[1][:, span].astype(F32)


STEPS = 5


class Pace:
    def __init__(self, token):
        self.token = token

    def __call__(self, streams, *carried, busy=False, long=False):
        last = {}
        for stream in streams:
            stream.steps += 1
            last[stream] = (stream.steps * (stream.route.reach + 1)) // STEPS
        first = True
        while first or any(stream.done < last[stream] for stream in streams):
            first = False
            moving = [stream for stream in streams if stream.done < last[stream]]
            waiting = [list(stream.pending()) for stream in moving]
            flat = [values for group in waiting for values in group]
            self.token, *out = lax.optimization_barrier((self.token, *flat, *carried))
            carried = out[len(flat) :]
            at = 0
            for stream, group in zip(moving, waiting):
                stream.resume(out[at : at + len(group)])
                at += len(group)
        if not busy:
            self.token = mark(self.token, 10**12 if long else 10**9)
            self.token, *carried = lax.optimization_barrier((self.token, *carried))
        return carried[0] if len(carried) == 1 else carried


def across_core(values):
    return lax.ppermute(values, "tensor", [(i, i ^ 1) for i in range(4)])


def across_chip(values):
    return lax.ppermute(values, "tensor", [(i, i ^ 2) for i in range(4)])


def halve(route, table):
    left = table.shape[0] // 2
    pairs = [(route.ring[i], route.ring[(i + left) % route.count]) for i in range(route.count)]
    return lax.ppermute(table[left:], "dp", pairs)


def on_device(
    route,
    activations,
    cotangent,
    segments,
    norm_one_gain,
    norm_one_bias,
    w_query,
    w_key,
    w_value,
    qkv_bias,
    w_out,
    norm_two_gain,
    norm_two_bias,
    w_gate,
    w_up,
    w_down,
):
    count = route.count
    third, depth = activations.shape
    length = segments.shape[0]
    width = depth // count
    part = width // 2
    heads_wide = w_query.shape[1]
    local_heads = heads_wide // HD
    shards = length // third
    here = lax.axis_index("tensor")
    place = here.astype(jnp.int32).reshape(1)
    advance = Pace(jnp.zeros((8, 128), jnp.int32) + here)
    device = lax.axis_index("dp").astype(jnp.int32)
    position = jnp.where(device % 2 == 0, device // 2, count - 1 - device // 2)
    ahead = (position + jnp.arange(count, dtype=jnp.int32)) % count
    order = jnp.where(ahead < count // 2, 2 * ahead, 2 * (count - 1 - ahead) + 1)

    def gather(values):
        return lax.all_gather(values, "tensor", axis=0, tiled=True)

    def scatter(values):
        return lax.psum_scatter(values, "tensor", scatter_dimension=0, tiled=True)

    def relative(values):
        def pick(entries):
            return jnp.concatenate([values[i : i + 1] for i in entries], axis=0)

        values = jnp.where(here % 2 == 1, pick((1, 0, 3, 2)), values)
        return jnp.where(here >= 2, pick((2, 3, 0, 1)), values)

    bias_size = qkv_bias.size
    norm_part = norm_one_gain.shape[0]
    ring_qk = Gathering(route, jnp.concatenate([w_query, w_key], axis=1), 0)
    ring_vo = Gathering(route, None, 1)
    ring_gate = Gathering(route, w_gate, 0)
    ring_up = Gathering(route, w_up, 1)
    ring_down = [Gathering(route, None, 0), Gathering(route, None, 1)]

    packed = jnp.stack([norm_one_gain, norm_one_bias, norm_two_gain, norm_two_bias])
    packed_core = across_core(packed)
    own_bf16 = reorder(order, activations)
    x_all = gather(own_bf16)
    packed = jnp.concatenate([packed, packed_core], axis=0)
    packed, w_down, w_value, w_out, cotangent = advance(
        [], packed, w_down, w_value, w_out, cotangent
    )
    packed_chip = across_chip(packed)
    weight_vo = jnp.concatenate([w_value, w_out.T], axis=1)
    packed_chip, weight_vo, cotangent, w_down = advance(
        [], packed_chip, weight_vo, cotangent, w_down
    )
    packed = jnp.concatenate([packed, packed_chip], axis=0).reshape(shards, 4, norm_part)
    packed = relative(packed).transpose(1, 0, 2).reshape(4, width)
    wide = 2 * heads_wide
    packed = jnp.concatenate(
        [
            jnp.pad(packed, ((0, 0), (0, wide - width))),
            jnp.pad(qkv_bias.reshape(1, bias_size), ((0, 11), (0, wide - bias_size))),
        ],
        axis=0,
    )
    ring_vo.flying = [jnp.concatenate([weight_vo, packed], axis=0)]
    cotangent, w_down = advance([ring_qk, ring_vo], cotangent, w_down, long=True)
    own_grad = reorder(order, cotangent)
    own_grad, w_down = advance([ring_qk], own_grad, w_down)
    down_rows = w_down.T
    ring_down[0].flying = [down_rows[:part]]
    ring_down[1].flying = [down_rows[part:]]
    x_all, own_grad = advance([ring_vo], x_all, own_grad)
    grad_all = gather(own_grad)
    mean_one, inverse_one = row_stats(x_all)
    mean_one, inverse_one, segments = advance([ring_qk], mean_one, inverse_one, segments)
    segment_down, segment_across = segments[:, None], segments[None, :]
    begins = jnp.sum((segment_across < segment_down).astype(F32), axis=1, keepdims=True)
    places = jnp.arange(length, dtype=jnp.int32)[:, None].astype(F32)
    lanes = jnp.arange(PAIR, dtype=jnp.int32) % HD
    frequency = 10000.0 ** (-2.0 * (lanes % (ROT // 2)).astype(F32) / ROT)
    angles = (places - begins) * frequency[None, :]
    cos_table = jnp.where(lanes < ROT, jnp.cos(angles), 1.0)
    sin_table = jnp.where(
        lanes < ROT, jnp.where(lanes < ROT // 2, -1.0, 1.0) * jnp.sin(angles), 0.0
    )
    cos_table, sin_table, segment_down, segment_across = advance(
        [ring_vo], cos_table, sin_table, segment_down, segment_across
    )
    advance([ring_qk], long=True)
    grad_all = advance([ring_vo], grad_all)
    advance([ring_qk, ring_gate])
    advance([ring_vo, ring_up], busy=True)
    blocks_a = ring_qk.all()
    blocks_b = ring_vo.all()
    norm_rows, bias_row = decode(order, blocks_b, depth, 3 * heads_wide)
    qk, values, normed = project_qkv(
        x_all, mean_one, inverse_one, norm_rows, bias_row, cos_table, sin_table, blocks_a, blocks_b
    )
    qk, values = advance([ring_gate], qk, values, busy=True)
    mixed, lse = attend_forward(qk, values, segment_down, segment_across, shards)
    mixed, lse = advance([ring_up], mixed, lse, busy=True)
    arriving = scatter(outward([(mixed, blocks_b, heads_wide)], depth, "from_heads")[0])
    advance([ring_gate])
    advance([ring_up], long=True)
    arriving = advance([ring_gate], arriving)
    middle, mean_two, inverse_two, n_own = second_norm(own_bf16, [arriving], norm_rows)
    normed_two = gather(n_own)
    middle = advance([], middle, long=True)
    advance([ring_up, ring_down[0]])
    advance([ring_gate])
    advance([ring_up, ring_down[1]])
    advance([ring_down[0]])
    normed_two = advance([ring_down[1]], normed_two, busy=True)
    gate_blocks = ring_gate.all()
    up_blocks = ring_up.all()
    kept = gated_forward(normed_two, gate_blocks, up_blocks, 0, None)
    kept = advance([ring_down[0]], *kept)
    kept = advance([ring_down[1]], *kept, busy=True)
    gate, up, hidden = gated_forward(normed_two, gate_blocks, up_blocks, 1, kept)
    gate, up, hidden = advance([ring_down[0]], gate, up, hidden)
    hidden = advance([ring_down[1]], hidden)
    down_sum = product(grad_all, hidden, 0, 0).astype(BF16)
    sum_down = Summing(route, lambda: [down_sum], width, 1, 0, 0)
    down_sum = advance([ring_down[0]], down_sum)
    advance([ring_down[1], sum_down], busy=True)
    down_blocks = [block for pair in zip(*(ring.all() for ring in ring_down)) for block in pair]

    gate_grad, up_grad = gated_backward(grad_all, gate, up, down_blocks)
    gate_grad, up_grad = advance([sum_down], gate_grad, up_grad)
    gate_sum = product(normed_two, gate_grad, 0, 0).astype(BF16)
    sum_gate = Summing(route, lambda: [gate_sum], width, 1, 0, 1)
    gate_sum, gate_grad, up_grad = advance([sum_gate], gate_sum, gate_grad, up_grad, busy=True)
    own, cross = outward(
        [(gate_grad, gate_blocks, None), (up_grad, up_blocks, None)], depth, "from_gates", place
    )
    own, cross = advance([sum_down], own, cross)
    own, cross, up_grad = advance([sum_gate], own, cross, up_grad, busy=True)
    arrived = across_core(cross)
    own, arrived, up_grad = advance([], own, arrived, up_grad, busy=True)
    far, near = meet(own, arrived)
    arriving = across_chip(far)
    near, up_grad = advance([], near, up_grad)
    up_sum = product(normed_two, up_grad, 0, 0).astype(BF16)
    sum_up = Summing(route, lambda: [up_sum], width, 1, 0, 0)
    up_sum = advance([sum_down], up_sum)
    arriving = advance([sum_gate], arriving)
    middle_grad, b_own, two_sums = second_norm_back(
        [near, arriving], middle, mean_two, inverse_two, norm_rows, own_grad
    )
    branch = gather(b_own)
    hidden, middle_grad = advance([], hidden, middle_grad, long=True)
    (result_terms,) = outward([(hidden, down_blocks, None)], depth, "from_hidden")
    result_terms = advance([sum_down, sum_up], result_terms)
    advance([sum_gate])
    branch, result_terms = advance([sum_up], branch, result_terms, busy=True)
    arriving_result = scatter(result_terms)
    mixed_grad = through_out(branch, blocks_b)
    mixed_grad, branch = advance([sum_gate], mixed_grad, branch, busy=True)
    grads = None
    for half in range(2):
        grads = attend_backward(
            qk,
            values,
            mixed,
            mixed_grad,
            lse,
            segment_down,
            segment_across,
            cos_table,
            sin_table,
            shards,
            half,
            grads,
        )
        grads = advance([sum_up], *grads, busy=half == 0)
    q_grad, k_grad, v_grad, bias_sums = grads
    q_sum = product(normed, q_grad, 0, 0).astype(BF16)
    k_sum = product(normed, k_grad, 0, 0).astype(BF16)
    sum_qk = Summing(route, lambda: [q_sum, k_sum], width, 1, 0, 1)
    q_sum, k_sum, v_grad, branch = advance([sum_qk], q_sum, k_sum, v_grad, branch)
    out_sum = product(branch, mixed, 0, 0).astype(BF16)
    v_sum = product(normed, v_grad, 0, 0).astype(BF16)
    sum_vo = Summing(route, lambda: [v_sum, out_sum], width, 1, 0, 0)
    out_sum, v_sum, q_grad, arriving_result = advance(
        [sum_qk, sum_vo], out_sum, v_sum, q_grad, arriving_result, busy=True
    )
    heads_terms, one_sums = through_heads(
        [q_grad, k_grad, v_grad], x_all, mean_one, inverse_one, blocks_a, blocks_b
    )
    arriving = scatter(heads_terms)
    one_sums, middle, arriving_result, down_sum = advance(
        [sum_up, sum_vo], one_sums, middle, arriving_result, down_sum, long=True
    )
    norm_grads = jnp.concatenate([one_sums, two_sums], axis=0)
    bias_sums = bias_sums.transpose(1, 0, 2).reshape(3, local_heads, count, HD // count)
    bias_sums = bias_sums.transpose(2, 0, 1, 3).reshape(count, bias_size)[order]
    extras = jnp.concatenate(
        [norm_grads.reshape(4, count, width).transpose(1, 0, 2).reshape(count, 4 * width), bias_sums],
        axis=1,
    )
    extras = jnp.pad(extras, ((0, 0), (0, -extras.shape[1] % 128)))
    result = finish_result(order, middle, arriving_result)
    moved = halve(route, extras)
    extras, moved, result, down_sum, gate_sum = advance(
        [sum_qk], extras, moved, result, down_sum, gate_sum
    )
    grad_down = sum_down.total(down_sum, 0).T
    extras = extras[: moved.shape[0]] + moved
    moved = halve(route, extras)
    extras, moved, grad_down, gate_sum = advance([sum_vo], extras, moved, grad_down, gate_sum)
    grad_gate = sum_gate.total(gate_sum, 0)
    extras = extras[: moved.shape[0]] + moved
    while extras.shape[0] > 2:
        extras = extras[: extras.shape[0] // 2] + halve(route, extras)
    moved = halve(route, extras)
    extras, moved, grad_gate, up_sum = advance([sum_qk], extras, moved, grad_gate, up_sum)
    grad_up = sum_up.total(up_sum, 0)
    extras = (extras[:1] + moved)[0]
    bias_grad = extras[4 * width : 4 * width + bias_size].reshape(qkv_bias.shape)
    norm_sums = extras[: 4 * width].reshape(4, width)
    moved = across_core(norm_sums)
    grad_up, moved = advance([sum_vo], grad_up, moved)
    norm_sums = norm_sums + moved
    moved = across_chip(norm_sums)
    moved = advance([sum_qk], moved)
    norm_sums = norm_sums + moved
    norm_sums = lax.dynamic_slice_in_dim(norm_sums, here * norm_part, norm_part, axis=1)
    arriving = advance([], arriving)
    input_grad = input_back(order, arriving, own_bf16, norm_rows, middle_grad)
    input_grad, norm_sums = advance([sum_vo], input_grad, norm_sums)

    return (
        result,
        input_grad,
        norm_sums[0],
        norm_sums[1],
        sum_qk.total(q_sum, 0),
        sum_qk.total(k_sum, heads_wide),
        sum_vo.total(v_sum, 0),
        bias_grad,
        sum_vo.total(out_sum, heads_wide).T,
        norm_sums[2],
        norm_sums[3],
        grad_gate,
        grad_up,
        grad_down,
    )


def solution(mesh):
    both = P(("dp", "tensor"))
    tokens = P(("dp", "tensor"), None)
    rows = P("dp", "tensor")
    columns = P("tensor", "dp")
    biases = P(None, "tensor", "dp")
    return jax.shard_map(
        functools.partial(on_device, Route(mesh.shape["dp"])),
        mesh=mesh,
        in_specs=(
            tokens,
            tokens,
            P("dp"),
            both,
            both,
            rows,
            rows,
            rows,
            biases,
            columns,
            both,
            both,
            rows,
            rows,
            columns,
        ),
        out_specs=(
            tokens,
            tokens,
            both,
            both,
            rows,
            rows,
            rows,
            biases,
            columns,
            both,
            both,
            rows,
            rows,
            columns,
        ),
        check_vma=False,
    )
```

```python
import functools

import jax
import jax.experimental.pallas as pl
import jax.experimental.pallas.tpu as pltpu
import jax.numpy as jnp
from jax import lax
from jax.sharding import PartitionSpec as P

HD = 64
ROT = 16
PAIR = 2 * HD
EPSILON = 1e-05
NEGATIVE = -1e30
F32 = jnp.float32
BF16 = jnp.bfloat16
MIB = 2**20
LIGHT = pl.CostEstimate(flops=10**9, bytes_accessed=1, transcendentals=1)
LONG = pl.CostEstimate(flops=10**12, bytes_accessed=1, transcendentals=1)


def product(left, right, left_dim, right_dim):
    return lax.dot_general(
        left, right, (((left_dim,), (right_dim,)), ((), ())), preferred_element_type=F32
    )


def turn(columns, cos_values, sin_values, opening):
    partner = jnp.where(opening, pltpu.roll(columns, PAIR - 8, 1), pltpu.roll(columns, 8, 1))
    return columns * cos_values + partner * sin_values


def opening_lanes(rows):
    return lax.broadcasted_iota(jnp.int32, (rows, PAIR), 1) % HD < 8


def forward_body(block, count, q_ref, k_ref, v_ref, down_ref, across_ref, mixed_ref, lse_ref):
    lane = lax.broadcasted_iota(jnp.int32, (block, PAIR), 1)
    earlier = lax.broadcasted_iota(jnp.int32, (block, block), 1) <= lax.broadcasted_iota(
        jnp.int32, (block, block), 0
    )
    spans = [pl.ds(i * block, block) for i in range(count)]
    for i in range(count):
        queries = q_ref[spans[i], :] * jnp.asarray(HD**-0.5, BF16)
        segment = down_ref[spans[i], :]
        kept = [across_ref[:, spans[j]] == segment for j in range(i + 1)]
        kept[i] = kept[i] & earlier
        sums = []
        for half in range(2):
            mine = lane < HD if half == 0 else lane >= HD
            chosen = jnp.where(mine, queries, jnp.zeros_like(queries))
            scores = [
                jnp.where(kept[j], product(chosen, k_ref[spans[j], :], 1, 1), NEGATIVE)
                for j in range(i + 1)
            ]
            tops = scores[0]
            for part in scores[1:]:
                tops = jnp.maximum(tops, part)
            top = tops.max(1, keepdims=True)
            out = None
            for j in range(i + 1):
                values = v_ref[spans[j], :]
                beside = jnp.where(mine, values, jnp.ones_like(values))
                term = product(jnp.exp(scores[j] - top).astype(BF16), beside, 1, 0)
                out = term if out is None else out + term
            other = slice(HD, HD + 1) if half == 0 else slice(0, 1)
            total = out[:, other]
            sums.append(out * (1.0 / total))
            lse = jnp.broadcast_to(top + jnp.log(total), (block, PAIR))
            lse_ref[0, half : half + 1, spans[i]] = lse.T[0:1, :]
        mixed_ref[spans[i], :] = jnp.where(lane < HD, sums[0], sums[1]).astype(BF16)


def attend_forward(qk, values, segment_down, segment_across, count):
    length, width = values.shape
    pairs = width // PAIR
    columns = lambda first: pl.BlockSpec((length, PAIR), lambda h: (0, h + first))
    whole = lambda shape: pl.BlockSpec(shape, lambda h: (0, 0))
    return pl.pallas_call(
        functools.partial(forward_body, length // count, count),
        grid_spec=pltpu.PrefetchScalarGridSpec(
            num_scalar_prefetch=0,
            grid=(pairs,),
            in_specs=[columns(0), columns(pairs), columns(0), whole((length, 1)), whole((1, length))],
            out_specs=[columns(0), pl.BlockSpec((1, 2, length), lambda h: (h, 0, 0))],
        ),
        out_shape=[
            jax.ShapeDtypeStruct((length, width), BF16),
            jax.ShapeDtypeStruct((pairs, 2, length), F32),
        ],
        compiler_params=pltpu.CompilerParams(vmem_limit_bytes=60 * MIB),
        cost_estimate=LIGHT,
        name="attend_forward",
    )(qk, qk, values, segment_down, segment_across)


def backward_body(
    block,
    count,
    kept,
    q_ref,
    k_ref,
    v_ref,
    mixed_ref,
    grad_ref,
    lse_ref,
    down_ref,
    across_ref,
    cos_ref,
    sin_ref,
    *refs,
):
    q_grad_ref, k_grad_ref, v_grad_ref, bias_ref, q_total, k_total, v_total = refs[kept:]
    lane = lax.broadcasted_iota(jnp.int32, (block, PAIR), 1)
    earlier = lax.broadcasted_iota(jnp.int32, (block, block), 0) <= lax.broadcasted_iota(
        jnp.int32, (block, block), 1
    )
    spans = [pl.ds(i * block, block) for i in range(count)]
    turned = [k_ref[span, :].T for span in spans]
    for i in range(count):
        queries = q_ref[spans[i], :] * jnp.asarray(HD**-0.5, BF16)
        upstream = grad_ref[spans[i], :]
        centres = (upstream.astype(F32) * mixed_ref[spans[i], :].astype(F32)).T
        segment = across_ref[:, spans[i]]
        allowed = [down_ref[spans[j], :] == segment for j in range(i + 1)]
        allowed[i] = allowed[i] & earlier
        sums = []
        for half in range(2):
            mine = lane < HD if half == 0 else lane >= HD
            nothing = jnp.zeros_like(queries)
            chosen = jnp.where(mine, queries, nothing)
            chosen_grad = jnp.where(mine, upstream, nothing)
            log_total = lse_ref[0, half : half + 1, spans[i]]
            centre = centres[half * HD : (half + 1) * HD, :].sum(0, keepdims=True)
            q_sum = None
            for j in range(i + 1):
                keys = k_ref[spans[j], :]
                scores = jnp.where(allowed[j], product(keys, chosen, 1, 1), NEGATIVE)
                weights = jnp.exp(scores - log_total)
                weight_grad = product(v_ref[spans[j], :], chosen_grad, 1, 1)
                score_grad = (weights * (weight_grad - centre)).astype(BF16)
                v_term = product(weights.astype(BF16), chosen_grad, 1, 0)
                k_term = product(score_grad, chosen, 1, 0)
                term = product(turned[j], score_grad, 1, 0)
                q_sum = term if q_sum is None else q_sum + term
                if i == j and half == 0:
                    v_total[spans[j], :] = v_term
                    k_total[spans[j], :] = k_term
                else:
                    v_total[spans[j], :] += v_term
                    k_total[spans[j], :] += k_term
            sums.append(q_sum[half * HD : (half + 1) * HD, :])
        q_total[spans[i], :] = jnp.concatenate(sums, axis=0).T
    opening = opening_lanes(block * count)
    cos_values = cos_ref[...]
    sin_values = -sin_ref[...]
    q_grad = turn(q_total[...] * (HD**-0.5), cos_values, sin_values, opening).astype(BF16)
    k_grad = turn(k_total[...], cos_values, sin_values, opening).astype(BF16)
    v_grad = v_total[...].astype(BF16)
    for at, (ref, grad) in enumerate(
        ((q_grad_ref, q_grad), (k_grad_ref, k_grad), (v_grad_ref, v_grad))
    ):
        ref[...] = grad
        bias_ref[0, at : at + 1, :] = grad.astype(F32).sum(0, keepdims=True)


def attend_backward(
    qk, values, mixed, mixed_grad, lse, segment_down, segment_across, cos_table, sin_table, count, half, kept
):
    length, width = values.shape
    pairs = width // PAIR
    kept = list(kept or [])
    some = pairs // 2
    start = half * some
    columns = lambda first: pl.BlockSpec((length, PAIR), lambda h: (0, h + first + start))
    whole = lambda shape: pl.BlockSpec(shape, lambda h: (0, 0))
    return pl.pallas_call(
        functools.partial(backward_body, length // count, count, len(kept)),
        grid_spec=pltpu.PrefetchScalarGridSpec(
            num_scalar_prefetch=0,
            grid=(some,),
            in_specs=[
                columns(0),
                columns(pairs),
                columns(0),
                columns(0),
                columns(0),
                pl.BlockSpec((1, 2, length), lambda h: (h + start, 0, 0)),
                whole((length, 1)),
                whole((1, length)),
                whole((length, PAIR)),
                whole((length, PAIR)),
            ]
            + [pl.BlockSpec(memory_space=pl.ANY)] * len(kept),
            out_specs=[
                columns(0),
                columns(0),
                columns(0),
                pl.BlockSpec((1, 3, PAIR), lambda h: (h + start, 0, 0)),
            ],
            scratch_shapes=[pltpu.VMEM((length, PAIR), F32)] * 3,
        ),
        out_shape=[jax.ShapeDtypeStruct((length, width), BF16)] * 3
        + [jax.ShapeDtypeStruct((pairs, 3, PAIR), F32)],
        input_output_aliases={10 + i: i for i in range(len(kept))},
        compiler_params=pltpu.CompilerParams(vmem_limit_bytes=60 * MIB),
        cost_estimate=LONG,
        name="attend_backward",
    )(
        qk, qk, values, mixed, mixed_grad, lse, segment_down, segment_across, cos_table, sin_table, *kept
    )


HBM = pl.BlockSpec(memory_space=pl.ANY)


def whole(shape):
    return pl.BlockSpec(shape, lambda *_: (0,) * len(shape), pipeline_mode=pl.Buffered(1))


def shaped(shape, dtype=BF16):
    return jax.ShapeDtypeStruct(shape, dtype)


def kernel_call(body, name, operands, in_specs, out_specs, out_shape, grid=(), scratch=(), scalars=(), aliases=None, vmem=40, flops=1, kept=False):
    return pl.pallas_call(
        body,
        grid_spec=pltpu.PrefetchScalarGridSpec(
            num_scalar_prefetch=len(scalars),
            grid=grid,
            in_specs=in_specs,
            out_specs=out_specs,
            scratch_shapes=list(scratch),
        ),
        out_shape=out_shape,
        input_output_aliases=aliases or {},
        compiler_params=pltpu.CompilerParams(vmem_limit_bytes=vmem * MIB, has_side_effects=kept),
        cost_estimate=pl.CostEstimate(flops=flops, bytes_accessed=1, transcendentals=1),
        name=name,
    )(*scalars, *operands)


def copies_into(blocks, target, semaphores, first, columns=None, rows=None):
    copies, at = [], 0
    for i, block in enumerate(blocks):
        deep = rows or block.shape[0]
        source = block if columns is None else block.at[pl.ds(0, deep), columns]
        copies.append(
            pltpu.make_async_copy(source, target.at[pl.ds(at, deep), :], semaphores.at[first + i])
        )
        at += deep
    return copies


def start_all(step, copies):
    @pl.when(step == 0)
    def _():
        for copy in copies:
            copy.start()


def wait_at(step, when, copies):
    @pl.when(step == when)
    def _():
        for copy in copies:
            copy.wait()


def halves(copies):
    return copies[: len(copies) // 2], copies[len(copies) // 2 :]


def mark_body(in_ref, out_ref):
    out_ref[...] = in_ref[...]


def mark(token, flops):
    return kernel_call(
        mark_body,
        "mark",
        [token],
        [whole(token.shape)],
        whole(token.shape),
        shaped(token.shape, token.dtype),
        grid=(1,),
        flops=flops,
        kept=True,
    )


def pick_columns(order, values):
    count = order.shape[0]
    width = values.shape[1] // count
    parts = [lax.dynamic_slice_in_dim(values, order[j] * width, width, 1) for j in range(count)]
    return jnp.concatenate(parts, axis=1)


def back_in_place(order, values):
    count = order.shape[0]
    if values.shape[1] // count % 128 == 0:
        return values
    places = jnp.arange(count, dtype=jnp.int32)
    back = jnp.sum(jnp.where(order[:, None] == places[None, :], places[:, None], 0), axis=0)
    return pick_columns(back, values)


def chunks(wide):
    return [(at, min(256, wide - at)) for at in range(0, wide, 256)]


def reorder_body(count, width, order_ref, in_ref, out_ref):
    for j in range(count):
        source = pl.ds(pl.multiple_of(order_ref[j] * width, width), width)
        out_ref[:, j * width : (j + 1) * width] = in_ref[:, source]


def reorder(order, values):
    count = order.shape[0]
    if values.shape[1] // count % 128:
        return pick_columns(order, values)
    return kernel_call(
        functools.partial(reorder_body, count, values.shape[1] // count),
        "reorder",
        [values],
        [whole(values.shape)],
        whole(values.shape),
        shaped(values.shape),
        grid=(1,),
        scalars=[order],
    )


def put_back(order_ref, out_ref, values):
    count = order_ref.shape[0]
    width = values.shape[1] // count
    if width % 128:
        out_ref[...] = values.astype(out_ref.dtype)
        return
    for j in range(count):
        target = pl.ds(pl.multiple_of(order_ref[j] * width, width), width)
        out_ref[:, target] = values[:, j * width : (j + 1) * width].astype(out_ref.dtype)


def stats_body(x_ref, mean_ref, inverse_ref):
    values = x_ref[...].astype(F32)
    mean = jnp.mean(values, axis=-1, keepdims=True)
    centred = values - mean
    mean_ref[...] = mean
    inverse_ref[...] = lax.rsqrt(jnp.mean(centred * centred, axis=-1, keepdims=True) + EPSILON)


def row_stats(inputs):
    length, depth = inputs.shape
    by_rows = lambda columns: pl.BlockSpec((length // 4, columns), lambda i: (i, 0))
    return kernel_call(
        stats_body,
        "row_stats",
        [inputs],
        [by_rows(depth)],
        [by_rows(1)] * 2,
        [shaped((length, 1), F32)] * 2,
        grid=(4,),
    )


def decode_body(count, chunk, order_ref, *refs):
    blocks, norm_ref, bias_ref = refs[:count], refs[-2], refs[-1]
    width = norm_ref.shape[1] // count
    wide = bias_ref.shape[1]
    small = wide // count
    rows = []
    for j, block in enumerate(blocks):
        norm_ref[:, j * width : (j + 1) * width] = block[0:4, :width].astype(F32)
        rows.append(block[4:5, :small].astype(F32))
    lane = lax.broadcasted_iota(jnp.int32, (small, wide), 1)
    source = lax.broadcasted_iota(jnp.int32, (small, wide), 0)
    spread = (lane // HD * chunk + lane % chunk == source).astype(BF16)
    spread = product(jnp.concatenate(rows, axis=0).astype(BF16), spread, 1, 0)
    lane = lax.broadcasted_iota(jnp.int32, (1, wide), 1)
    total = jnp.zeros((1, wide), F32)
    for j in range(count):
        total = jnp.where(lane % HD // chunk == order_ref[j], spread[j : j + 1, :], total)
    bias_ref[...] = total


def decode(order, blocks, depth, bias_wide):
    count = len(blocks)
    rows, wide = blocks[0].shape
    return kernel_call(
        functools.partial(decode_body, count, HD // count),
        "decode",
        blocks,
        [pl.BlockSpec((16, wide), lambda i, order: (rows // 16 - 1, 0))] * count,
        [whole((4, depth)), whole((1, bias_wide))],
        [shaped((4, depth), F32), shaped((1, bias_wide), F32)],
        grid=(1,),
        scalars=[order],
    )


def qkv_body(count, x_ref, norm_ref, bias_ref, mean_ref, inverse_ref, cos_ref, sin_ref, *refs):
    blocks_a, blocks_b, refs = refs[:count], refs[count : 2 * count], refs[2 * count :]
    qk_ref, v_ref, normed_ref, weight_a, weight_v, semaphores = refs
    step = pl.program_id(0)
    width = qk_ref.shape[1]
    deep = weight_a.shape[0] // count
    copies_a = copies_into(blocks_a, weight_a, semaphores, 0, rows=deep)
    copies_v = copies_into(blocks_b, weight_v, semaphores, count, pl.ds(0, width // 2), deep)
    start_all(step, copies_a + copies_v)
    values = (x_ref[...].astype(F32) - mean_ref[...]) * inverse_ref[...]
    normed = (values * norm_ref[0:1, :] + norm_ref[1:2, :]).astype(BF16)
    normed_ref[...] = normed
    wait_at(step, 0, copies_a + copies_v)
    opening = opening_lanes(normed.shape[0])
    cos_values = cos_ref[...]
    sin_values = sin_ref[...]
    for at, wide in chunks(width):
        both = product(normed, weight_a[:, at : at + wide], 1, 0) + bias_ref[:, at : at + wide]
        for pair in range(0, wide, PAIR):
            part = turn(both[:, pair : pair + PAIR], cos_values, sin_values, opening)
            qk_ref[:, at + pair : at + pair + PAIR] = part.astype(BF16)
    for at, wide in chunks(width // 2):
        values = product(normed, weight_v[:, at : at + wide], 1, 0)
        bias = bias_ref[:, width + at : width + at + wide]
        v_ref[:, at : at + wide] = (values + bias).astype(BF16)


def project_qkv(inputs, mean, inverse, norm_rows, bias_row, cos_table, sin_table, blocks_a, blocks_b):
    length, depth = inputs.shape
    rows = length // 4
    wide = blocks_a[0].shape[1]
    count = len(blocks_a)
    by_rows = lambda columns: pl.BlockSpec((rows, columns), lambda i: (i, 0))
    return kernel_call(
        functools.partial(qkv_body, count),
        "project_qkv",
        [inputs, norm_rows, bias_row, mean, inverse, cos_table, sin_table, *blocks_a, *blocks_b],
        [
            by_rows(depth),
            whole(norm_rows.shape),
            whole(bias_row.shape),
            by_rows(1),
            by_rows(1),
            by_rows(PAIR),
            by_rows(PAIR),
        ]
        + [HBM] * (2 * count),
        [by_rows(wide), by_rows(wide // 2), by_rows(depth)],
        [shaped((length, wide)), shaped((length, wide // 2)), shaped((length, depth))],
        grid=(4,),
        flops=10**9,
        scratch=[
            pltpu.VMEM((depth, wide), BF16),
            pltpu.VMEM((depth, wide // 2), BF16),
            pltpu.SemaphoreType.DMA((2 * count,)),
        ],
        vmem=60,
    )


def gated_body(count, x_ref, *refs):
    gate_blocks, up_blocks, refs = refs[:count], refs[count : 2 * count], refs[2 * count :]
    gate_ref, up_ref, hidden_ref, gate_weight, up_weight, semaphores = refs[-6:]
    step = pl.program_id(0)
    early, late = halves(copies_into(gate_blocks, gate_weight, semaphores, 0))
    early_up, late_up = halves(copies_into(up_blocks, up_weight, semaphores, count))
    start_all(step, early + late + early_up + late_up)
    half = gate_weight.shape[0] // 2
    wait_at(step, 0, early)
    gate = product(x_ref[:, :half], gate_weight[:half, :], 1, 0)
    wait_at(step, 0, late)
    gate = gate + product(x_ref[:, half:], gate_weight[half:, :], 1, 0)
    gate_ref[...] = gate.astype(BF16)
    wait_at(step, 0, early_up + late_up)
    up = product(x_ref[...], up_weight[...], 1, 0)
    up_ref[...] = up.astype(BF16)
    hidden_ref[...] = (gate * jax.nn.sigmoid(gate) * up).astype(BF16)


def gated_forward(inputs, gate_blocks, up_blocks, half, kept):
    length, depth = inputs.shape
    rows = length // 4
    wide = gate_blocks[0].shape[1]
    count = len(gate_blocks)
    kept = list(kept or [])
    place = lambda columns: pl.BlockSpec((rows, columns), lambda i: (2 * half + i, 0))
    first = 1 + 2 * count
    return kernel_call(
        functools.partial(gated_body, count),
        "gated_forward",
        [inputs, *gate_blocks, *up_blocks, *kept],
        [place(depth)] + [HBM] * (2 * count + len(kept)),
        [place(wide)] * 3,
        [shaped((length, wide))] * 3,
        grid=(2,),
        flops=10**9,
        scratch=[
            pltpu.VMEM((depth, wide), BF16),
            pltpu.VMEM((depth, wide), BF16),
            pltpu.SemaphoreType.DMA((2 * count,)),
        ],
        aliases={first + i: i for i in range(len(kept))},
        vmem=60,
    )


def gated_back_body(count, *refs):
    grad_ref, gate_ref, up_ref, refs = refs[0], refs[1], refs[2], refs[3:]
    blocks = refs[:count]
    gate_grad_ref, up_grad_ref, weight, semaphores = refs[-4:]
    step = pl.program_id(0)
    copies = copies_into(blocks, weight, semaphores, 0)
    start_all(step, copies)
    wait_at(step, 0, copies)
    rows = grad_ref[...]
    for at, wide in chunks(weight.shape[1]):
        span = slice(at, at + wide)
        hidden_grad = product(rows, weight[:, span], 1, 0)
        gate = gate_ref[:, span].astype(F32)
        sigmoid = jax.nn.sigmoid(gate)
        silu = gate * sigmoid
        up_grad_ref[:, span] = (hidden_grad * silu).astype(BF16)
        slope = sigmoid + silu * (1.0 - sigmoid)
        gate_grad_ref[:, span] = (hidden_grad * up_ref[:, span].astype(F32) * slope).astype(BF16)


def gated_backward(grads, gate, up, blocks):
    length, wide = gate.shape
    rows = length // 4
    depth = grads.shape[1]
    count = len(blocks)
    by_rows = lambda columns: pl.BlockSpec((rows, columns), lambda i: (i, 0))
    return kernel_call(
        functools.partial(gated_back_body, count),
        "gated_backward",
        [grads, gate, up, *blocks],
        [by_rows(depth), by_rows(wide), by_rows(wide)] + [HBM] * count,
        [by_rows(wide)] * 2,
        [shaped((length, wide))] * 2,
        grid=(4,),
        flops=10**9,
        scratch=[pltpu.VMEM((depth, wide), BF16), pltpu.SemaphoreType.DMA((count,))],
        vmem=60,
    )


STRIPES = 4


def outward_body(shape, columns, deep, apart, *refs):
    if apart:
        here, refs = refs[0][0], refs[1:]
    lefts, refs = refs[: len(shape)], refs[len(shape) :]
    outs = refs[sum(shape) : sum(shape) + 1 + apart]
    weights, semaphores = refs[sum(shape) + 1 + apart : -1], refs[-1]
    step = pl.program_id(0)
    at, groups = 0, []
    for count, weight, column in zip(shape, weights, columns):
        groups.append(
            copies_into(refs[at : at + count], weight, semaphores, at, column, deep)
        )
        at += count
    for stripe in range(STRIPES):
        start_all(
            step,
            [
                copy
                for group in groups
                for copy in group[stripe * len(group) // STRIPES : (stripe + 1) * len(group) // STRIPES]
            ],
        )
    for stripe in range(STRIPES):
        for group in groups:
            wait_at(
                step,
                stripe,
                group[stripe * len(group) // STRIPES : (stripe + 1) * len(group) // STRIPES],
            )
    tall = weights[0].shape[0] // STRIPES
    span = pl.ds(pl.multiple_of(step * tall, tall), tall)
    total = None
    for left, weight in zip(lefts, weights):
        term = product(left[...], weight[span, :], 1, 1)
        total = term if total is None else total + term
    if not apart:
        outs[0][...] = total.astype(BF16)
        return
    rows = total.shape[0] // 4
    for i in range(4):
        away = jnp.bitwise_xor(here, i)
        span = pl.ds(pl.multiple_of((1 - away // 2) * rows, rows), rows)
        values = total[i * rows : (i + 1) * rows].astype(BF16)
        for other, out_ref in enumerate(outs):

            @pl.when(away % 2 == other)
            def _():
                out_ref[span, :] = values


def outward(parts, depth, name, place=None):
    lefts = [left for left, _, _ in parts]
    length = lefts[0].shape[0]
    shape = [len(blocks) for _, blocks, _ in parts]
    tall = (0,) if place is None else (0, 1)
    deep = None
    columns = []
    for left, blocks, column in parts:
        if column is None:
            columns.append(None)
        else:
            columns.append(pl.ds(column, left.shape[1]))
            deep = depth // len(blocks)
    return kernel_call(
        functools.partial(outward_body, shape, columns, deep, place is not None),
        name,
        [*lefts, *(block for _, blocks, _ in parts for block in blocks)],
        [whole(left.shape) for left in lefts] + [HBM] * sum(shape),
        [pl.BlockSpec((length // len(tall), depth // STRIPES), lambda i, *_: (0, i)) for _ in tall],
        [shaped((length // len(tall), depth)) for _ in tall],
        scalars=() if place is None else (place,),
        grid=(STRIPES,),
        flops=10**9,
        scratch=[pltpu.VMEM((depth, left.shape[1]), BF16) for left in lefts]
        + [pltpu.SemaphoreType.DMA((sum(shape),))],
        vmem=60,
    )


def mixed_grad_body(count, rows_ref, *refs):
    blocks = refs[:count]
    out_ref, weight, semaphores = refs[count:]
    step = pl.program_id(0)
    wide = weight.shape[1]
    copies = copies_into(blocks, weight, semaphores, 0, pl.ds(wide, wide), weight.shape[0] // count)
    start_all(step, copies)
    wait_at(step, 0, copies)
    out_ref[...] = product(rows_ref[...], weight[...], 1, 0).astype(BF16)


def through_out(branch, blocks):
    length, depth = branch.shape
    rows = length // 4
    wide = blocks[0].shape[1] // 2
    count = len(blocks)
    return kernel_call(
        functools.partial(mixed_grad_body, count),
        "through_out",
        [branch, *blocks],
        [pl.BlockSpec((rows, depth), lambda i: (i, 0))] + [HBM] * count,
        pl.BlockSpec((rows, wide), lambda i: (i, 0)),
        shaped((length, wide)),
        grid=(4,),
        flops=10**9,
        scratch=[pltpu.VMEM((depth, wide), BF16), pltpu.SemaphoreType.DMA((count,))],
        vmem=60,
    )


def heads_body(count, q_ref, k_ref, v_ref, x_ref, mean_ref, inverse_ref, *refs):
    blocks_a, blocks_b = refs[:count], refs[count : 2 * count]
    out_ref, sums_ref, weight_a, weight_v, semaphores = refs[2 * count :]
    step = pl.program_id(0)
    wide = q_ref.shape[1]
    deep = weight_a.shape[0] // count
    copies_a = copies_into(blocks_a, weight_a, semaphores, 0, rows=deep)
    copies_v = copies_into(blocks_b, weight_v, semaphores, count, pl.ds(0, wide), deep)
    start_all(step, [copy for pair in zip(copies_a, copies_v) for copy in pair])
    for stripe in range(STRIPES):
        span = slice(stripe * count // STRIPES, (stripe + 1) * count // STRIPES)
        wait_at(step, stripe, copies_a[span] + copies_v[span])
    tall = weight_a.shape[0] // STRIPES
    span = pl.ds(pl.multiple_of(step * tall, tall), tall)
    total = product(q_ref[...], weight_a[span, :wide], 1, 1)
    total = total + product(k_ref[...], weight_a[span, wide:], 1, 1)
    total = total + product(v_ref[...], weight_v[span, :], 1, 1)
    out_ref[...] = total.astype(BF16)
    standard = (x_ref[...].astype(F32) - mean_ref[...]) * inverse_ref[...]
    sums_ref[0:1, :] = (total * standard).sum(0, keepdims=True)
    sums_ref[1:2, :] = total.sum(0, keepdims=True)


def through_heads(grads, inputs, mean, inverse, blocks_a, blocks_b):
    length, wide = grads[0].shape
    depth = inputs.shape[1]
    count = len(blocks_a)
    striped = lambda tall: pl.BlockSpec((tall, depth // STRIPES), lambda i: (0, i))
    return kernel_call(
        functools.partial(heads_body, count),
        "through_heads",
        [*grads, inputs, mean, inverse, *blocks_a, *blocks_b],
        [whole((length, wide))] * 3
        + [striped(length), whole((length, 1)), whole((length, 1))]
        + [HBM] * (2 * count),
        [striped(length), striped(2)],
        [shaped((length, depth)), shaped((2, depth), F32)],
        grid=(STRIPES,),
        flops=10**9,
        scratch=[
            pltpu.VMEM((depth, 2 * wide), BF16),
            pltpu.VMEM((depth, wide), BF16),
            pltpu.SemaphoreType.DMA((2 * count,)),
        ],
        vmem=60,
    )


def over_tokens_body(count, *refs):
    out_ref = refs[-1]
    first = 0
    for i in range(count):
        left, right = refs[2 * i], refs[2 * i + 1]
        wide = right.shape[1]
        out_ref[:, first : first + wide] = product(left[...], right[...], 0, 0).astype(BF16)
        first += wide


def over_tokens(groups, flops=10**9):
    length, depth = groups[0][0].shape
    wide = sum(right.shape[1] for _, right in groups)
    block = depth // STRIPES
    return kernel_call(
        functools.partial(over_tokens_body, len(groups)),
        "over_tokens",
        [values for group in groups for values in group],
        [
            spec
            for _, right in groups
            for spec in (pl.BlockSpec((length, block), lambda i: (0, i)), whole(right.shape))
        ],
        pl.BlockSpec((block, wide), lambda i: (i, 0)),
        shaped((depth, wide)),
        grid=(STRIPES,),
        flops=flops,
        vmem=60,
    )


def added(refs):
    total = refs[0][...].astype(F32)
    for ref in refs[1:]:
        total = total + ref[...].astype(F32)
    return total


def meet_body(own_ref, arrived_ref, far_ref, near_ref):
    rows = far_ref.shape[0]
    total = own_ref[...].astype(F32) + arrived_ref[...].astype(F32)
    far_ref[...] = total[:rows].astype(BF16)
    near_ref[...] = total[rows:]


def meet(own, arrived):
    length, depth = own.shape
    half = (length // 2, depth)
    return kernel_call(
        meet_body,
        "meet",
        [own, arrived],
        [whole(own.shape)] * 2,
        [whole(half)] * 2,
        [shaped(half), shaped(half, F32)],
        grid=(1,),
    )


def second_norm_body(x_ref, term_ref, norm_ref, middle_ref, mean_ref, inverse_ref, out_ref):
    middle = added([x_ref, term_ref])
    middle_ref[...] = middle
    mean = jnp.mean(middle, axis=-1, keepdims=True)
    centred = middle - mean
    inverse = lax.rsqrt(jnp.mean(centred * centred, axis=-1, keepdims=True) + EPSILON)
    mean_ref[...] = mean
    inverse_ref[...] = inverse
    out_ref[...] = (centred * inverse * norm_ref[2:3, :] + norm_ref[3:4, :]).astype(BF16)


def second_norm(inputs, terms, norm_rows):
    shape = inputs.shape
    column = (shape[0], 1)
    return kernel_call(
        second_norm_body,
        "second_norm",
        [inputs, *terms, norm_rows],
        [whole(shape)] * 2 + [whole(norm_rows.shape)],
        [whole(shape), whole(column), whole(column), whole(shape)],
        [shaped(shape, F32), shaped(column, F32), shaped(column, F32), shaped(shape)],
        grid=(1,),
    )


def norm_gradient(upstream, standard, inverse, gain):
    scaled = upstream * gain
    inner = (
        scaled
        - jnp.mean(scaled, axis=-1, keepdims=True)
        - standard * jnp.mean(scaled * standard, axis=-1, keepdims=True)
    )
    return inverse * inner


def second_back_body(near_ref, far_ref, middle_ref, mean_ref, inverse_ref, norm_ref, grad_ref, full_ref, branch_ref, sums_ref):
    upstream = added([near_ref, far_ref])
    inverse = inverse_ref[...]
    standard = (middle_ref[...] - mean_ref[...]) * inverse
    sums_ref[0:1, :] = (upstream * standard).sum(0, keepdims=True)
    sums_ref[1:2, :] = upstream.sum(0, keepdims=True)
    grad = grad_ref[...].astype(F32) + norm_gradient(upstream, standard, inverse, norm_ref[2:3, :])
    full_ref[...] = grad
    branch_ref[...] = grad.astype(BF16)


def second_norm_back(terms, middle, mean, inverse, norm_rows, grads):
    shape = middle.shape
    column = (shape[0], 1)
    return kernel_call(
        second_back_body,
        "second_norm_back",
        [*terms, middle, mean, inverse, norm_rows, grads],
        [whole(shape)] * 3 + [whole(column)] * 2 + [whole(norm_rows.shape), whole(shape)],
        [whole(shape), whole(shape), whole((2, shape[1]))],
        [shaped(shape, F32), shaped(shape), shaped((2, shape[1]), F32)],
        grid=(1,),
    )


def input_back_body(order_ref, upstream_ref, x_ref, norm_ref, grad_ref, out_ref):
    values = x_ref[...].astype(F32)
    centred = values - jnp.mean(values, axis=-1, keepdims=True)
    inverse = lax.rsqrt(jnp.mean(centred * centred, axis=-1, keepdims=True) + EPSILON)
    upstream = upstream_ref[...].astype(F32)
    grad = grad_ref[...] + norm_gradient(upstream, centred * inverse, inverse, norm_ref[0:1, :])
    put_back(order_ref, out_ref, grad)


def input_back(order, upstream, inputs, norm_rows, grads):
    shape = inputs.shape
    out = kernel_call(
        input_back_body,
        "input_back",
        [upstream, inputs, norm_rows, grads],
        [whole(shape)] * 2 + [whole(norm_rows.shape), whole(shape)],
        whole(shape),
        shaped(shape),
        grid=(1,),
        scalars=[order],
    )
    return back_in_place(order, out)


def result_body(order_ref, middle_ref, term_ref, out_ref):
    put_back(order_ref, out_ref, added([middle_ref, term_ref]))


def finish_result(order, middle, term):
    shape = middle.shape
    out = kernel_call(
        result_body,
        "finish_result",
        [middle, term],
        [whole(shape)] * 2,
        whole(shape),
        shaped(shape),
        grid=(1,),
        scalars=[order],
    )
    return back_in_place(order, out)


def hand_on_body(arrivals, sides, *refs):
    arrived, own, outs = refs[:arrivals], refs[arrivals : -sides], refs[-sides:]
    parts = len(own) // sides
    for side in range(sides):
        first = 0
        for part in own[side * parts : (side + 1) * parts]:
            span = slice(first, first + part.shape[1])
            values = part[...]
            if arrivals:
                values = (values.astype(F32) + arrived[side][:, span].astype(F32)).astype(BF16)
            outs[side][:, span] = values
            first += part.shape[1]


def hand_on(arrived, own, rows, places):
    shape = (rows, sum(part.shape[1] for part in own))
    sides = len(places)
    half = (rows // 2, shape[1])
    by_halves = pl.BlockSpec(half, lambda i: (i, 0))
    return kernel_call(
        functools.partial(hand_on_body, len(arrived), sides),
        "hand_on",
        [*arrived, *(part for _ in places for part in own)],
        [by_halves] * len(arrived)
        + [
            pl.BlockSpec((rows // 2, part.shape[1]), lambda i, at=at: (2 * at + i, 0))
            for at in places
            for part in own
        ],
        [by_halves] * sides,
        [shaped(shape)] * sides,
        grid=(2,),
        vmem=60,
    )


class Route:
    def __init__(self, count):
        self.count = count
        self.reach = count // 2
        self.ring = list(range(0, count, 2)) + list(range(count - 1, 0, -2))
        ahead = [(self.ring[i], self.ring[(i + 1) % count]) for i in range(count)]
        self.pairs = (ahead, [(b, a) for a, b in ahead])

    def send(self, values, direction):
        return lax.ppermute(values, "dp", self.pairs[direction])


class Gathering:
    def __init__(self, route, block, longer):
        self.route = route
        self.blocks = {0: block}
        self.steps = 0
        self.hops = [route.reach - (direction != longer) for direction in range(2)]
        self.done = 0
        self.flying = [block]

    def pending(self):
        return self.flying

    def resume(self, arrived):
        route = self.route
        if self.done == 0:
            self.blocks[0] = arrived[0]
            latest = [arrived[0], arrived[0]]
        else:
            arrived = list(arrived)
            latest = [None, None]
            for direction in range(2):
                if self.done <= self.hops[direction]:
                    latest[direction] = arrived.pop(0)
                    at = route.count - self.done if direction == 0 else self.done
                    self.blocks[at] = latest[direction]
        self.done += 1
        self.flying = [
            route.send(latest[direction], direction)
            for direction in range(2)
            if self.done <= self.hops[direction]
        ]

    def all(self):
        return [self.blocks[j] for j in range(self.route.count)]


class Summing:
    def __init__(self, route, own, rows, per, offset, longer):
        self.route = route
        self.own = own
        self.rows = rows
        self.place = lambda j: per * j + offset
        self.hops = [route.reach - (direction != longer) for direction in range(2)]
        self.steps = 0
        self.done = 0
        self.flying = None
        self.last = [None, None]

    def terms(self, arrived, directions):
        places = []
        for direction in directions:
            left = self.hops[direction] - self.done
            at = left if direction == 0 else (self.route.count - left) % self.route.count
            places.append(self.place(at))
        return hand_on(arrived, self.own(), self.rows, places)

    def pending(self):
        return self.flying if self.done else self.terms([], range(2))

    def resume(self, arrived):
        arrived = list(arrived)
        onward = range(2)
        if self.done:
            landed = [direction for direction in range(2) if self.done <= self.hops[direction]]
            onward = [direction for direction in landed if self.done < self.hops[direction]]
            by_way = dict(zip(landed, arrived))
            for direction in landed:
                if self.done == self.hops[direction]:
                    self.last[direction] = by_way[direction]
            if onward:
                arrived = self.terms([by_way[direction] for direction in onward], onward)
        self.done += 1
        self.flying = [self.route.send(values, way) for way, values in zip(onward, arrived)]

    def total(self, part, first):
        at = self.place(0) * self.rows
        own = part[at : at + self.rows].astype(F32)
        span = slice(first, first + part.shape[1])
        return own + self.last[0][:, span].astype(F32) + self.last[1][:, span].astype(F32)


STEPS = 5


class Pace:
    def __init__(self, token):
        self.token = token

    def __call__(self, streams, *carried, busy=False, long=False):
        last = {}
        for stream in streams:
            stream.steps += 1
            last[stream] = (stream.steps * (stream.route.reach + 1)) // STEPS
        first = True
        while first or any(stream.done < last[stream] for stream in streams):
            first = False
            moving = [stream for stream in streams if stream.done < last[stream]]
            waiting = [list(stream.pending()) for stream in moving]
            flat = [values for group in waiting for values in group]
            self.token, *out = lax.optimization_barrier((self.token, *flat, *carried))
            carried = out[len(flat) :]
            at = 0
            for stream, group in zip(moving, waiting):
                stream.resume(out[at : at + len(group)])
                at += len(group)
        if not busy:
            self.token = mark(self.token, 10**12 if long else 10**9)
            self.token, *carried = lax.optimization_barrier((self.token, *carried))
        return carried[0] if len(carried) == 1 else carried


def across_core(values):
    return lax.ppermute(values, "tensor", [(i, i ^ 1) for i in range(4)])


def across_chip(values):
    return lax.ppermute(values, "tensor", [(i, i ^ 2) for i in range(4)])


def halve(route, table):
    left = table.shape[0] // 2
    pairs = [(route.ring[i], route.ring[(i + left) % route.count]) for i in range(route.count)]
    return lax.ppermute(table[left:], "dp", pairs)


def on_device(
    route,
    activations,
    cotangent,
    segments,
    norm_one_gain,
    norm_one_bias,
    w_query,
    w_key,
    w_value,
    qkv_bias,
    w_out,
    norm_two_gain,
    norm_two_bias,
    w_gate,
    w_up,
    w_down,
):
    count = route.count
    third, depth = activations.shape
    length = segments.shape[0]
    width = depth // count
    part = width // 2
    heads_wide = w_query.shape[1]
    local_heads = heads_wide // HD
    shards = length // third
    here = lax.axis_index("tensor")
    place = here.astype(jnp.int32).reshape(1)
    advance = Pace(jnp.zeros((8, 128), jnp.int32) + here)
    device = lax.axis_index("dp").astype(jnp.int32)
    position = jnp.where(device % 2 == 0, device // 2, count - 1 - device // 2)
    ahead = (position + jnp.arange(count, dtype=jnp.int32)) % count
    order = jnp.where(ahead < count // 2, 2 * ahead, 2 * (count - 1 - ahead) + 1)

    def gather(values):
        return lax.all_gather(values, "tensor", axis=0, tiled=True)

    def scatter(values):
        return lax.psum_scatter(values, "tensor", scatter_dimension=0, tiled=True)

    def relative(values):
        def pick(entries):
            return jnp.concatenate([values[i : i + 1] for i in entries], axis=0)

        values = jnp.where(here % 2 == 1, pick((1, 0, 3, 2)), values)
        return jnp.where(here >= 2, pick((2, 3, 0, 1)), values)

    bias_size = qkv_bias.size
    norm_part = norm_one_gain.shape[0]
    ring_qk = Gathering(route, jnp.concatenate([w_query, w_key], axis=1), 0)
    ring_vo = Gathering(route, None, 1)
    ring_gate = Gathering(route, w_gate, 0)
    ring_up = Gathering(route, w_up, 1)
    ring_down = [Gathering(route, None, 0), Gathering(route, None, 1)]

    packed = jnp.stack([norm_one_gain, norm_one_bias, norm_two_gain, norm_two_bias])
    packed_core = across_core(packed)
    own_bf16 = reorder(order, activations)
    x_all = gather(own_bf16)
    packed = jnp.concatenate([packed, packed_core], axis=0)
    packed, w_down, w_value, w_out, cotangent = advance(
        [], packed, w_down, w_value, w_out, cotangent
    )
    packed_chip = across_chip(packed)
    weight_vo = jnp.concatenate([w_value, w_out.T], axis=1)
    packed_chip, weight_vo, cotangent, w_down = advance(
        [], packed_chip, weight_vo, cotangent, w_down
    )
    packed = jnp.concatenate([packed, packed_chip], axis=0).reshape(shards, 4, norm_part)
    packed = relative(packed).transpose(1, 0, 2).reshape(4, width)
    wide = 2 * heads_wide
    packed = jnp.concatenate(
        [
            jnp.pad(packed, ((0, 0), (0, wide - width))),
            jnp.pad(qkv_bias.reshape(1, bias_size), ((0, 11), (0, wide - bias_size))),
        ],
        axis=0,
    )
    ring_vo.flying = [jnp.concatenate([weight_vo, packed], axis=0)]
    cotangent, w_down = advance([ring_qk, ring_vo], cotangent, w_down, long=True)
    own_grad = reorder(order, cotangent)
    own_grad, w_down = advance([ring_qk], own_grad, w_down)
    down_rows = w_down.T
    ring_down[0].flying = [down_rows[:part]]
    ring_down[1].flying = [down_rows[part:]]
    x_all, own_grad = advance([ring_vo], x_all, own_grad)
    grad_all = gather(own_grad)
    mean_one, inverse_one = row_stats(x_all)
    mean_one, inverse_one, segments = advance([ring_qk], mean_one, inverse_one, segments)
    segment_down, segment_across = segments[:, None], segments[None, :]
    begins = jnp.sum((segment_across < segment_down).astype(F32), axis=1, keepdims=True)
    places = jnp.arange(length, dtype=jnp.int32)[:, None].astype(F32)
    lanes = jnp.arange(PAIR, dtype=jnp.int32) % HD
    frequency = 10000.0 ** (-2.0 * (lanes % (ROT // 2)).astype(F32) / ROT)
    angles = (places - begins) * frequency[None, :]
    cos_table = jnp.where(lanes < ROT, jnp.cos(angles), 1.0)
    sin_table = jnp.where(
        lanes < ROT, jnp.where(lanes < ROT // 2, -1.0, 1.0) * jnp.sin(angles), 0.0
    )
    cos_table, sin_table, segment_down, segment_across = advance(
        [ring_vo], cos_table, sin_table, segment_down, segment_across
    )
    advance([ring_qk], long=True)
    grad_all = advance([ring_vo], grad_all)
    advance([ring_qk, ring_gate])
    advance([ring_vo, ring_up], busy=True)
    blocks_a = ring_qk.all()
    blocks_b = ring_vo.all()
    norm_rows, bias_row = decode(order, blocks_b, depth, 3 * heads_wide)
    qk, values, normed = project_qkv(
        x_all, mean_one, inverse_one, norm_rows, bias_row, cos_table, sin_table, blocks_a, blocks_b
    )
    qk, values = advance([ring_gate], qk, values, busy=True)
    mixed, lse = attend_forward(qk, values, segment_down, segment_across, 2)
    mixed, lse = advance([ring_up], mixed, lse, busy=True)
    arriving = scatter(outward([(mixed, blocks_b, heads_wide)], depth, "from_heads")[0])
    advance([ring_gate])
    advance([ring_up], long=True)
    arriving = advance([ring_gate], arriving)
    middle, mean_two, inverse_two, n_own = second_norm(own_bf16, [arriving], norm_rows)
    normed_two = gather(n_own)
    middle = advance([], middle, long=True)
    advance([ring_up, ring_down[0]])
    advance([ring_gate])
    advance([ring_up, ring_down[1]])
    advance([ring_down[0]])
    normed_two = advance([ring_down[1]], normed_two, busy=True)
    gate_blocks = ring_gate.all()
    up_blocks = ring_up.all()
    kept = gated_forward(normed_two, gate_blocks, up_blocks, 0, None)
    kept = advance([ring_down[0]], *kept)
    kept = advance([ring_down[1]], *kept, busy=True)
    gate, up, hidden = gated_forward(normed_two, gate_blocks, up_blocks, 1, kept)
    gate, up, hidden = advance([ring_down[0]], gate, up, hidden)
    hidden = advance([ring_down[1]], hidden)
    down_sum = product(grad_all, hidden, 0, 0).astype(BF16)
    sum_down = Summing(route, lambda: [down_sum], width, 1, 0, 0)
    down_sum = advance([ring_down[0]], down_sum)
    advance([ring_down[1], sum_down], busy=True)
    down_blocks = [block for pair in zip(*(ring.all() for ring in ring_down)) for block in pair]

    gate_grad, up_grad = gated_backward(grad_all, gate, up, down_blocks)
    gate_grad, up_grad = advance([sum_down], gate_grad, up_grad)
    gate_sum = product(normed_two, gate_grad, 0, 0).astype(BF16)
    sum_gate = Summing(route, lambda: [gate_sum], width, 1, 0, 1)
    gate_sum, gate_grad, up_grad = advance([sum_gate], gate_sum, gate_grad, up_grad, busy=True)
    own, cross = outward(
        [(gate_grad, gate_blocks, None), (up_grad, up_blocks, None)], depth, "from_gates", place
    )
    own, cross = advance([sum_down], own, cross)
    own, cross, up_grad = advance([sum_gate], own, cross, up_grad, busy=True)
    arrived = across_core(cross)
    own, arrived, up_grad = advance([], own, arrived, up_grad, busy=True)
    far, near = meet(own, arrived)
    arriving = across_chip(far)
    near, up_grad = advance([], near, up_grad)
    up_sum = product(normed_two, up_grad, 0, 0).astype(BF16)
    sum_up = Summing(route, lambda: [up_sum], width, 1, 0, 0)
    up_sum = advance([sum_down], up_sum)
    arriving = advance([sum_gate], arriving)
    middle_grad, b_own, two_sums = second_norm_back(
        [near, arriving], middle, mean_two, inverse_two, norm_rows, own_grad
    )
    branch = gather(b_own)
    hidden, middle_grad = advance([], hidden, middle_grad, long=True)
    (result_terms,) = outward([(hidden, down_blocks, None)], depth, "from_hidden")
    result_terms = advance([sum_down, sum_up], result_terms)
    advance([sum_gate])
    branch, result_terms = advance([sum_up], branch, result_terms, busy=True)
    arriving_result = scatter(result_terms)
    mixed_grad = through_out(branch, blocks_b)
    mixed_grad, branch = advance([sum_gate], mixed_grad, branch, busy=True)
    grads = None
    for half in range(2):
        grads = attend_backward(
            qk,
            values,
            mixed,
            mixed_grad,
            lse,
            segment_down,
            segment_across,
            cos_table,
            sin_table,
            2,
            half,
            grads,
        )
        grads = advance([sum_up], *grads, busy=True)
    q_grad, k_grad, v_grad, bias_sums = grads
    qk_sum = over_tokens([(normed, q_grad), (normed, k_grad)])
    sum_qk = Summing(route, lambda: [qk_sum], width, 1, 0, 1)
    qk_sum, v_grad, branch = advance([sum_qk], qk_sum, v_grad, branch, busy=True)
    vo_sum = over_tokens([(normed, v_grad), (branch, mixed)])
    sum_vo = Summing(route, lambda: [vo_sum], width, 1, 0, 0)
    vo_sum = advance([sum_up], vo_sum)
    vo_sum, q_grad, arriving_result = advance(
        [sum_qk, sum_vo], vo_sum, q_grad, arriving_result, busy=True
    )
    heads_terms, one_sums = through_heads(
        [q_grad, k_grad, v_grad], x_all, mean_one, inverse_one, blocks_a, blocks_b
    )
    arriving = scatter(heads_terms)
    one_sums, middle, arriving_result, down_sum = advance(
        [sum_vo], one_sums, middle, arriving_result, down_sum, long=True
    )
    norm_grads = jnp.concatenate([one_sums, two_sums], axis=0)
    bias_sums = bias_sums.transpose(1, 0, 2).reshape(3, local_heads, count, HD // count)
    bias_sums = bias_sums.transpose(2, 0, 1, 3).reshape(count, bias_size)[order]
    extras = jnp.concatenate(
        [norm_grads.reshape(4, count, width).transpose(1, 0, 2).reshape(count, 4 * width), bias_sums],
        axis=1,
    )
    extras = jnp.pad(extras, ((0, 0), (0, -extras.shape[1] % 128)))
    result = finish_result(order, middle, arriving_result)
    moved = halve(route, extras)
    extras, moved, result, down_sum, gate_sum = advance(
        [sum_qk], extras, moved, result, down_sum, gate_sum
    )
    grad_down = sum_down.total(down_sum, 0).T
    extras = extras[: moved.shape[0]] + moved
    moved = halve(route, extras)
    extras, moved, grad_down, gate_sum = advance([sum_vo], extras, moved, grad_down, gate_sum)
    grad_gate = sum_gate.total(gate_sum, 0)
    extras = extras[: moved.shape[0]] + moved
    while extras.shape[0] > 2:
        extras = extras[: extras.shape[0] // 2] + halve(route, extras)
    moved = halve(route, extras)
    extras, moved, grad_gate, up_sum = advance([sum_qk], extras, moved, grad_gate, up_sum)
    grad_up = sum_up.total(up_sum, 0)
    extras = (extras[:1] + moved)[0]
    bias_grad = extras[4 * width : 4 * width + bias_size].reshape(qkv_bias.shape)
    norm_sums = extras[: 4 * width].reshape(4, width)
    moved = across_core(norm_sums)
    grad_up, moved = advance([sum_vo], grad_up, moved)
    norm_sums = norm_sums + moved
    moved = across_chip(norm_sums)
    moved = advance([sum_qk], moved)
    norm_sums = norm_sums + moved
    norm_sums = lax.dynamic_slice_in_dim(norm_sums, here * norm_part, norm_part, axis=1)
    arriving = advance([], arriving)
    input_grad = input_back(order, arriving, own_bf16, norm_rows, middle_grad)
    input_grad, norm_sums = advance([sum_vo], input_grad, norm_sums)

    q_k = sum_qk.total(qk_sum, 0)
    v_o = sum_vo.total(vo_sum, 0)
    return (
        result,
        input_grad,
        norm_sums[0],
        norm_sums[1],
        q_k[:, :heads_wide],
        q_k[:, heads_wide:],
        v_o[:, :heads_wide],
        bias_grad,
        v_o[:, heads_wide:].T,
        norm_sums[2],
        norm_sums[3],
        grad_gate,
        grad_up,
        grad_down,
    )


def solution(mesh):
    both = P(("dp", "tensor"))
    tokens = P(("dp", "tensor"), None)
    rows = P("dp", "tensor")
    columns = P("tensor", "dp")
    biases = P(None, "tensor", "dp")
    return jax.shard_map(
        functools.partial(on_device, Route(mesh.shape["dp"])),
        mesh=mesh,
        in_specs=(
            tokens,
            tokens,
            P("dp"),
            both,
            both,
            rows,
            rows,
            rows,
            biases,
            columns,
            both,
            both,
            rows,
            rows,
            columns,
        ),
        out_specs=(
            tokens,
            tokens,
            both,
            both,
            rows,
            rows,
            rows,
            biases,
            columns,
            both,
            both,
            rows,
            rows,
            columns,
        ),
        check_vma=False,
    )
```

```python
import functools

import jax
import jax.experimental.pallas as pl
import jax.experimental.pallas.tpu as pltpu
import jax.numpy as jnp
from jax import lax
from jax.sharding import PartitionSpec as P

HD = 64
ROT = 16
PAIR = 2 * HD
EPSILON = 1e-05
NEGATIVE = -1e30
F32 = jnp.float32
BF16 = jnp.bfloat16
MIB = 2**20
LIGHT = pl.CostEstimate(flops=10**9, bytes_accessed=1, transcendentals=1)
LONG = pl.CostEstimate(flops=10**12, bytes_accessed=1, transcendentals=1)


def product(left, right, left_dim, right_dim):
    return lax.dot_general(
        left, right, (((left_dim,), (right_dim,)), ((), ())), preferred_element_type=F32
    )


def turn(columns, cos_values, sin_values, opening):
    partner = jnp.where(opening, pltpu.roll(columns, PAIR - 8, 1), pltpu.roll(columns, 8, 1))
    return columns * cos_values + partner * sin_values


def opening_lanes(rows):
    return lax.broadcasted_iota(jnp.int32, (rows, PAIR), 1) % HD < 8


def forward_body(block, count, q_ref, k_ref, v_ref, down_ref, across_ref, mixed_ref, lse_ref):
    lane = lax.broadcasted_iota(jnp.int32, (block, PAIR), 1)
    earlier = lax.broadcasted_iota(jnp.int32, (block, block), 1) <= lax.broadcasted_iota(
        jnp.int32, (block, block), 0
    )
    spans = [pl.ds(i * block, block) for i in range(count)]
    for i in range(count):
        queries = q_ref[spans[i], :] * jnp.asarray(HD**-0.5, BF16)
        segment = down_ref[spans[i], :]
        kept = [across_ref[:, spans[j]] == segment for j in range(i + 1)]
        kept[i] = kept[i] & earlier
        sums = []
        for half in range(2):
            mine = lane < HD if half == 0 else lane >= HD
            chosen = jnp.where(mine, queries, jnp.zeros_like(queries))
            scores = [
                jnp.where(kept[j], product(chosen, k_ref[spans[j], :], 1, 1), NEGATIVE)
                for j in range(i + 1)
            ]
            tops = scores[0]
            for part in scores[1:]:
                tops = jnp.maximum(tops, part)
            top = tops.max(1, keepdims=True)
            out = None
            for j in range(i + 1):
                values = v_ref[spans[j], :]
                beside = jnp.where(mine, values, jnp.ones_like(values))
                term = product(jnp.exp(scores[j] - top).astype(BF16), beside, 1, 0)
                out = term if out is None else out + term
            other = slice(HD, HD + 1) if half == 0 else slice(0, 1)
            total = out[:, other]
            sums.append(out * (1.0 / total))
            lse = jnp.broadcast_to(top + jnp.log(total), (block, PAIR))
            lse_ref[0, half : half + 1, spans[i]] = lse.T[0:1, :]
        mixed_ref[spans[i], :] = jnp.where(lane < HD, sums[0], sums[1]).astype(BF16)


def attend_forward(qk, values, segment_down, segment_across, count):
    length, width = values.shape
    pairs = width // PAIR
    columns = lambda first: pl.BlockSpec((length, PAIR), lambda h: (0, h + first))
    whole = lambda shape: pl.BlockSpec(shape, lambda h: (0, 0))
    return pl.pallas_call(
        functools.partial(forward_body, length // count, count),
        grid_spec=pltpu.PrefetchScalarGridSpec(
            num_scalar_prefetch=0,
            grid=(pairs,),
            in_specs=[columns(0), columns(pairs), columns(0), whole((length, 1)), whole((1, length))],
            out_specs=[columns(0), pl.BlockSpec((1, 2, length), lambda h: (h, 0, 0))],
        ),
        out_shape=[
            jax.ShapeDtypeStruct((length, width), BF16),
            jax.ShapeDtypeStruct((pairs, 2, length), F32),
        ],
        compiler_params=pltpu.CompilerParams(vmem_limit_bytes=60 * MIB),
        cost_estimate=LIGHT,
        name="attend_forward",
    )(qk, qk, values, segment_down, segment_across)


def backward_body(
    block,
    count,
    kept,
    q_ref,
    k_ref,
    v_ref,
    mixed_ref,
    grad_ref,
    lse_ref,
    down_ref,
    across_ref,
    cos_ref,
    sin_ref,
    *refs,
):
    q_grad_ref, k_grad_ref, v_grad_ref, bias_ref, q_total, k_total, v_total = refs[kept:]
    lane = lax.broadcasted_iota(jnp.int32, (block, PAIR), 1)
    earlier = lax.broadcasted_iota(jnp.int32, (block, block), 0) <= lax.broadcasted_iota(
        jnp.int32, (block, block), 1
    )
    spans = [pl.ds(i * block, block) for i in range(count)]
    turned = [k_ref[span, :].T for span in spans]
    for i in range(count):
        queries = q_ref[spans[i], :] * jnp.asarray(HD**-0.5, BF16)
        upstream = grad_ref[spans[i], :]
        centres = (upstream.astype(F32) * mixed_ref[spans[i], :].astype(F32)).T
        segment = across_ref[:, spans[i]]
        allowed = [down_ref[spans[j], :] == segment for j in range(i + 1)]
        allowed[i] = allowed[i] & earlier
        sums = []
        for half in range(2):
            mine = lane < HD if half == 0 else lane >= HD
            nothing = jnp.zeros_like(queries)
            chosen = jnp.where(mine, queries, nothing)
            chosen_grad = jnp.where(mine, upstream, nothing)
            log_total = lse_ref[0, half : half + 1, spans[i]]
            centre = centres[half * HD : (half + 1) * HD, :].sum(0, keepdims=True)
            q_sum = None
            for j in range(i + 1):
                keys = k_ref[spans[j], :]
                scores = jnp.where(allowed[j], product(keys, chosen, 1, 1), NEGATIVE)
                weights = jnp.exp(scores - log_total)
                weight_grad = product(v_ref[spans[j], :], chosen_grad, 1, 1)
                score_grad = (weights * (weight_grad - centre)).astype(BF16)
                v_term = product(weights.astype(BF16), chosen_grad, 1, 0)
                k_term = product(score_grad, chosen, 1, 0)
                term = product(turned[j], score_grad, 1, 0)
                q_sum = term if q_sum is None else q_sum + term
                if i == j and half == 0:
                    v_total[spans[j], :] = v_term
                    k_total[spans[j], :] = k_term
                else:
                    v_total[spans[j], :] += v_term
                    k_total[spans[j], :] += k_term
            sums.append(q_sum[half * HD : (half + 1) * HD, :])
        q_total[spans[i], :] = jnp.concatenate(sums, axis=0).T
    opening = opening_lanes(block * count)
    cos_values = cos_ref[...]
    sin_values = -sin_ref[...]
    q_grad = turn(q_total[...] * (HD**-0.5), cos_values, sin_values, opening).astype(BF16)
    k_grad = turn(k_total[...], cos_values, sin_values, opening).astype(BF16)
    v_grad = v_total[...].astype(BF16)
    for at, (ref, grad) in enumerate(
        ((q_grad_ref, q_grad), (k_grad_ref, k_grad), (v_grad_ref, v_grad))
    ):
        ref[...] = grad
        bias_ref[0, at : at + 1, :] = grad.astype(F32).sum(0, keepdims=True)


def attend_backward(
    qk, values, mixed, mixed_grad, lse, segment_down, segment_across, cos_table, sin_table, count, half, kept
):
    length, width = values.shape
    pairs = width // PAIR
    kept = list(kept or [])
    some = pairs // 2
    start = half * some
    columns = lambda first: pl.BlockSpec((length, PAIR), lambda h: (0, h + first + start))
    whole = lambda shape: pl.BlockSpec(shape, lambda h: (0, 0))
    return pl.pallas_call(
        functools.partial(backward_body, length // count, count, len(kept)),
        grid_spec=pltpu.PrefetchScalarGridSpec(
            num_scalar_prefetch=0,
            grid=(some,),
            in_specs=[
                columns(0),
                columns(pairs),
                columns(0),
                columns(0),
                columns(0),
                pl.BlockSpec((1, 2, length), lambda h: (h + start, 0, 0)),
                whole((length, 1)),
                whole((1, length)),
                whole((length, PAIR)),
                whole((length, PAIR)),
            ]
            + [pl.BlockSpec(memory_space=pl.ANY)] * len(kept),
            out_specs=[
                columns(0),
                columns(0),
                columns(0),
                pl.BlockSpec((1, 3, PAIR), lambda h: (h + start, 0, 0)),
            ],
            scratch_shapes=[pltpu.VMEM((length, PAIR), F32)] * 3,
        ),
        out_shape=[jax.ShapeDtypeStruct((length, width), BF16)] * 3
        + [jax.ShapeDtypeStruct((pairs, 3, PAIR), F32)],
        input_output_aliases={10 + i: i for i in range(len(kept))},
        compiler_params=pltpu.CompilerParams(vmem_limit_bytes=60 * MIB),
        cost_estimate=LONG,
        name="attend_backward",
    )(
        qk, qk, values, mixed, mixed_grad, lse, segment_down, segment_across, cos_table, sin_table, *kept
    )


HBM = pl.BlockSpec(memory_space=pl.ANY)


def whole(shape):
    return pl.BlockSpec(shape, lambda *_: (0,) * len(shape), pipeline_mode=pl.Buffered(1))


def shaped(shape, dtype=BF16):
    return jax.ShapeDtypeStruct(shape, dtype)


def kernel_call(body, name, operands, in_specs, out_specs, out_shape, grid=(), scratch=(), scalars=(), aliases=None, vmem=40, flops=1, kept=False):
    return pl.pallas_call(
        body,
        grid_spec=pltpu.PrefetchScalarGridSpec(
            num_scalar_prefetch=len(scalars),
            grid=grid,
            in_specs=in_specs,
            out_specs=out_specs,
            scratch_shapes=list(scratch),
        ),
        out_shape=out_shape,
        input_output_aliases=aliases or {},
        compiler_params=pltpu.CompilerParams(vmem_limit_bytes=vmem * MIB, has_side_effects=kept),
        cost_estimate=pl.CostEstimate(flops=flops, bytes_accessed=1, transcendentals=1),
        name=name,
    )(*scalars, *operands)


def copies_into(blocks, target, semaphores, first, columns=None, rows=None):
    copies, at = [], 0
    for i, block in enumerate(blocks):
        deep = rows or block.shape[0]
        source = block if columns is None else block.at[pl.ds(0, deep), columns]
        copies.append(
            pltpu.make_async_copy(source, target.at[pl.ds(at, deep), :], semaphores.at[first + i])
        )
        at += deep
    return copies


def start_all(step, copies):
    @pl.when(step == 0)
    def _():
        for copy in copies:
            copy.start()


def wait_at(step, when, copies):
    @pl.when(step == when)
    def _():
        for copy in copies:
            copy.wait()


def halves(copies):
    return copies[: len(copies) // 2], copies[len(copies) // 2 :]


def mark_body(in_ref, out_ref):
    out_ref[...] = in_ref[...]


def mark(token, flops):
    return kernel_call(
        mark_body,
        "mark",
        [token],
        [whole(token.shape)],
        whole(token.shape),
        shaped(token.shape, token.dtype),
        grid=(1,),
        flops=flops,
        kept=True,
    )


def pick_columns(order, values):
    count = order.shape[0]
    width = values.shape[1] // count
    parts = [lax.dynamic_slice_in_dim(values, order[j] * width, width, 1) for j in range(count)]
    return jnp.concatenate(parts, axis=1)


def back_in_place(order, values):
    count = order.shape[0]
    if values.shape[1] // count % 128 == 0:
        return values
    places = jnp.arange(count, dtype=jnp.int32)
    back = jnp.sum(jnp.where(order[:, None] == places[None, :], places[:, None], 0), axis=0)
    return pick_columns(back, values)


def chunks(wide):
    return [(at, min(256, wide - at)) for at in range(0, wide, 256)]


def reorder_body(count, width, order_ref, in_ref, out_ref):
    for j in range(count):
        source = pl.ds(pl.multiple_of(order_ref[j] * width, width), width)
        out_ref[:, j * width : (j + 1) * width] = in_ref[:, source]


def reorder(order, values):
    count = order.shape[0]
    if values.shape[1] // count % 128:
        return pick_columns(order, values)
    return kernel_call(
        functools.partial(reorder_body, count, values.shape[1] // count),
        "reorder",
        [values],
        [whole(values.shape)],
        whole(values.shape),
        shaped(values.shape),
        vmem=60,
        grid=(1,),
        scalars=[order],
    )


def put_back(order_ref, out_ref, values):
    count = order_ref.shape[0]
    width = values.shape[1] // count
    if width % 128:
        out_ref[...] = values.astype(out_ref.dtype)
        return
    for j in range(count):
        target = pl.ds(pl.multiple_of(order_ref[j] * width, width), width)
        out_ref[:, target] = values[:, j * width : (j + 1) * width].astype(out_ref.dtype)


def stats_body(x_ref, mean_ref, inverse_ref):
    values = x_ref[...].astype(F32)
    mean = jnp.mean(values, axis=-1, keepdims=True)
    centred = values - mean
    mean_ref[...] = mean
    inverse_ref[...] = lax.rsqrt(jnp.mean(centred * centred, axis=-1, keepdims=True) + EPSILON)


def row_stats(inputs):
    length, depth = inputs.shape
    by_rows = lambda columns: pl.BlockSpec((length // 4, columns), lambda i: (i, 0))
    return kernel_call(
        stats_body,
        "row_stats",
        [inputs],
        [by_rows(depth)],
        [by_rows(1)] * 2,
        [shaped((length, 1), F32)] * 2,
        grid=(4,),
    )


def decode_body(count, chunk, order_ref, *refs):
    blocks, norm_ref, bias_ref = refs[:count], refs[-2], refs[-1]
    width = norm_ref.shape[1] // count
    wide = bias_ref.shape[1]
    small = wide // count
    rows = []
    for j, block in enumerate(blocks):
        norm_ref[:, j * width : (j + 1) * width] = block[0:4, :width].astype(F32)
        rows.append(block[4:5, :small].astype(F32))
    lane = lax.broadcasted_iota(jnp.int32, (small, wide), 1)
    source = lax.broadcasted_iota(jnp.int32, (small, wide), 0)
    spread = (lane // HD * chunk + lane % chunk == source).astype(BF16)
    spread = product(jnp.concatenate(rows, axis=0).astype(BF16), spread, 1, 0)
    lane = lax.broadcasted_iota(jnp.int32, (1, wide), 1)
    total = jnp.zeros((1, wide), F32)
    for j in range(count):
        total = jnp.where(lane % HD // chunk == order_ref[j], spread[j : j + 1, :], total)
    bias_ref[...] = total


def decode(order, blocks, depth, bias_wide):
    count = len(blocks)
    rows, wide = blocks[0].shape
    return kernel_call(
        functools.partial(decode_body, count, HD // count),
        "decode",
        blocks,
        [pl.BlockSpec((16, wide), lambda i, order: (rows // 16 - 1, 0))] * count,
        [whole((4, depth)), whole((1, bias_wide))],
        [shaped((4, depth), F32), shaped((1, bias_wide), F32)],
        grid=(1,),
        scalars=[order],
    )


def qkv_body(count, x_ref, norm_ref, bias_ref, mean_ref, inverse_ref, cos_ref, sin_ref, *refs):
    blocks_a, blocks_b, refs = refs[:count], refs[count : 2 * count], refs[2 * count :]
    qk_ref, v_ref, normed_ref, weight_a, weight_v, semaphores = refs
    step = pl.program_id(0)
    width = qk_ref.shape[1]
    deep = weight_a.shape[0] // count
    copies_a = copies_into(blocks_a, weight_a, semaphores, 0, rows=deep)
    copies_v = copies_into(blocks_b, weight_v, semaphores, count, pl.ds(0, width // 2), deep)
    start_all(step, copies_a + copies_v)
    values = (x_ref[...].astype(F32) - mean_ref[...]) * inverse_ref[...]
    normed = (values * norm_ref[0:1, :] + norm_ref[1:2, :]).astype(BF16)
    normed_ref[...] = normed
    wait_at(step, 0, copies_a + copies_v)
    opening = opening_lanes(normed.shape[0])
    cos_values = cos_ref[...]
    sin_values = sin_ref[...]
    for at, wide in chunks(width):
        both = product(normed, weight_a[:, at : at + wide], 1, 0) + bias_ref[:, at : at + wide]
        for pair in range(0, wide, PAIR):
            part = turn(both[:, pair : pair + PAIR], cos_values, sin_values, opening)
            qk_ref[:, at + pair : at + pair + PAIR] = part.astype(BF16)
    for at, wide in chunks(width // 2):
        values = product(normed, weight_v[:, at : at + wide], 1, 0)
        bias = bias_ref[:, width + at : width + at + wide]
        v_ref[:, at : at + wide] = (values + bias).astype(BF16)


def project_qkv(inputs, mean, inverse, norm_rows, bias_row, cos_table, sin_table, blocks_a, blocks_b):
    length, depth = inputs.shape
    rows = length // 4
    wide = blocks_a[0].shape[1]
    count = len(blocks_a)
    by_rows = lambda columns: pl.BlockSpec((rows, columns), lambda i: (i, 0))
    return kernel_call(
        functools.partial(qkv_body, count),
        "project_qkv",
        [inputs, norm_rows, bias_row, mean, inverse, cos_table, sin_table, *blocks_a, *blocks_b],
        [
            by_rows(depth),
            whole(norm_rows.shape),
            whole(bias_row.shape),
            by_rows(1),
            by_rows(1),
            by_rows(PAIR),
            by_rows(PAIR),
        ]
        + [HBM] * (2 * count),
        [by_rows(wide), by_rows(wide // 2), by_rows(depth)],
        [shaped((length, wide)), shaped((length, wide // 2)), shaped((length, depth))],
        grid=(4,),
        flops=10**9,
        scratch=[
            pltpu.VMEM((depth, wide), BF16),
            pltpu.VMEM((depth, wide // 2), BF16),
            pltpu.SemaphoreType.DMA((2 * count,)),
        ],
        vmem=60,
    )


def gated_body(count, x_ref, *refs):
    gate_blocks, up_blocks, refs = refs[:count], refs[count : 2 * count], refs[2 * count :]
    gate_ref, up_ref, hidden_ref, gate_weight, up_weight, semaphores = refs[-6:]
    step = pl.program_id(0)
    early, late = halves(copies_into(gate_blocks, gate_weight, semaphores, 0))
    early_up, late_up = halves(copies_into(up_blocks, up_weight, semaphores, count))
    start_all(step, early + late + early_up + late_up)
    half = gate_weight.shape[0] // 2
    wait_at(step, 0, early)
    gate = product(x_ref[:, :half], gate_weight[:half, :], 1, 0)
    wait_at(step, 0, late)
    gate = gate + product(x_ref[:, half:], gate_weight[half:, :], 1, 0)
    gate_ref[...] = gate.astype(BF16)
    wait_at(step, 0, early_up + late_up)
    up = product(x_ref[...], up_weight[...], 1, 0)
    up_ref[...] = up.astype(BF16)
    hidden_ref[...] = (gate * jax.nn.sigmoid(gate) * up).astype(BF16)


def gated_forward(inputs, gate_blocks, up_blocks, half, kept):
    length, depth = inputs.shape
    rows = length // 4
    wide = gate_blocks[0].shape[1]
    count = len(gate_blocks)
    kept = list(kept or [])
    place = lambda columns: pl.BlockSpec((rows, columns), lambda i: (2 * half + i, 0))
    first = 1 + 2 * count
    return kernel_call(
        functools.partial(gated_body, count),
        "gated_forward",
        [inputs, *gate_blocks, *up_blocks, *kept],
        [place(depth)] + [HBM] * (2 * count + len(kept)),
        [place(wide)] * 3,
        [shaped((length, wide))] * 3,
        grid=(2,),
        flops=10**9,
        scratch=[
            pltpu.VMEM((depth, wide), BF16),
            pltpu.VMEM((depth, wide), BF16),
            pltpu.SemaphoreType.DMA((2 * count,)),
        ],
        aliases={first + i: i for i in range(len(kept))},
        vmem=60,
    )


def gated_back_body(count, *refs):
    grad_ref, gate_ref, up_ref, refs = refs[0], refs[1], refs[2], refs[3:]
    blocks = refs[:count]
    gate_grad_ref, up_grad_ref, weight, semaphores = refs[-4:]
    step = pl.program_id(0)
    copies = copies_into(blocks, weight, semaphores, 0)
    start_all(step, copies)
    wait_at(step, 0, copies)
    rows = grad_ref[...]
    for at, wide in chunks(weight.shape[1]):
        span = slice(at, at + wide)
        hidden_grad = product(rows, weight[:, span], 1, 0)
        gate = gate_ref[:, span].astype(F32)
        sigmoid = jax.nn.sigmoid(gate)
        silu = gate * sigmoid
        up_grad_ref[:, span] = (hidden_grad * silu).astype(BF16)
        slope = sigmoid + silu * (1.0 - sigmoid)
        gate_grad_ref[:, span] = (hidden_grad * up_ref[:, span].astype(F32) * slope).astype(BF16)


def gated_backward(grads, gate, up, blocks):
    length, wide = gate.shape
    rows = length // 4
    depth = grads.shape[1]
    count = len(blocks)
    by_rows = lambda columns: pl.BlockSpec((rows, columns), lambda i: (i, 0))
    return kernel_call(
        functools.partial(gated_back_body, count),
        "gated_backward",
        [grads, gate, up, *blocks],
        [by_rows(depth), by_rows(wide), by_rows(wide)] + [HBM] * count,
        [by_rows(wide)] * 2,
        [shaped((length, wide))] * 2,
        grid=(4,),
        flops=10**9,
        scratch=[pltpu.VMEM((depth, wide), BF16), pltpu.SemaphoreType.DMA((count,))],
        vmem=60,
    )


STRIPES = 4


def outward_body(shape, columns, deep, apart, *refs):
    if apart:
        here, refs = refs[0][0], refs[1:]
    lefts, refs = refs[: len(shape)], refs[len(shape) :]
    outs = refs[sum(shape) : sum(shape) + 1 + apart]
    weights, semaphores = refs[sum(shape) + 1 + apart : -1], refs[-1]
    step = pl.program_id(0)
    at, groups = 0, []
    for count, weight, column in zip(shape, weights, columns):
        groups.append(
            copies_into(refs[at : at + count], weight, semaphores, at, column, deep)
        )
        at += count
    for stripe in range(STRIPES):
        start_all(
            step,
            [
                copy
                for group in groups
                for copy in group[stripe * len(group) // STRIPES : (stripe + 1) * len(group) // STRIPES]
            ],
        )
    for stripe in range(STRIPES):
        for group in groups:
            wait_at(
                step,
                stripe,
                group[stripe * len(group) // STRIPES : (stripe + 1) * len(group) // STRIPES],
            )
    tall = weights[0].shape[0] // STRIPES
    span = pl.ds(pl.multiple_of(step * tall, tall), tall)
    total = None
    for left, weight in zip(lefts, weights):
        term = product(left[...], weight[span, :], 1, 1)
        total = term if total is None else total + term
    if not apart:
        outs[0][...] = total.astype(BF16)
        return
    rows = total.shape[0] // 4
    for i in range(4):
        away = jnp.bitwise_xor(here, i)
        span = pl.ds(pl.multiple_of((1 - away // 2) * rows, rows), rows)
        values = total[i * rows : (i + 1) * rows].astype(BF16)
        for other, out_ref in enumerate(outs):

            @pl.when(away % 2 == other)
            def _():
                out_ref[span, :] = values


def outward(parts, depth, name, place=None):
    lefts = [left for left, _, _ in parts]
    length = lefts[0].shape[0]
    shape = [len(blocks) for _, blocks, _ in parts]
    tall = (0,) if place is None else (0, 1)
    deep = None
    columns = []
    for left, blocks, column in parts:
        if column is None:
            columns.append(None)
        else:
            columns.append(pl.ds(column, left.shape[1]))
            deep = depth // len(blocks)
    return kernel_call(
        functools.partial(outward_body, shape, columns, deep, place is not None),
        name,
        [*lefts, *(block for _, blocks, _ in parts for block in blocks)],
        [whole(left.shape) for left in lefts] + [HBM] * sum(shape),
        [pl.BlockSpec((length // len(tall), depth // STRIPES), lambda i, *_: (0, i)) for _ in tall],
        [shaped((length // len(tall), depth)) for _ in tall],
        scalars=() if place is None else (place,),
        grid=(STRIPES,),
        flops=10**9,
        scratch=[pltpu.VMEM((depth, left.shape[1]), BF16) for left in lefts]
        + [pltpu.SemaphoreType.DMA((sum(shape),))],
        vmem=60,
    )


def mixed_grad_body(count, rows_ref, *refs):
    blocks = refs[:count]
    out_ref, weight, semaphores = refs[count:]
    step = pl.program_id(0)
    wide = weight.shape[1]
    copies = copies_into(blocks, weight, semaphores, 0, pl.ds(wide, wide), weight.shape[0] // count)
    start_all(step, copies)
    wait_at(step, 0, copies)
    out_ref[...] = product(rows_ref[...], weight[...], 1, 0).astype(BF16)


def through_out(branch, blocks):
    length, depth = branch.shape
    rows = length // 4
    wide = blocks[0].shape[1] // 2
    count = len(blocks)
    return kernel_call(
        functools.partial(mixed_grad_body, count),
        "through_out",
        [branch, *blocks],
        [pl.BlockSpec((rows, depth), lambda i: (i, 0))] + [HBM] * count,
        pl.BlockSpec((rows, wide), lambda i: (i, 0)),
        shaped((length, wide)),
        grid=(4,),
        flops=10**9,
        scratch=[pltpu.VMEM((depth, wide), BF16), pltpu.SemaphoreType.DMA((count,))],
        vmem=60,
    )


def heads_body(count, q_ref, k_ref, v_ref, x_ref, mean_ref, inverse_ref, *refs):
    blocks_a, blocks_b = refs[:count], refs[count : 2 * count]
    out_ref, sums_ref, weight_a, weight_v, semaphores = refs[2 * count :]
    step = pl.program_id(0)
    wide = q_ref.shape[1]
    deep = weight_a.shape[0] // count
    copies_a = copies_into(blocks_a, weight_a, semaphores, 0, rows=deep)
    copies_v = copies_into(blocks_b, weight_v, semaphores, count, pl.ds(0, wide), deep)
    start_all(step, [copy for pair in zip(copies_a, copies_v) for copy in pair])
    for stripe in range(STRIPES):
        span = slice(stripe * count // STRIPES, (stripe + 1) * count // STRIPES)
        wait_at(step, stripe, copies_a[span] + copies_v[span])
    tall = weight_a.shape[0] // STRIPES
    span = pl.ds(pl.multiple_of(step * tall, tall), tall)
    total = product(q_ref[...], weight_a[span, :wide], 1, 1)
    total = total + product(k_ref[...], weight_a[span, wide:], 1, 1)
    total = total + product(v_ref[...], weight_v[span, :], 1, 1)
    out_ref[...] = total.astype(BF16)
    standard = (x_ref[...].astype(F32) - mean_ref[...]) * inverse_ref[...]
    sums_ref[0:1, :] = (total * standard).sum(0, keepdims=True)
    sums_ref[1:2, :] = total.sum(0, keepdims=True)


def through_heads(grads, inputs, mean, inverse, blocks_a, blocks_b):
    length, wide = grads[0].shape
    depth = inputs.shape[1]
    count = len(blocks_a)
    striped = lambda tall: pl.BlockSpec((tall, depth // STRIPES), lambda i: (0, i))
    return kernel_call(
        functools.partial(heads_body, count),
        "through_heads",
        [*grads, inputs, mean, inverse, *blocks_a, *blocks_b],
        [whole((length, wide))] * 3
        + [striped(length), whole((length, 1)), whole((length, 1))]
        + [HBM] * (2 * count),
        [striped(length), striped(2)],
        [shaped((length, depth)), shaped((2, depth), F32)],
        grid=(STRIPES,),
        flops=10**9,
        scratch=[
            pltpu.VMEM((depth, 2 * wide), BF16),
            pltpu.VMEM((depth, wide), BF16),
            pltpu.SemaphoreType.DMA((2 * count,)),
        ],
        vmem=60,
    )


def over_tokens_body(count, *refs):
    out_ref = refs[-1]
    first = 0
    for i in range(count):
        left, right = refs[2 * i], refs[2 * i + 1]
        wide = right.shape[1]
        out_ref[:, first : first + wide] = product(left[...], right[...], 0, 0).astype(BF16)
        first += wide


def over_tokens(groups, flops=10**9):
    length, depth = groups[0][0].shape
    wide = sum(right.shape[1] for _, right in groups)
    block = depth // STRIPES
    return kernel_call(
        functools.partial(over_tokens_body, len(groups)),
        "over_tokens",
        [values for group in groups for values in group],
        [
            spec
            for _, right in groups
            for spec in (pl.BlockSpec((length, block), lambda i: (0, i)), whole(right.shape))
        ],
        pl.BlockSpec((block, wide), lambda i: (i, 0)),
        shaped((depth, wide)),
        grid=(STRIPES,),
        flops=flops,
        vmem=60,
    )


def added(refs):
    total = refs[0][...].astype(F32)
    for ref in refs[1:]:
        total = total + ref[...].astype(F32)
    return total


def meet_body(own_ref, arrived_ref, far_ref, near_ref):
    rows = far_ref.shape[0]
    total = own_ref[...].astype(F32) + arrived_ref[...].astype(F32)
    far_ref[...] = total[:rows].astype(BF16)
    near_ref[...] = total[rows:]


def meet(own, arrived):
    length, depth = own.shape
    half = (length // 2, depth)
    return kernel_call(
        meet_body,
        "meet",
        [own, arrived],
        [whole(own.shape)] * 2,
        [whole(half)] * 2,
        [shaped(half), shaped(half, F32)],
        grid=(1,),
    )


def second_norm_body(x_ref, term_ref, norm_ref, middle_ref, mean_ref, inverse_ref, out_ref):
    middle = added([x_ref, term_ref])
    middle_ref[...] = middle
    mean = jnp.mean(middle, axis=-1, keepdims=True)
    centred = middle - mean
    inverse = lax.rsqrt(jnp.mean(centred * centred, axis=-1, keepdims=True) + EPSILON)
    mean_ref[...] = mean
    inverse_ref[...] = inverse
    out_ref[...] = (centred * inverse * norm_ref[2:3, :] + norm_ref[3:4, :]).astype(BF16)


def second_norm(inputs, terms, norm_rows):
    shape = inputs.shape
    column = (shape[0], 1)
    return kernel_call(
        second_norm_body,
        "second_norm",
        [inputs, *terms, norm_rows],
        [whole(shape)] * 2 + [whole(norm_rows.shape)],
        [whole(shape), whole(column), whole(column), whole(shape)],
        [shaped(shape, F32), shaped(column, F32), shaped(column, F32), shaped(shape)],
        vmem=60,
        grid=(1,),
    )


def norm_gradient(upstream, standard, inverse, gain):
    scaled = upstream * gain
    inner = (
        scaled
        - jnp.mean(scaled, axis=-1, keepdims=True)
        - standard * jnp.mean(scaled * standard, axis=-1, keepdims=True)
    )
    return inverse * inner


def second_back_body(near_ref, far_ref, middle_ref, mean_ref, inverse_ref, norm_ref, grad_ref, full_ref, branch_ref, sums_ref):
    upstream = added([near_ref, far_ref])
    inverse = inverse_ref[...]
    standard = (middle_ref[...] - mean_ref[...]) * inverse
    sums_ref[0:1, :] = (upstream * standard).sum(0, keepdims=True)
    sums_ref[1:2, :] = upstream.sum(0, keepdims=True)
    grad = grad_ref[...].astype(F32) + norm_gradient(upstream, standard, inverse, norm_ref[2:3, :])
    full_ref[...] = grad
    branch_ref[...] = grad.astype(BF16)


def second_norm_back(terms, middle, mean, inverse, norm_rows, grads):
    shape = middle.shape
    column = (shape[0], 1)
    return kernel_call(
        second_back_body,
        "second_norm_back",
        [*terms, middle, mean, inverse, norm_rows, grads],
        [whole(shape)] * 3 + [whole(column)] * 2 + [whole(norm_rows.shape), whole(shape)],
        [whole(shape), whole(shape), whole((2, shape[1]))],
        [shaped(shape, F32), shaped(shape), shaped((2, shape[1]), F32)],
        vmem=60,
        grid=(1,),
    )


def input_back_body(order_ref, upstream_ref, x_ref, norm_ref, grad_ref, out_ref):
    values = x_ref[...].astype(F32)
    centred = values - jnp.mean(values, axis=-1, keepdims=True)
    inverse = lax.rsqrt(jnp.mean(centred * centred, axis=-1, keepdims=True) + EPSILON)
    upstream = upstream_ref[...].astype(F32)
    grad = grad_ref[...] + norm_gradient(upstream, centred * inverse, inverse, norm_ref[0:1, :])
    put_back(order_ref, out_ref, grad)


def input_back(order, upstream, inputs, norm_rows, grads):
    shape = inputs.shape
    out = kernel_call(
        input_back_body,
        "input_back",
        [upstream, inputs, norm_rows, grads],
        [whole(shape)] * 2 + [whole(norm_rows.shape), whole(shape)],
        whole(shape),
        shaped(shape),
        grid=(1,),
        scalars=[order],
    )
    return back_in_place(order, out)


def result_body(order_ref, middle_ref, term_ref, out_ref):
    put_back(order_ref, out_ref, added([middle_ref, term_ref]))


def finish_result(order, middle, term):
    shape = middle.shape
    out = kernel_call(
        result_body,
        "finish_result",
        [middle, term],
        [whole(shape)] * 2,
        whole(shape),
        shaped(shape),
        grid=(1,),
        scalars=[order],
    )
    return back_in_place(order, out)


def hand_on_body(arrivals, sides, *refs):
    arrived, own, outs = refs[:arrivals], refs[arrivals : -sides], refs[-sides:]
    parts = len(own) // sides
    for side in range(sides):
        first = 0
        for part in own[side * parts : (side + 1) * parts]:
            span = slice(first, first + part.shape[1])
            values = part[...]
            if arrivals:
                values = (values.astype(F32) + arrived[side][:, span].astype(F32)).astype(BF16)
            outs[side][:, span] = values
            first += part.shape[1]


def hand_on(arrived, own, rows, places):
    shape = (rows, sum(part.shape[1] for part in own))
    sides = len(places)
    half = (rows // 2, shape[1])
    by_halves = pl.BlockSpec(half, lambda i: (i, 0))
    return kernel_call(
        functools.partial(hand_on_body, len(arrived), sides),
        "hand_on",
        [*arrived, *(part for _ in places for part in own)],
        [by_halves] * len(arrived)
        + [
            pl.BlockSpec((rows // 2, part.shape[1]), lambda i, at=at: (2 * at + i, 0))
            for at in places
            for part in own
        ],
        [by_halves] * sides,
        [shaped(shape)] * sides,
        grid=(2,),
        vmem=60,
    )


class Route:
    def __init__(self, count):
        self.count = count
        self.reach = count // 2
        self.ring = list(range(0, count, 2)) + list(range(count - 1, 0, -2))
        ahead = [(self.ring[i], self.ring[(i + 1) % count]) for i in range(count)]
        self.pairs = (ahead, [(b, a) for a, b in ahead])

    def send(self, values, direction):
        return lax.ppermute(values, "dp", self.pairs[direction])


class Gathering:
    def __init__(self, route, block, longer):
        self.route = route
        self.blocks = {0: block}
        self.steps = 0
        self.hops = [route.reach - (direction != longer) for direction in range(2)]
        self.done = 0
        self.flying = [block]

    def pending(self):
        return self.flying

    def resume(self, arrived):
        route = self.route
        if self.done == 0:
            self.blocks[0] = arrived[0]
            latest = [arrived[0], arrived[0]]
        else:
            arrived = list(arrived)
            latest = [None, None]
            for direction in range(2):
                if self.done <= self.hops[direction]:
                    latest[direction] = arrived.pop(0)
                    at = route.count - self.done if direction == 0 else self.done
                    self.blocks[at] = latest[direction]
        self.done += 1
        self.flying = [
            route.send(latest[direction], direction)
            for direction in range(2)
            if self.done <= self.hops[direction]
        ]

    def all(self):
        return [self.blocks[j] for j in range(self.route.count)]


class Summing:
    def __init__(self, route, own, rows, per, offset, longer):
        self.route = route
        self.own = own
        self.rows = rows
        self.place = lambda j: per * j + offset
        self.hops = [route.reach - (direction != longer) for direction in range(2)]
        self.steps = 0
        self.done = 0
        self.flying = None
        self.last = [None, None]

    def terms(self, arrived, directions):
        places = []
        for direction in directions:
            left = self.hops[direction] - self.done
            at = left if direction == 0 else (self.route.count - left) % self.route.count
            places.append(self.place(at))
        return hand_on(arrived, self.own(), self.rows, places)

    def pending(self):
        return self.flying if self.done else self.terms([], range(2))

    def resume(self, arrived):
        arrived = list(arrived)
        onward = range(2)
        if self.done:
            landed = [direction for direction in range(2) if self.done <= self.hops[direction]]
            onward = [direction for direction in landed if self.done < self.hops[direction]]
            by_way = dict(zip(landed, arrived))
            for direction in landed:
                if self.done == self.hops[direction]:
                    self.last[direction] = by_way[direction]
            if onward:
                arrived = self.terms([by_way[direction] for direction in onward], onward)
        self.done += 1
        self.flying = [self.route.send(values, way) for way, values in zip(onward, arrived)]

    def total(self, part, first):
        at = self.place(0) * self.rows
        own = part[at : at + self.rows].astype(F32)
        span = slice(first, first + part.shape[1])
        return own + self.last[0][:, span].astype(F32) + self.last[1][:, span].astype(F32)


STEPS = 5


class Pace:
    def __init__(self, token):
        self.token = token

    def __call__(self, streams, *carried, busy=False, long=False):
        last = {}
        for stream in streams:
            stream.steps += 1
            last[stream] = (stream.steps * (stream.route.reach + 1)) // STEPS
        first = True
        while first or any(stream.done < last[stream] for stream in streams):
            first = False
            moving = [stream for stream in streams if stream.done < last[stream]]
            waiting = [list(stream.pending()) for stream in moving]
            flat = [values for group in waiting for values in group]
            self.token, *out = lax.optimization_barrier((self.token, *flat, *carried))
            carried = out[len(flat) :]
            at = 0
            for stream, group in zip(moving, waiting):
                stream.resume(out[at : at + len(group)])
                at += len(group)
        if not busy:
            self.token = mark(self.token, 10**12 if long else 10**9)
            self.token, *carried = lax.optimization_barrier((self.token, *carried))
        return carried[0] if len(carried) == 1 else carried


def across_core(values):
    return lax.ppermute(values, "tensor", [(i, i ^ 1) for i in range(4)])


def across_chip(values):
    return lax.ppermute(values, "tensor", [(i, i ^ 2) for i in range(4)])


def halve(route, table):
    left = table.shape[0] // 2
    pairs = [(route.ring[i], route.ring[(i + left) % route.count]) for i in range(route.count)]
    return lax.ppermute(table[left:], "dp", pairs)


def on_device(
    route,
    activations,
    cotangent,
    segments,
    norm_one_gain,
    norm_one_bias,
    w_query,
    w_key,
    w_value,
    qkv_bias,
    w_out,
    norm_two_gain,
    norm_two_bias,
    w_gate,
    w_up,
    w_down,
):
    count = route.count
    third, depth = activations.shape
    length = segments.shape[0]
    width = depth // count
    part = width // 2
    heads_wide = w_query.shape[1]
    local_heads = heads_wide // HD
    shards = length // third
    here = lax.axis_index("tensor")
    place = here.astype(jnp.int32).reshape(1)
    advance = Pace(jnp.zeros((8, 128), jnp.int32) + here)
    device = lax.axis_index("dp").astype(jnp.int32)
    position = jnp.where(device % 2 == 0, device // 2, count - 1 - device // 2)
    ahead = (position + jnp.arange(count, dtype=jnp.int32)) % count
    order = jnp.where(ahead < count // 2, 2 * ahead, 2 * (count - 1 - ahead) + 1)

    def gather(values):
        return lax.all_gather(values, "tensor", axis=0, tiled=True)

    def scatter(values):
        return lax.psum_scatter(values, "tensor", scatter_dimension=0, tiled=True)

    def relative(values):
        def pick(entries):
            return jnp.concatenate([values[i : i + 1] for i in entries], axis=0)

        values = jnp.where(here % 2 == 1, pick((1, 0, 3, 2)), values)
        return jnp.where(here >= 2, pick((2, 3, 0, 1)), values)

    bias_size = qkv_bias.size
    norm_part = norm_one_gain.shape[0]
    ring_qk = Gathering(route, jnp.concatenate([w_query, w_key], axis=1), 0)
    ring_vo = Gathering(route, None, 1)
    ring_gate = Gathering(route, w_gate, 0)
    ring_up = Gathering(route, w_up, 1)
    ring_down = [Gathering(route, None, 0), Gathering(route, None, 1)]

    packed = jnp.stack([norm_one_gain, norm_one_bias, norm_two_gain, norm_two_bias])
    packed_core = across_core(packed)
    packed_chip = across_chip(packed)
    packed_far = lax.ppermute(packed, "tensor", [(i, i ^ 3) for i in range(4)])
    own_bf16 = reorder(order, activations)
    x_all = gather(own_bf16)
    weight_vo = jnp.concatenate([w_value, w_out.T], axis=1)
    packed, packed_core, packed_chip, packed_far, weight_vo, cotangent, w_down = advance(
        [], packed, packed_core, packed_chip, packed_far, weight_vo, cotangent, w_down
    )
    packed = jnp.stack([packed, packed_core, packed_chip, packed_far])
    packed = relative(packed).transpose(1, 0, 2).reshape(4, width)
    wide = 2 * heads_wide
    packed = jnp.concatenate(
        [
            jnp.pad(packed, ((0, 0), (0, wide - width))),
            jnp.pad(qkv_bias.reshape(1, bias_size), ((0, 11), (0, wide - bias_size))),
        ],
        axis=0,
    )
    ring_vo.flying = [jnp.concatenate([weight_vo, packed], axis=0)]
    cotangent, w_down = advance([ring_qk, ring_vo], cotangent, w_down, long=True)
    own_grad = reorder(order, cotangent)
    own_grad, w_down = advance([ring_qk], own_grad, w_down)
    down_rows = w_down.T
    ring_down[0].flying = [down_rows[:part]]
    ring_down[1].flying = [down_rows[part:]]
    own_grad = advance([ring_vo], own_grad)
    x_all, own_grad = advance([ring_qk], x_all, own_grad)
    grad_all = gather(own_grad)
    mean_one, inverse_one = row_stats(x_all)
    mean_one, inverse_one, segments = advance([ring_vo], mean_one, inverse_one, segments)
    segment_down, segment_across = segments[:, None], segments[None, :]
    begins = jnp.sum((segment_across < segment_down).astype(F32), axis=1, keepdims=True)
    places = jnp.arange(length, dtype=jnp.int32)[:, None].astype(F32)
    lanes = jnp.arange(PAIR, dtype=jnp.int32) % HD
    frequency = 10000.0 ** (-2.0 * (lanes % (ROT // 2)).astype(F32) / ROT)
    angles = (places - begins) * frequency[None, :]
    cos_table = jnp.where(lanes < ROT, jnp.cos(angles), 1.0)
    sin_table = jnp.where(
        lanes < ROT, jnp.where(lanes < ROT // 2, -1.0, 1.0) * jnp.sin(angles), 0.0
    )
    cos_table, sin_table, segment_down, segment_across = advance(
        [ring_qk], cos_table, sin_table, segment_down, segment_across
    )
    advance([ring_vo])
    advance([ring_qk, ring_gate])
    advance([ring_vo, ring_up], long=True)
    blocks_a = ring_qk.all()
    blocks_b = ring_vo.all()
    norm_rows, bias_row = decode(order, blocks_b, depth, 3 * heads_wide)
    qk, values, normed = project_qkv(
        x_all, mean_one, inverse_one, norm_rows, bias_row, cos_table, sin_table, blocks_a, blocks_b
    )
    qk, values, grad_all = advance([ring_gate], qk, values, grad_all, busy=True)
    mixed, lse = attend_forward(qk, values, segment_down, segment_across, 2)
    mixed, lse = advance([ring_up], mixed, lse, busy=True)
    arriving = scatter(outward([(mixed, blocks_b, heads_wide)], depth, "from_heads")[0])
    advance([ring_gate])
    advance([ring_up], long=True)
    arriving = advance([ring_gate], arriving)
    middle, mean_two, inverse_two, n_own = second_norm(own_bf16, [arriving], norm_rows)
    normed_two = gather(n_own)
    middle = advance([], middle, long=True)
    advance([ring_up, ring_down[0]])
    advance([ring_gate])
    advance([ring_up, ring_down[1]])
    advance([ring_down[0]])
    normed_two = advance([ring_down[1]], normed_two, busy=True)
    gate_blocks = ring_gate.all()
    up_blocks = ring_up.all()
    kept = gated_forward(normed_two, gate_blocks, up_blocks, 0, None)
    kept = advance([ring_down[0]], *kept)
    kept = advance([ring_down[1]], *kept, busy=True)
    gate, up, hidden = gated_forward(normed_two, gate_blocks, up_blocks, 1, kept)
    gate, up, hidden = advance([ring_down[0]], gate, up, hidden)
    hidden = advance([ring_down[1]], hidden)
    down_sum = product(grad_all, hidden, 0, 0).astype(BF16)
    sum_down = Summing(route, lambda: [down_sum], width, 1, 0, 0)
    down_sum = advance([ring_down[0]], down_sum)
    advance([ring_down[1], sum_down], busy=True)
    down_blocks = [block for pair in zip(*(ring.all() for ring in ring_down)) for block in pair]

    gate_grad, up_grad = gated_backward(grad_all, gate, up, down_blocks)
    gate_grad, up_grad = advance([sum_down], gate_grad, up_grad)
    gate_sum = product(normed_two, gate_grad, 0, 0).astype(BF16)
    sum_gate = Summing(route, lambda: [gate_sum], width, 1, 0, 1)
    gate_sum, gate_grad, up_grad = advance([sum_gate], gate_sum, gate_grad, up_grad, busy=True)
    own, cross = outward(
        [(gate_grad, gate_blocks, None), (up_grad, up_blocks, None)], depth, "from_gates", place
    )
    own, cross = advance([sum_down], own, cross)
    own, cross, up_grad = advance([sum_gate], own, cross, up_grad, busy=True)
    arrived = across_core(cross)
    own, arrived, up_grad = advance([], own, arrived, up_grad, busy=True)
    far, near = meet(own, arrived)
    arriving = across_chip(far)
    near, up_grad = advance([], near, up_grad)
    up_sum = product(normed_two, up_grad, 0, 0).astype(BF16)
    sum_up = Summing(route, lambda: [up_sum], width, 1, 0, 0)
    up_sum = advance([sum_down], up_sum)
    arriving = advance([sum_gate], arriving)
    middle_grad, b_own, two_sums = second_norm_back(
        [near, arriving], middle, mean_two, inverse_two, norm_rows, own_grad
    )
    branch = gather(b_own)
    hidden, middle_grad = advance([], hidden, middle_grad, long=True)
    (result_terms,) = outward([(hidden, down_blocks, None)], depth, "from_hidden")
    result_terms = advance([sum_down, sum_up], result_terms)
    advance([sum_gate])
    branch, result_terms = advance([sum_up], branch, result_terms, busy=True)
    arriving_result = scatter(result_terms)
    mixed_grad = through_out(branch, blocks_b)
    mixed_grad, branch = advance([], mixed_grad, branch, busy=True)
    grads = None
    for half in range(2):
        grads = attend_backward(
            qk,
            values,
            mixed,
            mixed_grad,
            lse,
            segment_down,
            segment_across,
            cos_table,
            sin_table,
            2,
            half,
            grads,
        )
        if half == 0:
            grads = advance([sum_gate], *grads)
        grads = advance([sum_up], *grads, busy=True)
    q_grad, k_grad, v_grad, bias_sums = grads
    qk_sum = over_tokens([(normed, q_grad), (normed, k_grad)])
    sum_qk = Summing(route, lambda: [qk_sum], width, 1, 0, 1)
    qk_sum, v_grad, branch = advance([sum_qk], qk_sum, v_grad, branch, busy=True)
    vo_sum = over_tokens([(normed, v_grad), (branch, mixed)])
    sum_vo = Summing(route, lambda: [vo_sum], width, 1, 0, 0)
    vo_sum = advance([sum_up], vo_sum)
    vo_sum, q_grad, arriving_result = advance(
        [sum_qk, sum_vo], vo_sum, q_grad, arriving_result, busy=True
    )
    heads_terms, one_sums = through_heads(
        [q_grad, k_grad, v_grad], x_all, mean_one, inverse_one, blocks_a, blocks_b
    )
    arriving = scatter(heads_terms)
    one_sums, middle, arriving_result, down_sum = advance(
        [sum_vo], one_sums, middle, arriving_result, down_sum, long=True
    )
    norm_grads = jnp.concatenate([one_sums, two_sums], axis=0)
    bias_sums = bias_sums.transpose(1, 0, 2).reshape(3, local_heads, count, HD // count)
    bias_sums = bias_sums.transpose(2, 0, 1, 3).reshape(count, bias_size)[order]
    extras = jnp.concatenate(
        [norm_grads.reshape(4, count, width).transpose(1, 0, 2).reshape(count, 4 * width), bias_sums],
        axis=1,
    )
    extras = jnp.pad(extras, ((0, 0), (0, -extras.shape[1] % 128)))
    result = finish_result(order, middle, arriving_result)
    moved = halve(route, extras)
    extras, moved, result, down_sum, gate_sum = advance(
        [sum_qk], extras, moved, result, down_sum, gate_sum
    )
    grad_down = sum_down.total(down_sum, 0).T
    extras = extras[: moved.shape[0]] + moved
    moved = halve(route, extras)
    extras, moved, grad_down, gate_sum = advance([sum_vo], extras, moved, grad_down, gate_sum)
    grad_gate = sum_gate.total(gate_sum, 0)
    extras = extras[: moved.shape[0]] + moved
    while extras.shape[0] > 2:
        extras = extras[: extras.shape[0] // 2] + halve(route, extras)
    moved = halve(route, extras)
    extras, moved, grad_gate, up_sum = advance([sum_qk], extras, moved, grad_gate, up_sum)
    grad_up = sum_up.total(up_sum, 0)
    extras = (extras[:1] + moved)[0]
    bias_grad = extras[4 * width : 4 * width + bias_size].reshape(qkv_bias.shape)
    norm_sums = extras[: 4 * width].reshape(4, width)
    moved = across_core(norm_sums)
    grad_up, moved = advance([sum_vo], grad_up, moved)
    norm_sums = norm_sums + moved
    moved = across_chip(norm_sums)
    moved = advance([sum_qk], moved)
    norm_sums = norm_sums + moved
    norm_sums = lax.dynamic_slice_in_dim(norm_sums, here * norm_part, norm_part, axis=1)
    arriving = advance([], arriving)
    input_grad = input_back(order, arriving, own_bf16, norm_rows, middle_grad)
    input_grad, norm_sums = advance([sum_vo], input_grad, norm_sums)

    q_k = sum_qk.total(qk_sum, 0)
    v_o = sum_vo.total(vo_sum, 0)
    return (
        result,
        input_grad,
        norm_sums[0],
        norm_sums[1],
        q_k[:, :heads_wide],
        q_k[:, heads_wide:],
        v_o[:, :heads_wide],
        bias_grad,
        v_o[:, heads_wide:].T,
        norm_sums[2],
        norm_sums[3],
        grad_gate,
        grad_up,
        grad_down,
    )


def solution(mesh):
    both = P(("dp", "tensor"))
    tokens = P(("dp", "tensor"), None)
    rows = P("dp", "tensor")
    columns = P("tensor", "dp")
    biases = P(None, "tensor", "dp")
    return jax.shard_map(
        functools.partial(on_device, Route(mesh.shape["dp"])),
        mesh=mesh,
        in_specs=(
            tokens,
            tokens,
            P("dp"),
            both,
            both,
            rows,
            rows,
            rows,
            biases,
            columns,
            both,
            both,
            rows,
            rows,
            columns,
        ),
        out_specs=(
            tokens,
            tokens,
            both,
            both,
            rows,
            rows,
            rows,
            biases,
            columns,
            both,
            both,
            rows,
            rows,
            columns,
        ),
        check_vma=False,
    )
```
